1024 devices in a mesh: dp: 8 (over z_lo), mx: 16 (over y, z_hi), my: 8 (over x, core).
Axes of the slice: x: 4, y: 8, z: 16 (z_hi: 2, z_lo: 8; z = z_hi * 8 + z_lo), core: 2. Of those that a mesh axis runs over, the one named last changes fastest.
Arguments:
- tokens: bfloat16 [2048, 6144], P(('dp', 'mx')), may hold values from -6 to 6
- w_in: bfloat16 [6144, 24576], P('my', 'mx'), may hold values from -0.078125 to 0.078125
- w_out: bfloat16 [16384, 6144], P('mx', 'my'), may hold values from -0.046875 to 0.046875
- cotangent: bfloat16 [2048, 6144], P(('dp', 'mx'), 'my'), may hold values from -0.29882812 to 0.29882812
Outputs:
- grad_in: bfloat16 [8, 768, 24576], P('dp', 'my', 'mx')
- grad_out: bfloat16 [8, 2048, 6144], P('dp', 'mx', 'my')
The draws below stay inside these ranges and needn't reach their ends.
All inputs are finite; a program needn't handle non-finite values.
Results may differ from the reference program's by a relative error of at most 0.03.
Values may be sent and summed in bfloat16 or wider, within the bound.
No kernel may reach another device: no remote copies, remote signals or barrier semaphores. Data moves between devices by JAX's collectives and lax.ppermute only.
A program may use at most 32 MiB of HBM per device.

```python
import jax
import jax.numpy as jnp
from jax import lax

D = 6144
HEAD = 128
HEADS_DEV = 2
PATCHES = 128
IMAGES = 2
ROWS = 2048
FIN_DEV = 1536
FH_DEV = 1024
FIN = 24576
FH = 16384
N_DP = 8
N_MX = 16
N_MY = 8


def block_levels(key, shape, pieces, low, high):
    loudness = 1.0
    for dim, parts in pieces:
        draws = jax.random.uniform(jax.random.fold_in(jax.random.fold_in(key, 6), dim), (parts,), jnp.float32, low / len(pieces), high / len(pieces))
        loudness = loudness * jnp.repeat(jnp.exp(draws), shape[dim] // parts).reshape((-1,) + (1,) * (len(shape) - 1 - dim))
    return loudness


def scatter_about(rng, shape, deviation, limit, cuts=(), held_as=jnp.bfloat16):
    result = jax.random.normal(rng, shape, jnp.float32) * deviation
    if len(cuts) > 0:
        result = block_levels(rng, shape, cuts, -0.22, 0.18) * result
    return jnp.clip(result, min=-limit, max=limit).astype(held_as)


def setup_inputs(seed: int = 0) -> dict:
    key_list = jax.random.split(jax.random.key(seed), 5)
    tokens = scatter_about(key_list[0], (ROWS, D), 1.0, 6.0, ((0, 128),))
    w_in = scatter_about(key_list[1], (D, FIN), D ** -0.5, 0.078125, ((0, 8), (1, 16)))
    w_out = scatter_about(key_list[2], (FH, D), FH ** -0.5, 0.046875, ((0, 16), (1, 8)))
    cotangent = scatter_about(key_list[3], (ROWS, D), 0.05, 0.29882812, ((0, 128), (1, 8)))
    return dict(tokens=tokens, w_in=w_in, w_out=w_out, cotangent=cotangent)


EPS = 1e-06

def normalize(values):
    center = values - lax.optimization_barrier(jnp.mean(values, axis=-1, keepdims=True))
    spread = lax.optimization_barrier(jnp.mean(center * center, axis=-1, keepdims=True))
    return center * lax.rsqrt(spread + EPS)

def mixer(pre_rows, keyval, first_row, patches):
    rows = pre_rows.shape[0]
    total = keyval.shape[0]
    width = HEADS_DEV * HEAD
    query = normalize(pre_rows[:, :width].reshape(rows, HEADS_DEV, HEAD))
    keys = normalize(keyval[:, :width].reshape(total, HEADS_DEV, HEAD))
    values = keyval[:, width:].reshape(total, HEADS_DEV, HEAD)
    scores = jnp.einsum('qhd,khd->hqk', query, keys, precision=lax.Precision.HIGHEST) * HEAD ** (-0.5)
    query_image = (first_row + lax.iota(jnp.int32, rows)) // patches
    key_image = lax.iota(jnp.int32, total) // patches
    same = (query_image[:, None] == key_image[None, :]).astype(scores.dtype)
    weights = jnp.exp(scores) * same[None]
    weights = weights / lax.optimization_barrier(jnp.sum(weights, axis=-1, keepdims=True))
    attended = jnp.einsum('hqk,khd->qhd', weights, values, precision=lax.Precision.HIGHEST).reshape(rows, width)
    units = jax.nn.gelu(pre_rows[:, 3 * width:], approximate=False)
    return jnp.concatenate([attended, units], axis=1)

def settle(values):
    rounded = lax.optimization_barrier(values.astype(jnp.bfloat16))
    return rounded.astype(jnp.float32)

def block_terms(block_pre, block_grad):
    width = HEADS_DEV * HEAD
    keyval = block_pre[:, width:3 * width]
    hidden, pull = jax.vjp(lambda a, b: mixer(a, b, 0, PATCHES), block_pre, keyval)
    d_rows, d_keyval = pull(block_grad)
    d_pre = d_rows.at[:, width:3 * width].add(d_keyval)
    return (hidden.astype(jnp.bfloat16), d_pre.astype(jnp.bfloat16))

def reference(tokens, w_in, w_out, cotangent):
    rows = IMAGES * PATCHES
    dims = (((0,), (0,)), ((), ()))

    def group(index, sums):
        x_rows = lax.dynamic_slice_in_dim(tokens, index * rows, rows, 0)
        grad_rows = lax.dynamic_slice_in_dim(cotangent, index * rows, rows, 0)
        normed = normalize(x_rows.astype(jnp.float32)).astype(jnp.bfloat16)
        pre = jnp.dot(normed, w_in, preferred_element_type=jnp.float32).astype(jnp.bfloat16)
        d_hidden = lax.dot_general(grad_rows, w_out, (((1,), (1,)), ((), ())), preferred_element_type=jnp.float32)
        pre_blocks = pre.astype(jnp.float32).reshape(rows, N_MX, FIN_DEV).transpose(1, 0, 2)
        grad_blocks = d_hidden.reshape(rows, N_MX, FH_DEV).transpose(1, 0, 2)
        hidden, d_pre = lax.map(lambda pair: block_terms(pair[0], pair[1]), (pre_blocks, grad_blocks))
        hidden = hidden.transpose(1, 0, 2).reshape(rows, N_MX * FH_DEV)
        d_pre = d_pre.transpose(1, 0, 2).reshape(rows, N_MX * FIN_DEV)
        grad_in = lax.dot_general(normed, d_pre, dims, preferred_element_type=jnp.float32)
        grad_out = lax.dot_general(hidden, grad_rows, dims, preferred_element_type=jnp.float32)
        return (sums[0] + settle(grad_in), sums[1] + settle(grad_out))
    start = (jnp.zeros((D, N_MX * FIN_DEV), jnp.float32), jnp.zeros((N_MX * FH_DEV, D), jnp.float32))
    total_in, total_out = lax.fori_loop(0, N_DP, group, start)
    span_in = D // (N_MY * N_DP)
    span_out = FH_DEV // N_DP
    grad_in = total_in.astype(jnp.bfloat16).reshape(N_MY, N_DP, span_in, N_MX * FIN_DEV)
    grad_in = grad_in.transpose(1, 0, 2, 3).reshape(N_DP, N_MY * span_in, N_MX * FIN_DEV)
    grad_out = total_out.astype(jnp.bfloat16).reshape(N_MX, N_DP, span_out, D)
    grad_out = grad_out.transpose(1, 0, 2, 3).reshape(N_DP, N_MX * span_out, D)
    return (grad_in, grad_out)
```

```python
import functools

import jax
import jax.numpy as jnp
from jax import lax
from jax.experimental import pallas as pl
from jax.experimental.pallas import tpu as pltpu
from jax.sharding import Mesh
from jax.sharding import PartitionSpec as P

HEAD = 128
HEADS_DEV = 2
PATCHES = 128
IMAGES = 2
UNITS = 384
EPS = 1e-06

INTERPRET = False
VMEM_LIMIT = 48 * 1024 * 1024

DP = ("dh", "dl")
MX = ("y", "zh")
MY = ("x", "c")

F32 = jnp.float32
BF16 = jnp.bfloat16


def params():
    return pltpu.CompilerParams(vmem_limit_bytes=VMEM_LIMIT)


def norm_kernel(place_ref, tokens_ref, mine_ref, cot_ref, out_ref):
    x = tokens_ref[...].astype(F32)
    mean = jnp.mean(x, axis=-1, keepdims=True)
    center = x - mean
    spread = jnp.mean(center * center, axis=-1, keepdims=True)
    mine = (mine_ref[...].astype(F32) - mean) * lax.rsqrt(spread + EPS)
    out_ref[0] = mine.astype(BF16)
    out_ref[1] = cot_ref[...]


def norm_rows(place, tokens, cotangent):
    rows, features = tokens.shape
    dblock = cotangent.shape[1]
    return pl.pallas_call(
        norm_kernel,
        out_shape=jax.ShapeDtypeStruct((2, rows, dblock), BF16),
        grid_spec=pltpu.PrefetchScalarGridSpec(
            num_scalar_prefetch=1,
            grid=(1,),
            in_specs=[
                pl.BlockSpec((rows, features), lambda s, place: (0, 0)),
                pl.BlockSpec((rows, dblock), lambda s, place: (0, place[0])),
                pl.BlockSpec((rows, dblock), lambda s, place: (0, 0)),
            ],
            out_specs=pl.BlockSpec((2, rows, dblock), lambda s, place: (0, 0, 0)),
        ),
        compiler_params=params(),
        interpret=INTERPRET,
    )(place, tokens, tokens, cotangent)


def products_kernel(y_ref, cot_ref, wa, wb, wc, va, vb, vc, out_ref):
    total = IMAGES * PATCHES
    dblock = wa.shape[0]
    y = y_ref[...].reshape(total, dblock)
    cot = cot_ref[...].reshape(total, dblock)
    w = jnp.concatenate([wa[...], wb[...], wc[...]], axis=1)
    v = jnp.concatenate([va[...], vb[...], vc[...]], axis=0)
    pre = jnp.dot(y, w, preferred_element_type=F32)
    grad = lax.dot_general(cot, v, (((1,), (1,)), ((), ())), preferred_element_type=F32)
    out_ref[0, :, 0, :, :UNITS] = pre.astype(BF16).reshape(IMAGES, PATCHES, UNITS)
    out_ref[0, :, 0, :, UNITS:] = grad.astype(BF16).reshape(IMAGES, PATCHES, UNITS)


def products(gathered, w_in, w_out):
    parts, _, rows, dblock = gathered.shape

    def half(which):
        return pl.BlockSpec((parts, pl.squeezed, rows, dblock), lambda s: (0, which, 0, 0))

    def w_cols(a):
        return pl.BlockSpec(
            (dblock, HEAD), lambda s: (0, jnp.where(s < 2, s + 2 * a, 3 * s + a))
        )

    def v_rows(a):
        return pl.BlockSpec((HEAD, dblock), lambda s: (jnp.where(s < 2, s, 3 * s - 4 + a), 0))

    return pl.pallas_call(
        products_kernel,
        out_shape=jax.ShapeDtypeStruct((2, IMAGES, 2, PATCHES, 2 * UNITS), BF16),
        grid=(4,),
        in_specs=[half(0), half(1)]
        + [w_cols(a) for a in range(3)]
        + [v_rows(a) for a in range(3)],
        out_specs=pl.BlockSpec(
            (1, IMAGES, 1, PATCHES, 2 * UNITS), lambda s: (s // 2, 0, s % 2, 0, 0)
        ),
        compiler_params=params(),
        interpret=INTERPRET,
    )(gathered, gathered, w_in, w_in, w_in, w_out, w_out, w_out)


def exact(a, b, contract):
    return lax.dot_general(
        a, b, (contract, ((), ())), precision=lax.Precision.HIGHEST, preferred_element_type=F32
    )


def head_norm(values):
    center = values - jnp.mean(values, axis=-1, keepdims=True)
    scale = lax.rsqrt(jnp.mean(center * center, axis=-1, keepdims=True) + EPS)
    return center * scale, scale


def head_norm_pull(normed, scale, grad):
    along = jnp.mean(grad * normed, axis=-1, keepdims=True)
    return scale * (grad - jnp.mean(grad, axis=-1, keepdims=True) - normed * along)


def unit_kernel(place_ref, terms_ref, hidden_ref, d_pre_ref):
    summed = terms_ref[0].astype(F32)
    for part in range(1, terms_ref.shape[0]):
        summed = summed + terms_ref[part].astype(F32)
    pre = summed[:, :UNITS].astype(BF16).astype(F32)
    grad = summed[:, UNITS:]

    @pl.when(place_ref[0] < 4)
    def attention():
        value = pre[:, 2 * HEAD :]
        d_out = grad[:, :HEAD]
        query, query_scale = head_norm(pre[:, :HEAD])
        key, key_scale = head_norm(pre[:, HEAD : 2 * HEAD])
        weights = jnp.exp(exact(query, key, ((1,), (1,))) * HEAD ** (-0.5))
        weights = weights / jnp.sum(weights, axis=-1, keepdims=True)
        out = exact(weights, value, ((1,), (0,)))
        d_value = exact(weights, d_out, ((0,), (0,)))
        d_weights = exact(d_out, value, ((1,), (1,)))
        along = jnp.sum(d_weights * weights, axis=-1, keepdims=True)
        d_scores = weights * (d_weights - along) * HEAD ** (-0.5)
        d_query = exact(d_scores, key, ((1,), (0,)))
        d_key = exact(d_scores, query, ((0,), (0,)))
        hidden_ref[:, :HEAD] = out.astype(BF16)
        hidden_ref[:, HEAD:] = jnp.zeros((PATCHES, 2 * HEAD), BF16)
        d_pre_ref[:, :HEAD] = head_norm_pull(query, query_scale, d_query).astype(BF16)
        d_pre_ref[:, HEAD : 2 * HEAD] = head_norm_pull(key, key_scale, d_key).astype(BF16)
        d_pre_ref[:, 2 * HEAD :] = d_value.astype(BF16)

    @pl.when(place_ref[0] >= 4)
    def units():
        below = 0.5 * (1.0 + lax.erf(pre * 2.0**-0.5))
        density = jnp.exp(-0.5 * pre * pre) * 0.3989422804014327
        hidden_ref[...] = (pre * below).astype(BF16)
        d_pre_ref[...] = (grad * (below + pre * density)).astype(BF16)


def unit(place, terms):
    shape = jax.ShapeDtypeStruct((PATCHES, UNITS), BF16)
    return pl.pallas_call(
        unit_kernel,
        out_shape=(shape, shape),
        grid_spec=pltpu.PrefetchScalarGridSpec(
            num_scalar_prefetch=1,
            grid=(1,),
            in_specs=[pl.BlockSpec(terms.shape, lambda s, place: (0, 0, 0))],
            out_specs=[pl.BlockSpec((PATCHES, UNITS), lambda s, place: (0, 0))] * 2,
        ),
        compiler_params=params(),
        interpret=INTERPRET,
    )(place, terms)


def grad_out_kernel(pieces_ref, cot_ref, out_ref):
    total = IMAGES * PATCHES
    cot = cot_ref[...].reshape(total, cot_ref.shape[-1])
    dims = (((0,), (0,)), ((), ()))
    for s in range(4):
        width = HEAD if s < 2 else UNITS
        first = s * HEAD if s < 2 else 2 * HEAD + (s - 2) * UNITS
        base = s if s < 2 else s + 2
        hidden = jnp.concatenate(
            [pieces_ref[base][:, :width], pieces_ref[base + 2][:, :width]], axis=0
        )
        out_ref[first : first + width] = lax.dot_general(
            hidden, cot, dims, preferred_element_type=F32
        ).astype(BF16)


def grad_out_terms(pieces, gathered):
    parts, _, rows, dblock = gathered.shape
    height = 2 * HEAD + 2 * UNITS
    return pl.pallas_call(
        grad_out_kernel,
        out_shape=jax.ShapeDtypeStruct((height, dblock), BF16),
        grid=(1,),
        in_specs=[
            pl.BlockSpec(pieces.shape, lambda s: (0, 0, 0)),
            pl.BlockSpec((parts, pl.squeezed, rows, dblock), lambda s: (0, 1, 0, 0)),
        ],
        out_specs=pl.BlockSpec((height, dblock), lambda s: (0, 0)),
        compiler_params=params(),
        interpret=INTERPRET,
    )(pieces, gathered)


def grad_in_kernel(y_ref, own_ref, other_ref, out_ref):
    total = IMAGES * PATCHES
    dims = (((0,), (0,)), ((), ()))
    y = y_ref[...].reshape(2 * total, y_ref.shape[-1])
    for s in range(4):
        base = s if s < 2 else s + 2
        d_pre = jnp.concatenate(
            [own_ref[base], own_ref[base + 2], other_ref[base], other_ref[base + 2]], axis=0
        )
        terms = lax.dot_general(y, d_pre, dims, preferred_element_type=F32).astype(BF16)
        if s < 2:
            for a in range(3):
                first = (2 * a + s) * HEAD
                out_ref[:, first : first + HEAD] = terms[:, a * HEAD : (a + 1) * HEAD]
        else:
            first = 6 * HEAD + (s - 2) * UNITS
            out_ref[:, first : first + UNITS] = terms


def grad_in_terms(y_pair, own, other):
    width = 6 * HEAD + 2 * UNITS
    whole = pl.BlockSpec(own.shape, lambda s: (0, 0, 0))
    return pl.pallas_call(
        grad_in_kernel,
        out_shape=jax.ShapeDtypeStruct((y_pair.shape[-1], width), BF16),
        grid=(1,),
        in_specs=[pl.BlockSpec(y_pair.shape, lambda s: (0, 0, 0)), whole, whole],
        out_specs=pl.BlockSpec((y_pair.shape[-1], width), lambda s: (0, 0)),
        compiler_params=params(),
        interpret=INTERPRET,
    )(y_pair, own, other)


def swap(values, axis):
    return lax.ppermute(values, axis, [(0, 1), (1, 0)])


def shards(tokens, w_in, w_out, cotangent):
    parts = lax.axis_size(MY)
    place = lax.axis_index(MY).astype(jnp.int32).reshape(1)
    dblock = w_in.shape[0]
    total = IMAGES * PATCHES

    with jax.named_scope("token_rows"):
        mine = norm_rows(place, tokens, cotangent)
        rows = jnp.concatenate([mine, swap(mine, "zh")], axis=1)
        gathered = lax.all_gather(rows, "y", axis=0, tiled=False)

    with jax.named_scope("y_of_two_groups"):
        y_all = gathered[:, 0].reshape(total, dblock)
        half = dblock // 2
        side = lax.axis_index("dh")
        y_keep = lax.dynamic_slice_in_dim(y_all, side * half, half, 1)
        y_give = lax.dynamic_slice_in_dim(y_all, (1 - side) * half, half, 1)
        y_pair = jnp.stack([y_keep, swap(y_give, "dh")])

    with jax.named_scope("units"):
        terms = products(gathered, w_in, w_out).reshape(parts * PATCHES, 2 * UNITS)
        terms = lax.all_to_all(terms, MY, 0, 0, tiled=True)
        hidden, d_pre = unit(place, terms.reshape(parts, PATCHES, 2 * UNITS))

    with jax.named_scope("hidden_rows"):
        hidden_all = lax.all_gather(hidden, MY, axis=0, tiled=False)
        d_pre_other = swap(d_pre, "dh")
        grad_out = grad_out_terms(hidden_all, gathered)
        grad_out = lax.psum_scatter(grad_out, DP, scatter_dimension=0, tiled=True)

    with jax.named_scope("d_pre_rows"):
        own = lax.all_gather(d_pre, MY, axis=0, tiled=False)
        other = lax.all_gather(d_pre_other, MY, axis=0, tiled=False)
        grad_in = grad_in_terms(y_pair, own, other)
        grad_in = lax.all_to_all(grad_in, "dl", 0, 0, tiled=True)
        near = lax.axis_size("dl")
        grad_in = grad_in.reshape(near, half // near, grad_in.shape[1])
        grad_in = jnp.sum(grad_in.astype(F32), axis=0).astype(BF16)

    return grad_in[None], grad_out[None]


def solution(mesh):
    sizes = dict(mesh.shape)
    lines = sizes["mx"] // 2
    cut = (2, sizes["dp"] // 2, lines, 2, sizes["my"] // 2, 2)
    fine = Mesh(mesh.devices.reshape(cut), DP + MX + MY)
    return jax.shard_map(
        shards,
        mesh=fine,
        in_specs=(P(DP + MX, None), P(MY, MX), P(MX, MY), P(DP + MX, MY)),
        out_specs=(P(DP, MY, MX), P(DP, MX, MY)),
        check_vma=False,
    )
```

```python
import functools

import jax
import jax.numpy as jnp
from jax import lax
from jax.experimental import pallas as pl
from jax.experimental.pallas import tpu as pltpu
from jax.sharding import Mesh
from jax.sharding import PartitionSpec as P

HEAD = 128
HEADS_DEV = 2
PATCHES = 128
IMAGES = 2
UNITS = 384
EPS = 1e-06

INTERPRET = False
VMEM_LIMIT = 48 * 1024 * 1024

DP = ("dh", "dl")
MX = ("y", "zh")
MY = ("x", "c")

F32 = jnp.float32
BF16 = jnp.bfloat16


def params():
    return pltpu.CompilerParams(vmem_limit_bytes=VMEM_LIMIT)


def norm_kernel(place_ref, tokens_ref, mine_ref, cot_ref, out_ref):
    x = tokens_ref[...].astype(F32)
    mean = jnp.mean(x, axis=-1, keepdims=True)
    center = x - mean
    spread = jnp.mean(center * center, axis=-1, keepdims=True)
    mine = (mine_ref[...].astype(F32) - mean) * lax.rsqrt(spread + EPS)
    out_ref[0] = mine.astype(BF16)
    out_ref[1] = cot_ref[...]


def norm_rows(place, tokens, cotangent):
    rows, features = tokens.shape
    dblock = cotangent.shape[1]
    return pl.pallas_call(
        norm_kernel,
        out_shape=jax.ShapeDtypeStruct((2, rows, dblock), BF16),
        grid_spec=pltpu.PrefetchScalarGridSpec(
            num_scalar_prefetch=1,
            grid=(1,),
            in_specs=[
                pl.BlockSpec((rows, features), lambda s, place: (0, 0)),
                pl.BlockSpec((rows, dblock), lambda s, place: (0, place[0])),
                pl.BlockSpec((rows, dblock), lambda s, place: (0, 0)),
            ],
            out_specs=pl.BlockSpec((2, rows, dblock), lambda s, place: (0, 0, 0)),
        ),
        compiler_params=params(),
        interpret=INTERPRET,
    )(place, tokens, tokens, cotangent)


def products_kernel(y_ref, cot_ref, wa, wb, wc, va, vb, vc, out_ref, flag_ref):
    total = IMAGES * PATCHES
    dblock = wa.shape[0]
    y = y_ref[...].reshape(total, dblock)
    cot = cot_ref[...].reshape(total, dblock)
    w = jnp.concatenate([wa[...], wb[...], wc[...]], axis=1)
    v = jnp.concatenate([va[...], vb[...], vc[...]], axis=0)
    pre = jnp.dot(y, w, preferred_element_type=F32)
    grad = lax.dot_general(cot, v, (((1,), (1,)), ((), ())), preferred_element_type=F32)
    out_ref[0, :, 0, :, :UNITS] = pre.astype(BF16).reshape(IMAGES, PATCHES, UNITS)
    out_ref[0, :, 0, :, UNITS:] = grad.astype(BF16).reshape(IMAGES, PATCHES, UNITS)
    flag_ref[...] = jnp.zeros_like(flag_ref)


def products(gathered, w_in, w_out):
    parts, _, rows, dblock = gathered.shape

    def half(which):
        return pl.BlockSpec((parts, pl.squeezed, rows, dblock), lambda s: (0, which, 0, 0))

    def w_cols(a):
        return pl.BlockSpec(
            (dblock, HEAD), lambda s: (0, jnp.where(s < 2, s + 2 * a, 3 * s + a))
        )

    def v_rows(a):
        return pl.BlockSpec((HEAD, dblock), lambda s: (jnp.where(s < 2, s, 3 * s - 4 + a), 0))

    return pl.pallas_call(
        products_kernel,
        out_shape=(
            jax.ShapeDtypeStruct((2, IMAGES, 2, PATCHES, 2 * UNITS), BF16),
            jax.ShapeDtypeStruct((8, HEAD), F32),
        ),
        grid=(4,),
        in_specs=[half(0), half(1)]
        + [w_cols(a) for a in range(3)]
        + [v_rows(a) for a in range(3)],
        out_specs=[
            pl.BlockSpec((1, IMAGES, 1, PATCHES, 2 * UNITS), lambda s: (s // 2, 0, s % 2, 0, 0)),
            pl.BlockSpec((8, HEAD), lambda s: (0, 0)),
        ],
        compiler_params=params(),
        interpret=INTERPRET,
    )(gathered, gathered, w_in, w_in, w_in, w_out, w_out, w_out)


def exact(a, b, contract):
    return lax.dot_general(
        a, b, (contract, ((), ())), precision=lax.Precision.HIGHEST, preferred_element_type=F32
    )


def head_norm(values):
    center = values - jnp.mean(values, axis=-1, keepdims=True)
    scale = lax.rsqrt(jnp.mean(center * center, axis=-1, keepdims=True) + EPS)
    return center * scale, scale


def head_norm_pull(normed, scale, grad):
    along = jnp.mean(grad * normed, axis=-1, keepdims=True)
    return scale * (grad - jnp.mean(grad, axis=-1, keepdims=True) - normed * along)


def unit_kernel(place_ref, terms_ref, earlier_ref, other_ref, hidden_ref, d_pre_ref):
    summed = terms_ref[0].astype(F32)
    for part in range(1, terms_ref.shape[0]):
        summed = summed + terms_ref[part].astype(F32)
    pre = summed[:, :UNITS].astype(BF16).astype(F32)
    grad = summed[:, UNITS:]

    @pl.when(place_ref[0] < 4)
    def attention():
        value = pre[:, 2 * HEAD :]
        d_out = grad[:, :HEAD]
        query, query_scale = head_norm(pre[:, :HEAD])
        key, key_scale = head_norm(pre[:, HEAD : 2 * HEAD])
        weights = jnp.exp(exact(query, key, ((1,), (1,))) * HEAD ** (-0.5))
        weights = weights / jnp.sum(weights, axis=-1, keepdims=True)
        out = exact(weights, value, ((1,), (0,)))
        d_value = exact(weights, d_out, ((0,), (0,)))
        d_weights = exact(d_out, value, ((1,), (1,)))
        along = jnp.sum(d_weights * weights, axis=-1, keepdims=True)
        d_scores = weights * (d_weights - along) * HEAD ** (-0.5)
        d_query = exact(d_scores, key, ((1,), (0,)))
        d_key = exact(d_scores, query, ((0,), (0,)))
        hidden_ref[:, :HEAD] = out.astype(BF16)
        hidden_ref[:, HEAD:] = jnp.zeros((PATCHES, 2 * HEAD), BF16)
        d_pre_ref[:, :HEAD] = head_norm_pull(query, query_scale, d_query).astype(BF16)
        d_pre_ref[:, HEAD : 2 * HEAD] = head_norm_pull(key, key_scale, d_key).astype(BF16)
        d_pre_ref[:, 2 * HEAD :] = d_value.astype(BF16)

    @pl.when(place_ref[0] >= 4)
    def units():
        below = 0.5 * (1.0 + lax.erf(pre * 2.0**-0.5))
        density = jnp.exp(-0.5 * pre * pre) * 0.3989422804014327
        hidden_ref[...] = (pre * below).astype(BF16)
        d_pre_ref[...] = (grad * (below + pre * density)).astype(BF16)


def unit(place, terms, earlier, other):
    shape = jax.ShapeDtypeStruct((PATCHES, UNITS), BF16)
    return pl.pallas_call(
        unit_kernel,
        out_shape=(shape, shape),
        grid_spec=pltpu.PrefetchScalarGridSpec(
            num_scalar_prefetch=1,
            grid=(1,),
            in_specs=[
                pl.BlockSpec(terms.shape, lambda s, place: (0, 0, 0)),
                pl.BlockSpec(memory_space=pl.ANY),
                pl.BlockSpec(memory_space=pl.ANY),
            ],
            out_specs=[pl.BlockSpec((PATCHES, UNITS), lambda s, place: (0, 0))] * 2,
        ),
        compiler_params=params(),
        interpret=INTERPRET,
    )(place, terms, earlier, other)


def by_owner_kernel(place_ref, pieces_ref, earlier_ref, out_ref):
    for s in range(2):
        out_ref[s] = pieces_ref[0, 0, s, :, :HEAD]
        for a in range(3):
            out_ref[2 + 3 * s + a] = pieces_ref[1, 0, s, :, a * HEAD : (a + 1) * HEAD]


def by_owner(place, pieces, earlier):
    rows = pieces.shape[-2]
    return pl.pallas_call(
        by_owner_kernel,
        out_shape=jax.ShapeDtypeStruct((8, rows, HEAD), BF16),
        grid_spec=pltpu.PrefetchScalarGridSpec(
            num_scalar_prefetch=1,
            grid=(1,),
            in_specs=[
                pl.BlockSpec(
                    (2, 1, 2, rows, UNITS), lambda s, place: (0, place[0] // 4, 0, 0, 0)
                ),
                pl.BlockSpec(memory_space=pl.ANY),
            ],
            out_specs=pl.BlockSpec((8, rows, HEAD), lambda s, place: (0, 0, 0)),
        ),
        compiler_params=params(),
        interpret=INTERPRET,
    )(place, pieces, earlier)


def halves_kernel(side_ref, keep_in, give_in, earlier_ref, keep_ref, give_ref):
    keep_ref[...] = keep_in[...].reshape(keep_ref.shape)
    give_ref[...] = give_in[...].reshape(give_ref.shape)


def halves(side, gathered, earlier):
    parts, _, rows, dblock = gathered.shape
    half = dblock // 2
    block = (parts, pl.squeezed, rows, half)
    shape = jax.ShapeDtypeStruct((parts * rows, half), BF16)
    return pl.pallas_call(
        halves_kernel,
        out_shape=(shape, shape),
        grid_spec=pltpu.PrefetchScalarGridSpec(
            num_scalar_prefetch=1,
            grid=(1,),
            in_specs=[
                pl.BlockSpec(block, lambda s, side: (0, 0, 0, side[0])),
                pl.BlockSpec(block, lambda s, side: (0, 0, 0, 1 - side[0])),
                pl.BlockSpec(memory_space=pl.ANY),
            ],
            out_specs=[pl.BlockSpec((parts * rows, half), lambda s, side: (0, 0))] * 2,
        ),
        compiler_params=params(),
        interpret=INTERPRET,
    )(side, gathered, gathered, earlier)


def cotangent_kernel(rows_ref, earlier_ref, out_ref):
    out_ref[...] = rows_ref[...]


def cotangent_rows(gathered, count, earlier):
    groups, _, rows, dblock = gathered.shape
    return pl.pallas_call(
        cotangent_kernel,
        out_shape=jax.ShapeDtypeStruct((groups, count, dblock), BF16),
        grid=(1,),
        in_specs=[
            pl.BlockSpec((groups, pl.squeezed, count, dblock), lambda s: (0, 1, 0, 0)),
            pl.BlockSpec(memory_space=pl.ANY),
        ],
        out_specs=pl.BlockSpec((groups, count, dblock), lambda s: (0, 0, 0)),
        compiler_params=params(),
        interpret=INTERPRET,
    )(gathered, earlier)


def grad_out_kernel(hidden_ref, cot_ref, out_ref, sum_ref):
    step = pl.program_id(0)
    total = cot_ref.shape[0] * cot_ref.shape[1] * cot_ref.shape[2]
    hidden = hidden_ref[...].reshape(total, HEAD)
    cot = cot_ref[...].reshape(total, cot_ref.shape[-1])
    terms = lax.dot_general(hidden, cot, (((0,), (0,)), ((), ())), preferred_element_type=F32)

    @pl.when(step == 0)
    def first():
        sum_ref[...] = terms

    @pl.when(step > 0)
    def later():
        sum_ref[...] += terms

    @pl.when(step == pl.num_programs(0) - 1)
    def last():
        out_ref[...] = sum_ref[...].astype(BF16)


def grad_out_rows(hidden, cot):
    lines, groups, rows, dblock = cot.shape
    steps = 2 if lines % 2 == 0 else 1
    return pl.pallas_call(
        grad_out_kernel,
        out_shape=jax.ShapeDtypeStruct((HEAD, dblock), BF16),
        grid=(steps,),
        in_specs=[
            pl.BlockSpec((lines // steps, groups, rows, HEAD), lambda s: (s, 0, 0, 0)),
            pl.BlockSpec((lines // steps, groups, rows, dblock), lambda s: (s, 0, 0, 0)),
        ],
        out_specs=pl.BlockSpec((HEAD, dblock), lambda s: (0, 0)),
        scratch_shapes=[pltpu.VMEM((HEAD, dblock), F32)],
        compiler_params=params(),
        interpret=INTERPRET,
    )(hidden, cot)


def grad_in_kernel(y_own_ref, y_other_ref, own_ref, other_ref, out_ref):
    dims = (((0,), (0,)), ((), ()))
    y = jnp.concatenate([y_own_ref[...], y_other_ref[...]], axis=0)
    for s in range(4):
        base = s if s < 2 else s + 2
        d_pre = jnp.concatenate(
            [own_ref[base], own_ref[base + 2], other_ref[base], other_ref[base + 2]], axis=0
        )
        terms = lax.dot_general(y, d_pre, dims, preferred_element_type=F32).astype(BF16)
        if s < 2:
            for a in range(3):
                first = (2 * a + s) * HEAD
                out_ref[:, first : first + HEAD] = terms[:, a * HEAD : (a + 1) * HEAD]
        else:
            first = 6 * HEAD + (s - 2) * UNITS
            out_ref[:, first : first + UNITS] = terms


def grad_in_terms(y_own, y_other, own, other):
    features = y_own.shape[-1]
    width = 6 * HEAD + 2 * UNITS
    y = pl.BlockSpec(y_own.shape, lambda s: (0, 0))
    whole = pl.BlockSpec(own.shape, lambda s: (0, 0, 0))
    return pl.pallas_call(
        grad_in_kernel,
        out_shape=jax.ShapeDtypeStruct((features, width), BF16),
        grid=(1,),
        in_specs=[y, y, whole, whole],
        out_specs=pl.BlockSpec((features, width), lambda s: (0, 0)),
        compiler_params=params(),
        interpret=INTERPRET,
    )(y_own, y_other, own, other)


def swap(values, axis):
    return lax.ppermute(values, axis, [(0, 1), (1, 0)])


def send(values, axis):
    shape = values.shape
    flat = values.reshape((shape[0] * shape[1],) + shape[2:])
    return lax.all_to_all(flat, axis, 0, 0, tiled=True).reshape(shape)


def shards(tokens, w_in, w_out, cotangent):
    parts = lax.axis_size(MY)
    groups = lax.axis_size(DP)
    place = lax.axis_index(MY).astype(jnp.int32).reshape(1)
    side = lax.axis_index("dh").astype(jnp.int32).reshape(1)
    dblock = w_in.shape[0]
    total = IMAGES * PATCHES
    kinds = (2, IMAGES, 2)
    lines = 8
    block = total // lines

    with jax.named_scope("token_rows"):
        mine = norm_rows(place, tokens, cotangent)
        rows = jnp.concatenate([mine, swap(mine, "zh")], axis=1)
        gathered = lax.all_gather(rows, "y", axis=0, tiled=False)

    with jax.named_scope("units"):
        partial, flag = products(gathered, w_in, w_out)
        terms = send(partial.reshape(parts, PATCHES, 2 * UNITS), MY)
        y_own, y_give = halves(side, gathered, flag)

    with jax.named_scope("y_of_two_groups"):
        y_other = swap(y_give, "dh")

    with jax.named_scope("cotangent_of_all_groups"):
        count = rows.shape[1]
        padded = jnp.concatenate([rows, rows[:, : count // 2]], axis=1)
        cot_rows = lax.all_gather(padded, DP, axis=0, tiled=False)
        cot_rows = cotangent_rows(cot_rows, count, y_other)
        cot_all = lax.all_gather(cot_rows, "y", axis=0, tiled=False)
        held = cot_all.shape[0]
        cot_all = cot_all.reshape(held, groups, lines // held, block, dblock)
        cot_all = cot_all.swapaxes(1, 2).reshape(lines, groups, block, dblock)

    with jax.named_scope("units"):
        hidden, d_pre = unit(place, terms, cot_rows, y_other)

    with jax.named_scope("d_pre_of_two_groups"):
        d_pre_other = swap(d_pre, "dh")
        own = lax.all_gather(d_pre, MY, axis=0, tiled=False)
        other = lax.all_gather(d_pre_other, MY, axis=0, tiled=False)
        grad_in = grad_in_terms(y_own, y_other, own, other)
        grad_in = send(grad_in.reshape(4, dblock // 8, grad_in.shape[1]), "dl")

    with jax.named_scope("hidden_of_all_groups"):
        pieces = hidden.reshape(1, lines // IMAGES, block, UNITS)
        pieces = jnp.broadcast_to(pieces, (IMAGES,) + pieces.shape[1:])
        pieces = send(pieces.reshape(parts, block, UNITS), MY)
        owned = by_owner(place, pieces.reshape(kinds + (block, UNITS)), own)
        owned = lax.all_gather(send(owned, DP), MY, axis=0, tiled=False)
        grad_out = grad_out_rows(owned, cot_all)

    with jax.named_scope("grad_in_sum"):
        grad_in = jnp.sum(grad_in.astype(F32), axis=0).astype(BF16)

    return grad_in[None], grad_out[None]


def solution(mesh):
    sizes = dict(mesh.shape)
    lines = sizes["mx"] // 2
    cut = (2, sizes["dp"] // 2, lines, 2, sizes["my"] // 2, 2)
    fine = Mesh(mesh.devices.reshape(cut), DP + MX + MY)
    return jax.shard_map(
        shards,
        mesh=fine,
        in_specs=(P(DP + MX, None), P(MY, MX), P(MX, MY), P(DP + MX, MY)),
        out_specs=(P(DP, MY, MX), P(DP, MX, MY)),
        check_vma=False,
    )
```

```python
import functools

import jax
import jax.numpy as jnp
from jax import lax
from jax.experimental import pallas as pl
from jax.experimental.pallas import tpu as pltpu
from jax.sharding import Mesh
from jax.sharding import PartitionSpec as P

HEAD = 128
HEADS_DEV = 2
PATCHES = 128
IMAGES = 2
UNITS = 384
EPS = 1e-06

INTERPRET = False
VMEM_LIMIT = 48 * 1024 * 1024

DP = ("dh", "dl")
MX = ("y", "zh")
MY = ("x", "c")

F32 = jnp.float32
BF16 = jnp.bfloat16


def params():
    return pltpu.CompilerParams(vmem_limit_bytes=VMEM_LIMIT)


def norm_kernel(place_ref, tokens_ref, mine_ref, cot_ref, out_ref):
    x = tokens_ref[...].astype(F32)
    mean = jnp.mean(x, axis=-1, keepdims=True)
    center = x - mean
    spread = jnp.mean(center * center, axis=-1, keepdims=True)
    mine = (mine_ref[...].astype(F32) - mean) * lax.rsqrt(spread + EPS)
    out_ref[0] = mine.astype(BF16)
    out_ref[1] = cot_ref[...]


def norm_rows(place, tokens, cotangent):
    rows, features = tokens.shape
    dblock = cotangent.shape[1]
    return pl.pallas_call(
        norm_kernel,
        out_shape=jax.ShapeDtypeStruct((2, rows, dblock), BF16),
        grid_spec=pltpu.PrefetchScalarGridSpec(
            num_scalar_prefetch=1,
            grid=(1,),
            in_specs=[
                pl.BlockSpec((rows, features), lambda s, place: (0, 0)),
                pl.BlockSpec((rows, dblock), lambda s, place: (0, place[0])),
                pl.BlockSpec((rows, dblock), lambda s, place: (0, 0)),
            ],
            out_specs=pl.BlockSpec((2, rows, dblock), lambda s, place: (0, 0, 0)),
        ),
        compiler_params=params(),
        interpret=INTERPRET,
    )(place, tokens, tokens, cotangent)


def products_kernel(y_ref, cot_ref, wa, wb, wc, va, vb, vc, out_ref, rows_ref):
    total = IMAGES * PATCHES
    dblock = wa.shape[0]
    y = y_ref[...].reshape(total, dblock)
    cot = cot_ref[...].reshape(total, dblock)
    w = jnp.concatenate([wa[...], wb[...], wc[...]], axis=1)
    v = jnp.concatenate([va[...], vb[...], vc[...]], axis=0)
    pre = jnp.dot(y, w, preferred_element_type=F32)
    grad = lax.dot_general(cot, v, (((1,), (1,)), ((), ())), preferred_element_type=F32)
    out_ref[0, :, 0, :, :UNITS] = pre.astype(BF16).reshape(IMAGES, PATCHES, UNITS)
    out_ref[0, :, 0, :, UNITS:] = grad.astype(BF16).reshape(IMAGES, PATCHES, UNITS)

    @pl.when(pl.program_id(0) == 0)
    def copy():
        rows_ref[...] = cot


def products(gathered, w_in, w_out):
    parts, _, rows, dblock = gathered.shape

    def half(which):
        return pl.BlockSpec((parts, pl.squeezed, rows, dblock), lambda s: (0, which, 0, 0))

    def w_cols(a):
        return pl.BlockSpec(
            (dblock, HEAD), lambda s: (0, jnp.where(s < 2, s + 2 * a, 3 * s + a))
        )

    def v_rows(a):
        return pl.BlockSpec((HEAD, dblock), lambda s: (jnp.where(s < 2, s, 3 * s - 4 + a), 0))

    return pl.pallas_call(
        products_kernel,
        out_shape=(
            jax.ShapeDtypeStruct((2, IMAGES, 2, PATCHES, 2 * UNITS), BF16),
            jax.ShapeDtypeStruct((IMAGES * PATCHES, dblock), BF16),
        ),
        grid=(4,),
        in_specs=[half(0), half(1)]
        + [w_cols(a) for a in range(3)]
        + [v_rows(a) for a in range(3)],
        out_specs=[
            pl.BlockSpec((1, IMAGES, 1, PATCHES, 2 * UNITS), lambda s: (s // 2, 0, s % 2, 0, 0)),
            pl.BlockSpec((IMAGES * PATCHES, dblock), lambda s: (0, 0)),
        ],
        compiler_params=params(),
        interpret=INTERPRET,
    )(gathered, gathered, w_in, w_in, w_in, w_out, w_out, w_out)


def exact(a, b, contract):
    return lax.dot_general(
        a, b, (contract, ((), ())), precision=lax.Precision.HIGHEST, preferred_element_type=F32
    )


def head_norm(values):
    center = values - jnp.mean(values, axis=-1, keepdims=True)
    scale = lax.rsqrt(jnp.mean(center * center, axis=-1, keepdims=True) + EPS)
    return center * scale, scale


def head_norm_pull(normed, scale, grad):
    along = jnp.mean(grad * normed, axis=-1, keepdims=True)
    return scale * (grad - jnp.mean(grad, axis=-1, keepdims=True) - normed * along)


def unit_kernel(place_ref, terms_ref, earlier_ref, hidden_ref, d_pre_ref):
    summed = terms_ref[0].astype(F32)
    for part in range(1, terms_ref.shape[0]):
        summed = summed + terms_ref[part].astype(F32)
    pre = summed[:, :UNITS].astype(BF16).astype(F32)
    grad = summed[:, UNITS:]

    @pl.when(place_ref[0] < 4)
    def attention():
        value = pre[:, 2 * HEAD :]
        d_out = grad[:, :HEAD]
        query, query_scale = head_norm(pre[:, :HEAD])
        key, key_scale = head_norm(pre[:, HEAD : 2 * HEAD])
        weights = jnp.exp(exact(query, key, ((1,), (1,))) * HEAD ** (-0.5))
        weights = weights / jnp.sum(weights, axis=-1, keepdims=True)
        out = exact(weights, value, ((1,), (0,)))
        d_value = exact(weights, d_out, ((0,), (0,)))
        d_weights = exact(d_out, value, ((1,), (1,)))
        along = jnp.sum(d_weights * weights, axis=-1, keepdims=True)
        d_scores = weights * (d_weights - along) * HEAD ** (-0.5)
        d_query = exact(d_scores, key, ((1,), (0,)))
        d_key = exact(d_scores, query, ((0,), (0,)))
        hidden_ref[:, :HEAD] = out.astype(BF16)
        hidden_ref[:, HEAD:] = jnp.zeros((PATCHES, 2 * HEAD), BF16)
        d_pre_ref[:, :HEAD] = head_norm_pull(query, query_scale, d_query).astype(BF16)
        d_pre_ref[:, HEAD : 2 * HEAD] = head_norm_pull(key, key_scale, d_key).astype(BF16)
        d_pre_ref[:, 2 * HEAD :] = d_value.astype(BF16)

    @pl.when(place_ref[0] >= 4)
    def units():
        below = 0.5 * (1.0 + lax.erf(pre * 2.0**-0.5))
        density = jnp.exp(-0.5 * pre * pre) * 0.3989422804014327
        hidden_ref[...] = (pre * below).astype(BF16)
        d_pre_ref[...] = (grad * (below + pre * density)).astype(BF16)


def unit(place, terms, earlier):
    shape = jax.ShapeDtypeStruct((PATCHES, UNITS), BF16)
    return pl.pallas_call(
        unit_kernel,
        out_shape=(shape, shape),
        grid_spec=pltpu.PrefetchScalarGridSpec(
            num_scalar_prefetch=1,
            grid=(1,),
            in_specs=[
                pl.BlockSpec(terms.shape, lambda s, place: (0, 0, 0)),
                pl.BlockSpec(memory_space=pl.ANY),
            ],
            out_specs=[pl.BlockSpec((PATCHES, UNITS), lambda s, place: (0, 0))] * 2,
        ),
        compiler_params=params(),
        interpret=INTERPRET,
    )(place, terms, earlier)


def by_owner_kernel(place_ref, pieces_ref, earlier_ref, out_ref):
    for s in range(2):
        out_ref[s] = pieces_ref[0, 0, s, :, :HEAD]
        for a in range(3):
            out_ref[2 + 3 * s + a] = pieces_ref[1, 0, s, :, a * HEAD : (a + 1) * HEAD]


def by_owner(place, pieces, earlier):
    rows = pieces.shape[-2]
    return pl.pallas_call(
        by_owner_kernel,
        out_shape=jax.ShapeDtypeStruct((8, rows, HEAD), BF16),
        grid_spec=pltpu.PrefetchScalarGridSpec(
            num_scalar_prefetch=1,
            grid=(1,),
            in_specs=[
                pl.BlockSpec(
                    (2, 1, 2, rows, UNITS), lambda s, place: (0, place[0] // 4, 0, 0, 0)
                ),
                pl.BlockSpec(memory_space=pl.ANY),
            ],
            out_specs=pl.BlockSpec((8, rows, HEAD), lambda s, place: (0, 0, 0)),
        ),
        compiler_params=params(),
        interpret=INTERPRET,
    )(place, pieces, earlier)


def halves_kernel(side_ref, keep_in, give_in, earlier_ref, keep_ref, give_ref):
    keep_ref[...] = keep_in[...].reshape(keep_ref.shape)
    give_ref[...] = give_in[...].reshape(give_ref.shape)


def halves(side, gathered, earlier):
    parts, _, rows, dblock = gathered.shape
    half = dblock // 2
    block = (parts, pl.squeezed, rows, half)
    shape = jax.ShapeDtypeStruct((parts * rows, half), BF16)
    return pl.pallas_call(
        halves_kernel,
        out_shape=(shape, shape),
        grid_spec=pltpu.PrefetchScalarGridSpec(
            num_scalar_prefetch=1,
            grid=(1,),
            in_specs=[
                pl.BlockSpec(block, lambda s, side: (0, 0, 0, side[0])),
                pl.BlockSpec(block, lambda s, side: (0, 0, 0, 1 - side[0])),
                pl.BlockSpec(memory_space=pl.ANY),
            ],
            out_specs=[pl.BlockSpec((parts * rows, half), lambda s, side: (0, 0))] * 2,
        ),
        compiler_params=params(),
        interpret=INTERPRET,
    )(side, gathered, gathered, earlier)


def grad_out_kernel(hidden_ref, cot_ref, out_ref, sum_ref):
    step = pl.program_id(0)
    lines, groups, rows, _ = hidden_ref.shape
    terms = 0.0
    for g in range(groups):
        hidden = hidden_ref[:, g].reshape(lines * rows, HEAD)
        terms = terms + lax.dot_general(
            hidden, cot_ref[g], (((0,), (0,)), ((), ())), preferred_element_type=F32
        )

    @pl.when(step == 0)
    def first():
        sum_ref[...] = terms

    @pl.when(step > 0)
    def later():
        sum_ref[...] += terms

    @pl.when(step == pl.num_programs(0) - 1)
    def last():
        out_ref[...] = sum_ref[...].astype(BF16)


def grad_out_rows(hidden, cot):
    lines, groups, rows, _ = hidden.shape
    dblock = cot.shape[-1]
    each = groups // 4
    return pl.pallas_call(
        grad_out_kernel,
        out_shape=jax.ShapeDtypeStruct((HEAD, dblock), BF16),
        grid=(groups // each,),
        in_specs=[
            pl.BlockSpec((lines, each, rows, HEAD), lambda s: (0, s, 0, 0)),
            pl.BlockSpec((each, lines * rows, dblock), lambda s: (s, 0, 0)),
        ],
        out_specs=pl.BlockSpec((HEAD, dblock), lambda s: (0, 0)),
        scratch_shapes=[pltpu.VMEM((HEAD, dblock), F32)],
        compiler_params=params(),
        interpret=INTERPRET,
    )(hidden, cot)


def grad_in_kernel(y_own_ref, y_other_ref, own_ref, other_ref, out_ref):
    dims = (((0,), (0,)), ((), ()))
    y = jnp.concatenate([y_own_ref[...], y_other_ref[...]], axis=0)
    for s in range(4):
        base = s if s < 2 else s + 2
        d_pre = jnp.concatenate(
            [own_ref[base], own_ref[base + 2], other_ref[base], other_ref[base + 2]], axis=0
        )
        terms = lax.dot_general(y, d_pre, dims, preferred_element_type=F32).astype(BF16)
        if s < 2:
            for a in range(3):
                first = (2 * a + s) * HEAD
                out_ref[:, first : first + HEAD] = terms[:, a * HEAD : (a + 1) * HEAD]
        else:
            first = 6 * HEAD + (s - 2) * UNITS
            out_ref[:, first : first + UNITS] = terms


def grad_in_terms(y_own, y_other, own, other):
    features = y_own.shape[-1]
    width = 6 * HEAD + 2 * UNITS
    y = pl.BlockSpec(y_own.shape, lambda s: (0, 0))
    whole = pl.BlockSpec(own.shape, lambda s: (0, 0, 0))
    return pl.pallas_call(
        grad_in_kernel,
        out_shape=jax.ShapeDtypeStruct((features, width), BF16),
        grid=(1,),
        in_specs=[y, y, whole, whole],
        out_specs=pl.BlockSpec((features, width), lambda s: (0, 0)),
        compiler_params=params(),
        interpret=INTERPRET,
    )(y_own, y_other, own, other)


def sum_kernel(parts_ref, earlier_ref, out_ref):
    summed = parts_ref[0].astype(F32)
    for part in range(1, parts_ref.shape[0]):
        summed = summed + parts_ref[part].astype(F32)
    out_ref[...] = summed.astype(BF16)


def sum_parts(parts, earlier):
    shape = parts.shape[1:]
    return pl.pallas_call(
        sum_kernel,
        out_shape=jax.ShapeDtypeStruct(shape, BF16),
        grid=(1,),
        in_specs=[
            pl.BlockSpec(parts.shape, lambda s: (0, 0, 0)),
            pl.BlockSpec(memory_space=pl.ANY),
        ],
        out_specs=pl.BlockSpec(shape, lambda s: (0, 0)),
        compiler_params=params(),
        interpret=INTERPRET,
    )(parts, earlier)


def swap(values, axis):
    return lax.ppermute(values, axis, [(0, 1), (1, 0)])


def send(values, axis):
    shape = values.shape
    flat = values.reshape((shape[0] * shape[1],) + shape[2:])
    return lax.all_to_all(flat, axis, 0, 0, tiled=True).reshape(shape)


def shards(tokens, w_in, w_out, cotangent):
    parts = lax.axis_size(MY)
    place = lax.axis_index(MY).astype(jnp.int32).reshape(1)
    side = lax.axis_index("dh").astype(jnp.int32).reshape(1)
    dblock = w_in.shape[0]
    total = IMAGES * PATCHES
    kinds = (2, IMAGES, 2)
    lines = 8
    block = total // lines

    with jax.named_scope("token_rows"):
        mine = norm_rows(place, tokens, cotangent)
        rows = jnp.concatenate([mine, swap(mine, "zh")], axis=1)
        gathered = lax.all_gather(rows, "y", axis=0, tiled=False)

    with jax.named_scope("units"):
        partial, cot_rows = products(gathered, w_in, w_out)
        terms = send(partial.reshape(parts, PATCHES, 2 * UNITS), MY)

    with jax.named_scope("cotangent_of_all_groups"):
        cot_all = lax.all_gather(cot_rows, DP, axis=0, tiled=False)

    with jax.named_scope("y_of_two_groups"):
        y_own, y_give = halves(side, gathered, cot_rows)
        y_other = swap(y_give, "dh")

    with jax.named_scope("units"):
        hidden, d_pre = unit(place, terms, y_own)

    with jax.named_scope("d_pre_of_two_groups"):
        d_pre_other = swap(d_pre, "dh")
        own = lax.all_gather(d_pre, MY, axis=0, tiled=False)
        other = lax.all_gather(d_pre_other, MY, axis=0, tiled=False)
        grad_in = grad_in_terms(y_own, y_other, own, other)
        grad_in = send(grad_in.reshape(4, dblock // 8, grad_in.shape[1]), "dl")

    with jax.named_scope("hidden_of_all_groups"):
        pieces = hidden.reshape(1, lines // IMAGES, block, UNITS)
        pieces = jnp.broadcast_to(pieces, (IMAGES,) + pieces.shape[1:])
        pieces = send(pieces.reshape(parts, block, UNITS), MY)
        owned = by_owner(place, pieces.reshape(kinds + (block, UNITS)), own)
        owned = lax.all_gather(send(owned, DP), MY, axis=0, tiled=False)
        grad_out = grad_out_rows(owned, cot_all)

    with jax.named_scope("grad_in_sum"):
        grad_in = sum_parts(grad_in, grad_out)

    return grad_in[None], grad_out[None]


def solution(mesh):
    sizes = dict(mesh.shape)
    lines = sizes["mx"] // 2
    cut = (2, sizes["dp"] // 2, lines, 2, sizes["my"] // 2, 2)
    fine = Mesh(mesh.devices.reshape(cut), DP + MX + MY)
    return jax.shard_map(
        shards,
        mesh=fine,
        in_specs=(P(DP + MX, None), P(MY, MX), P(MX, MY), P(DP + MX, MY)),
        out_specs=(P(DP, MY, MX), P(DP, MX, MY)),
        check_vma=False,
    )
```

```python
import functools

import jax
import jax.numpy as jnp
from jax import lax
from jax.experimental import pallas as pl
from jax.experimental.pallas import tpu as pltpu
from jax.sharding import Mesh
from jax.sharding import PartitionSpec as P

HEAD = 128
HEADS_DEV = 2
PATCHES = 128
IMAGES = 2
UNITS = 384
EPS = 1e-06

INTERPRET = False
VMEM_LIMIT = 66 * 10**6

DP = ("dh", "dl")
MX = ("y", "zh")
MY = ("x", "c")

F32 = jnp.float32
BF16 = jnp.bfloat16


def params(spare=0):
    return pltpu.CompilerParams(vmem_limit_bytes=VMEM_LIMIT - spare)


def norm_kernel(place_ref, tokens_ref, mine_ref, cot_ref, out_ref):
    x = tokens_ref[...].astype(F32)
    mean = jnp.mean(x, axis=-1, keepdims=True)
    center = x - mean
    spread = jnp.mean(center * center, axis=-1, keepdims=True)
    mine = (mine_ref[...].astype(F32) - mean) * lax.rsqrt(spread + EPS)
    out_ref[0] = mine.astype(BF16)
    out_ref[1] = cot_ref[...]


def norm_rows(place, tokens, cotangent):
    rows, features = tokens.shape
    dblock = cotangent.shape[1]
    return pl.pallas_call(
        norm_kernel,
        out_shape=jax.ShapeDtypeStruct((2, rows, dblock), BF16),
        grid_spec=pltpu.PrefetchScalarGridSpec(
            num_scalar_prefetch=1,
            grid=(1,),
            in_specs=[
                pl.BlockSpec((rows, features), lambda s, place: (0, 0)),
                pl.BlockSpec((rows, dblock), lambda s, place: (0, place[0])),
                pl.BlockSpec((rows, dblock), lambda s, place: (0, 0)),
            ],
            out_specs=pl.BlockSpec((2, rows, dblock), lambda s, place: (0, 0, 0)),
        ),
        compiler_params=params(),
        interpret=INTERPRET,
    )(place, tokens, tokens, cotangent)


def products_kernel(y_ref, cot_ref, wa, wb, wc, va, vb, vc, out_ref, flag_ref):
    total = IMAGES * PATCHES
    dblock = wa.shape[0]
    y = y_ref[...].reshape(total, dblock)
    cot = cot_ref[...].reshape(total, dblock)
    w = jnp.concatenate([wa[...], wb[...], wc[...]], axis=1)
    v = jnp.concatenate([va[...], vb[...], vc[...]], axis=0)
    pre = jnp.dot(y, w, preferred_element_type=F32)
    grad = lax.dot_general(cot, v, (((1,), (1,)), ((), ())), preferred_element_type=F32)
    out_ref[0, :, 0, :, :UNITS] = pre.astype(BF16).reshape(IMAGES, PATCHES, UNITS)
    out_ref[0, :, 0, :, UNITS:] = grad.astype(BF16).reshape(IMAGES, PATCHES, UNITS)
    flag_ref[...] = jnp.zeros_like(flag_ref)


def products(gathered, w_in, w_out):
    parts, _, rows, dblock = gathered.shape

    def half(which):
        return pl.BlockSpec((parts, pl.squeezed, rows, dblock), lambda s: (0, which, 0, 0))

    def w_cols(a):
        return pl.BlockSpec(
            (dblock, HEAD), lambda s: (0, jnp.where(s < 2, s + 2 * a, 3 * s + a))
        )

    def v_rows(a):
        return pl.BlockSpec((HEAD, dblock), lambda s: (jnp.where(s < 2, s, 3 * s - 4 + a), 0))

    return pl.pallas_call(
        products_kernel,
        out_shape=(
            jax.ShapeDtypeStruct((2, IMAGES, 2, PATCHES, 2 * UNITS), BF16),
            jax.ShapeDtypeStruct((8, HEAD), F32),
        ),
        grid=(4,),
        in_specs=[half(0), half(1)]
        + [w_cols(a) for a in range(3)]
        + [v_rows(a) for a in range(3)],
        out_specs=[
            pl.BlockSpec((1, IMAGES, 1, PATCHES, 2 * UNITS), lambda s: (s // 2, 0, s % 2, 0, 0)),
            pl.BlockSpec((8, HEAD), lambda s: (0, 0)),
        ],
        compiler_params=params(),
        interpret=INTERPRET,
    )(gathered, gathered, w_in, w_in, w_in, w_out, w_out, w_out)


def exact(a, b, contract):
    return lax.dot_general(
        a, b, (contract, ((), ())), precision=lax.Precision.HIGHEST, preferred_element_type=F32
    )


def head_norm(values):
    center = values - jnp.mean(values, axis=-1, keepdims=True)
    scale = lax.rsqrt(jnp.mean(center * center, axis=-1, keepdims=True) + EPS)
    return center * scale, scale


def head_norm_pull(normed, scale, grad):
    along = jnp.mean(grad * normed, axis=-1, keepdims=True)
    return scale * (grad - jnp.mean(grad, axis=-1, keepdims=True) - normed * along)


def unit_kernel(place_ref, terms_ref, earlier_ref, hidden_ref, d_pre_ref):
    summed = terms_ref[0].astype(F32)
    for part in range(1, terms_ref.shape[0]):
        summed = summed + terms_ref[part].astype(F32)
    pre = summed[:, :UNITS].astype(BF16).astype(F32)
    grad = summed[:, UNITS:]

    @pl.when(place_ref[0] < 4)
    def attention():
        value = pre[:, 2 * HEAD :]
        d_out = grad[:, :HEAD]
        query, query_scale = head_norm(pre[:, :HEAD])
        key, key_scale = head_norm(pre[:, HEAD : 2 * HEAD])
        weights = jnp.exp(exact(query, key, ((1,), (1,))) * HEAD ** (-0.5))
        weights = weights / jnp.sum(weights, axis=-1, keepdims=True)
        out = exact(weights, value, ((1,), (0,)))
        d_value = exact(weights, d_out, ((0,), (0,)))
        d_weights = exact(d_out, value, ((1,), (1,)))
        along = jnp.sum(d_weights * weights, axis=-1, keepdims=True)
        d_scores = weights * (d_weights - along) * HEAD ** (-0.5)
        d_query = exact(d_scores, key, ((1,), (0,)))
        d_key = exact(d_scores, query, ((0,), (0,)))
        hidden_ref[:, :HEAD] = out.astype(BF16)
        hidden_ref[:, HEAD:] = jnp.zeros((PATCHES, 2 * HEAD), BF16)
        d_pre_ref[:, :HEAD] = head_norm_pull(query, query_scale, d_query).astype(BF16)
        d_pre_ref[:, HEAD : 2 * HEAD] = head_norm_pull(key, key_scale, d_key).astype(BF16)
        d_pre_ref[:, 2 * HEAD :] = d_value.astype(BF16)

    @pl.when(place_ref[0] >= 4)
    def units():
        below = 0.5 * (1.0 + lax.erf(pre * 2.0**-0.5))
        density = jnp.exp(-0.5 * pre * pre) * 0.3989422804014327
        hidden_ref[...] = (pre * below).astype(BF16)
        d_pre_ref[...] = (grad * (below + pre * density)).astype(BF16)


def unit(place, terms, earlier):
    shape = jax.ShapeDtypeStruct((PATCHES, UNITS), BF16)
    return pl.pallas_call(
        unit_kernel,
        out_shape=(shape, shape),
        grid_spec=pltpu.PrefetchScalarGridSpec(
            num_scalar_prefetch=1,
            grid=(1,),
            in_specs=[
                pl.BlockSpec(terms.shape, lambda s, place: (0, 0, 0)),
                pl.BlockSpec(memory_space=pl.ANY),
            ],
            out_specs=[pl.BlockSpec((PATCHES, UNITS), lambda s, place: (0, 0))] * 2,
        ),
        compiler_params=params(),
        interpret=INTERPRET,
    )(place, terms, earlier)


def by_owner_kernel(place_ref, pieces_ref, earlier_ref, out_ref):
    for s in range(2):
        out_ref[s] = pieces_ref[0, 0, s, :, :HEAD]
        for a in range(3):
            out_ref[2 + 3 * s + a] = pieces_ref[1, 0, s, :, a * HEAD : (a + 1) * HEAD]


def by_owner(place, pieces, earlier):
    rows = pieces.shape[-2]
    return pl.pallas_call(
        by_owner_kernel,
        out_shape=jax.ShapeDtypeStruct((8, rows, HEAD), BF16),
        grid_spec=pltpu.PrefetchScalarGridSpec(
            num_scalar_prefetch=1,
            grid=(1,),
            in_specs=[
                pl.BlockSpec(
                    (2, 1, 2, rows, UNITS), lambda s, place: (0, place[0] // 4, 0, 0, 0)
                ),
                pl.BlockSpec(memory_space=pl.ANY),
            ],
            out_specs=pl.BlockSpec((8, rows, HEAD), lambda s, place: (0, 0, 0)),
        ),
        compiler_params=params(16 * 10**6),
        interpret=INTERPRET,
    )(place, pieces, earlier)


def halves_kernel(side_ref, keep_in, give_in, earlier_ref, keep_ref, give_ref):
    keep_ref[...] = keep_in[...].reshape(keep_ref.shape)
    give_ref[...] = give_in[...].reshape(give_ref.shape)


def halves(side, gathered, earlier):
    parts, _, rows, dblock = gathered.shape
    half = dblock // 2
    block = (parts, pl.squeezed, rows, half)
    shape = jax.ShapeDtypeStruct((parts * rows, half), BF16)
    return pl.pallas_call(
        halves_kernel,
        out_shape=(shape, shape),
        grid_spec=pltpu.PrefetchScalarGridSpec(
            num_scalar_prefetch=1,
            grid=(1,),
            in_specs=[
                pl.BlockSpec(block, lambda s, side: (0, 0, 0, side[0])),
                pl.BlockSpec(block, lambda s, side: (0, 0, 0, 1 - side[0])),
                pl.BlockSpec(memory_space=pl.ANY),
            ],
            out_specs=[pl.BlockSpec((parts * rows, half), lambda s, side: (0, 0))] * 2,
        ),
        compiler_params=params(),
        interpret=INTERPRET,
    )(side, gathered, gathered, earlier)


def cotangent_kernel(rows_ref, *refs):
    refs[-1][...] = rows_ref[...]


def cotangent_rows(gathered, count, earlier):
    groups, _, rows, dblock = gathered.shape
    return pl.pallas_call(
        cotangent_kernel,
        out_shape=jax.ShapeDtypeStruct((groups, count, dblock), BF16),
        grid=(1,),
        in_specs=[
            pl.BlockSpec((groups, pl.squeezed, count, dblock), lambda s: (0, 1, 0, 0)),
        ]
        + [pl.BlockSpec(memory_space=pl.ANY)] * len(earlier),
        out_specs=pl.BlockSpec((groups, count, dblock), lambda s: (0, 0, 0)),
        compiler_params=params(),
        interpret=INTERPRET,
    )(gathered, *earlier)


def grad_out_kernel(hidden_ref, cot_ref, out_ref, sum_ref):
    step = pl.program_id(0)
    total = cot_ref.shape[0] * cot_ref.shape[1] * cot_ref.shape[2]
    hidden = hidden_ref[...].reshape(total, HEAD)
    cot = cot_ref[...].reshape(total, cot_ref.shape[-1])
    terms = lax.dot_general(hidden, cot, (((0,), (0,)), ((), ())), preferred_element_type=F32)

    @pl.when(step == 0)
    def first():
        sum_ref[...] = terms

    @pl.when(step > 0)
    def later():
        sum_ref[...] += terms

    @pl.when(step == pl.num_programs(0) - 1)
    def last():
        out_ref[...] = sum_ref[...].astype(BF16)


def grad_out_rows(hidden, cot):
    lines, groups, rows, dblock = cot.shape
    steps = 2 if lines % 2 == 0 else 1
    return pl.pallas_call(
        grad_out_kernel,
        out_shape=jax.ShapeDtypeStruct((HEAD, dblock), BF16),
        grid=(steps,),
        in_specs=[
            pl.BlockSpec((lines // steps, groups, rows, HEAD), lambda s: (s, 0, 0, 0)),
            pl.BlockSpec((lines // steps, groups, rows, dblock), lambda s: (s, 0, 0, 0)),
        ],
        out_specs=pl.BlockSpec((HEAD, dblock), lambda s: (0, 0)),
        scratch_shapes=[pltpu.VMEM((HEAD, dblock), F32)],
        compiler_params=params(),
        interpret=INTERPRET,
    )(hidden, cot)


def grad_in_kernel(y_own_ref, y_other_ref, own_ref, other_ref, out_ref):
    dims = (((0,), (0,)), ((), ()))
    y = jnp.concatenate([y_own_ref[...], y_other_ref[...]], axis=0)
    for s in range(4):
        base = s if s < 2 else s + 2
        d_pre = jnp.concatenate(
            [own_ref[base], own_ref[base + 2], other_ref[base], other_ref[base + 2]], axis=0
        )
        terms = lax.dot_general(y, d_pre, dims, preferred_element_type=F32).astype(BF16)
        if s < 2:
            for a in range(3):
                first = (2 * a + s) * HEAD
                out_ref[:, first : first + HEAD] = terms[:, a * HEAD : (a + 1) * HEAD]
        else:
            first = 6 * HEAD + (s - 2) * UNITS
            out_ref[:, first : first + UNITS] = terms


def grad_in_terms(y_own, y_other, own, other):
    features = y_own.shape[-1]
    width = 6 * HEAD + 2 * UNITS
    y = pl.BlockSpec(y_own.shape, lambda s: (0, 0))
    whole = pl.BlockSpec(own.shape, lambda s: (0, 0, 0))
    return pl.pallas_call(
        grad_in_kernel,
        out_shape=jax.ShapeDtypeStruct((features, width), BF16),
        grid=(1,),
        in_specs=[y, y, whole, whole],
        out_specs=pl.BlockSpec((features, width), lambda s: (0, 0)),
        compiler_params=params(5 * 10**6),
        interpret=INTERPRET,
    )(y_own, y_other, own, other)


def sum_kernel(parts_ref, earlier_ref, out_ref):
    summed = parts_ref[0].astype(F32)
    for part in range(1, parts_ref.shape[0]):
        summed = summed + parts_ref[part].astype(F32)
    out_ref[...] = summed.astype(BF16)


def sum_parts(parts, earlier):
    shape = parts.shape[1:]
    return pl.pallas_call(
        sum_kernel,
        out_shape=jax.ShapeDtypeStruct(shape, BF16),
        grid=(1,),
        in_specs=[
            pl.BlockSpec(parts.shape, lambda s: (0, 0, 0)),
            pl.BlockSpec(memory_space=pl.ANY),
        ],
        out_specs=pl.BlockSpec(shape, lambda s: (0, 0)),
        compiler_params=params(),
        interpret=INTERPRET,
    )(parts, earlier)


def swap(values, axis):
    return lax.ppermute(values, axis, [(0, 1), (1, 0)])


def send(values, axis):
    shape = values.shape
    flat = values.reshape((shape[0] * shape[1],) + shape[2:])
    return lax.all_to_all(flat, axis, 0, 0, tiled=True).reshape(shape)


def shards(tokens, w_in, w_out, cotangent):
    parts = lax.axis_size(MY)
    groups = lax.axis_size(DP)
    place = lax.axis_index(MY).astype(jnp.int32).reshape(1)
    side = lax.axis_index("dh").astype(jnp.int32).reshape(1)
    dblock = w_in.shape[0]
    total = IMAGES * PATCHES
    kinds = (2, IMAGES, 2)
    lines = 8
    block = total // lines

    with jax.named_scope("token_rows"):
        mine = norm_rows(place, tokens, cotangent)
        rows = jnp.concatenate([mine, swap(mine, "zh")], axis=1)
        gathered = lax.all_gather(rows, "y", axis=0, tiled=False)

    with jax.named_scope("units"):
        partial, flag = products(gathered, w_in, w_out)
        terms = send(partial.reshape(parts, PATCHES, 2 * UNITS), MY)

    with jax.named_scope("y_of_two_groups"):
        y_own, y_give = halves(side, gathered, flag)
        y_other = swap(y_give, "dh")

    with jax.named_scope("units"):
        hidden, d_pre = unit(place, terms, y_own)

    with jax.named_scope("d_pre_of_two_groups"):
        d_pre_other = swap(d_pre, "dh")
        own = lax.all_gather(d_pre, MY, axis=0, tiled=False)
        other = lax.all_gather(d_pre_other, MY, axis=0, tiled=False)
        grad_in = grad_in_terms(y_own, y_other, own, other)
        grad_in = send(grad_in.reshape(4, dblock // 8, grad_in.shape[1]), "dl")

    with jax.named_scope("hidden_of_all_groups"):
        pieces = hidden.reshape(1, lines // IMAGES, block, UNITS)
        pieces = jnp.broadcast_to(pieces, (IMAGES,) + pieces.shape[1:])
        pieces = send(pieces.reshape(parts, block, UNITS), MY)
        owned = by_owner(place, pieces.reshape(kinds + (block, UNITS)), own)

    with jax.named_scope("cotangent_of_all_groups"):
        count = rows.shape[1]
        padded = jnp.concatenate([rows, rows[:, : count // 2]], axis=1)
        cot_rows = lax.all_gather(padded, DP, axis=0, tiled=False)
        cot_rows = cotangent_rows(cot_rows, count, (owned, d_pre_other, y_other))
        cot_all = lax.all_gather(cot_rows, "y", axis=0, tiled=False)
        held = cot_all.shape[0]
        cot_all = cot_all.reshape(held, groups, lines // held, block, dblock)
        cot_all = cot_all.swapaxes(1, 2).reshape(lines, groups, block, dblock)

    with jax.named_scope("hidden_of_all_groups"):
        owned = lax.all_gather(send(owned, DP), MY, axis=0, tiled=False)
        grad_out = grad_out_rows(owned, cot_all)

    with jax.named_scope("grad_in_sum"):
        grad_in = sum_parts(grad_in, grad_out)

    return grad_in[None], grad_out[None]


def solution(mesh):
    sizes = dict(mesh.shape)
    lines = sizes["mx"] // 2
    cut = (2, sizes["dp"] // 2, lines, 2, sizes["my"] // 2, 2)
    fine = Mesh(mesh.devices.reshape(cut), DP + MX + MY)
    return jax.shard_map(
        shards,
        mesh=fine,
        in_specs=(P(DP + MX, None), P(MY, MX), P(MX, MY), P(DP + MX, MY)),
        out_specs=(P(DP, MY, MX), P(DP, MX, MY)),
        check_vma=False,
    )
```

```python
import functools

import jax
import jax.numpy as jnp
from jax import lax
from jax.experimental import pallas as pl
from jax.experimental.pallas import tpu as pltpu
from jax.sharding import Mesh
from jax.sharding import PartitionSpec as P

HEAD = 128
HEADS_DEV = 2
PATCHES = 128
IMAGES = 2
UNITS = 384
EPS = 1e-06

INTERPRET = False
VMEM_LIMIT = 48 * 2**20

DP = ("dh", "dl")
MX = ("y", "zh")
MY = ("x", "c")

F32 = jnp.float32
BF16 = jnp.bfloat16


def stay(values):
    return pltpu.with_memory_space_constraint(values, pltpu.HBM)


def params():
    return pltpu.CompilerParams(vmem_limit_bytes=VMEM_LIMIT)


def norm_kernel(place_ref, tokens_ref, mine_ref, cot_ref, out_ref):
    x = tokens_ref[...].astype(F32)
    mean = jnp.mean(x, axis=-1, keepdims=True)
    center = x - mean
    spread = jnp.mean(center * center, axis=-1, keepdims=True)
    mine = (mine_ref[...].astype(F32) - mean) * lax.rsqrt(spread + EPS)
    out_ref[0] = mine.astype(BF16)
    out_ref[1] = cot_ref[...]


def norm_rows(place, tokens, cotangent):
    rows, features = tokens.shape
    dblock = cotangent.shape[1]
    return pl.pallas_call(
        norm_kernel,
        out_shape=jax.ShapeDtypeStruct((2, rows, dblock), BF16),
        grid_spec=pltpu.PrefetchScalarGridSpec(
            num_scalar_prefetch=1,
            grid=(1,),
            in_specs=[
                pl.BlockSpec((rows, features), lambda s, place: (0, 0)),
                pl.BlockSpec((rows, dblock), lambda s, place: (0, place[0])),
                pl.BlockSpec((rows, dblock), lambda s, place: (0, 0)),
            ],
            out_specs=pl.BlockSpec((2, rows, dblock), lambda s, place: (0, 0, 0)),
        ),
        compiler_params=params(),
        interpret=INTERPRET,
    )(place, stay(tokens), stay(tokens), stay(cotangent))


def join_kernel(mine_ref, other_ref, rows_ref, longer_ref):
    count = mine_ref.shape[1]
    for ref in (rows_ref, longer_ref):
        ref[:, :count] = mine_ref[...]
        ref[:, count : 2 * count] = other_ref[...]
    longer_ref[:, 2 * count :] = mine_ref[...]


def join_rows(mine, other):
    kinds, count, dblock = mine.shape
    part = pl.BlockSpec(mine.shape, lambda s: (0, 0, 0))
    shapes = [(kinds, 2 * count, dblock), (kinds, 3 * count, dblock)]
    return pl.pallas_call(
        join_kernel,
        out_shape=[jax.ShapeDtypeStruct(shape, BF16) for shape in shapes],
        grid=(1,),
        in_specs=[part, part],
        out_specs=[pl.BlockSpec(shape, lambda s: (0, 0, 0)) for shape in shapes],
        compiler_params=params(),
        interpret=INTERPRET,
    )(mine, other)


def products_kernel(y_ref, cot_ref, wa, wb, wc, va, vb, vc, out_ref, flag_ref):
    total = IMAGES * PATCHES
    dblock = wa.shape[0]
    y = y_ref[...].reshape(total, dblock)
    cot = cot_ref[...].reshape(total, dblock)
    w = jnp.concatenate([wa[...], wb[...], wc[...]], axis=1)
    v = jnp.concatenate([va[...], vb[...], vc[...]], axis=0)
    pre = jnp.dot(y, w, preferred_element_type=F32)
    grad = lax.dot_general(cot, v, (((1,), (1,)), ((), ())), preferred_element_type=F32)
    out_ref[0, :, 0, :, :UNITS] = pre.astype(BF16).reshape(IMAGES, PATCHES, UNITS)
    out_ref[0, :, 0, :, UNITS:] = grad.astype(BF16).reshape(IMAGES, PATCHES, UNITS)
    flag_ref[...] = jnp.zeros_like(flag_ref)


def products(gathered, w_in, w_out):
    parts, _, rows, dblock = gathered.shape

    def half(which):
        return pl.BlockSpec((parts, pl.squeezed, rows, dblock), lambda s: (0, which, 0, 0))

    def w_cols(a):
        return pl.BlockSpec(
            (dblock, HEAD), lambda s: (0, jnp.where(s < 2, s + 2 * a, 3 * s + a))
        )

    def v_rows(a):
        return pl.BlockSpec((HEAD, dblock), lambda s: (jnp.where(s < 2, s, 3 * s - 4 + a), 0))

    return pl.pallas_call(
        products_kernel,
        out_shape=(
            pltpu.HBM((2, IMAGES, 2, PATCHES, 2 * UNITS), BF16),
            pltpu.HBM((8, HEAD), F32),
        ),
        grid=(4,),
        in_specs=[half(0), half(1)]
        + [w_cols(a) for a in range(3)]
        + [v_rows(a) for a in range(3)],
        out_specs=[
            pl.BlockSpec((1, IMAGES, 1, PATCHES, 2 * UNITS), lambda s: (s // 2, 0, s % 2, 0, 0)),
            pl.BlockSpec((8, HEAD), lambda s: (0, 0)),
        ],
        compiler_params=params(),
        interpret=INTERPRET,
    )(gathered, gathered, *[stay(w_in)] * 3, *[stay(w_out)] * 3)


def exact(a, b, contract):
    return lax.dot_general(
        a, b, (contract, ((), ())), precision=lax.Precision.HIGHEST, preferred_element_type=F32
    )


def head_norm(values):
    center = values - jnp.mean(values, axis=-1, keepdims=True)
    scale = lax.rsqrt(jnp.mean(center * center, axis=-1, keepdims=True) + EPS)
    return center * scale, scale


def head_norm_pull(normed, scale, grad):
    along = jnp.mean(grad * normed, axis=-1, keepdims=True)
    return scale * (grad - jnp.mean(grad, axis=-1, keepdims=True) - normed * along)


def unit_kernel(place_ref, terms_ref, earlier_ref, hidden_ref, d_pre_ref):
    summed = terms_ref[0].astype(F32)
    for part in range(1, terms_ref.shape[0]):
        summed = summed + terms_ref[part].astype(F32)
    pre = summed[:, :UNITS].astype(BF16).astype(F32)
    grad = summed[:, UNITS:]

    @pl.when(place_ref[0] < 4)
    def attention():
        value = pre[:, 2 * HEAD :]
        d_out = grad[:, :HEAD]
        query, query_scale = head_norm(pre[:, :HEAD])
        key, key_scale = head_norm(pre[:, HEAD : 2 * HEAD])
        weights = jnp.exp(exact(query, key, ((1,), (1,))) * HEAD ** (-0.5))
        weights = weights / jnp.sum(weights, axis=-1, keepdims=True)
        out = exact(weights, value, ((1,), (0,)))
        d_value = exact(weights, d_out, ((0,), (0,)))
        d_weights = exact(d_out, value, ((1,), (1,)))
        along = jnp.sum(d_weights * weights, axis=-1, keepdims=True)
        d_scores = weights * (d_weights - along) * HEAD ** (-0.5)
        d_query = exact(d_scores, key, ((1,), (0,)))
        d_key = exact(d_scores, query, ((0,), (0,)))
        for i in range(IMAGES):
            hidden_ref[i, :, :HEAD] = out.astype(BF16)
            hidden_ref[i, :, HEAD:] = jnp.zeros((PATCHES, 2 * HEAD), BF16)
        d_pre_ref[:, :HEAD] = head_norm_pull(query, query_scale, d_query).astype(BF16)
        d_pre_ref[:, HEAD : 2 * HEAD] = head_norm_pull(key, key_scale, d_key).astype(BF16)
        d_pre_ref[:, 2 * HEAD :] = d_value.astype(BF16)

    @pl.when(place_ref[0] >= 4)
    def units():
        below = 0.5 * (1.0 + lax.erf(pre * 2.0**-0.5))
        density = jnp.exp(-0.5 * pre * pre) * 0.3989422804014327
        for i in range(IMAGES):
            hidden_ref[i] = (pre * below).astype(BF16)
        d_pre_ref[...] = (grad * (below + pre * density)).astype(BF16)


def unit(place, terms, earlier):
    return pl.pallas_call(
        unit_kernel,
        out_shape=(
            jax.ShapeDtypeStruct((IMAGES, PATCHES, UNITS), BF16),
            jax.ShapeDtypeStruct((PATCHES, UNITS), BF16),
        ),
        grid_spec=pltpu.PrefetchScalarGridSpec(
            num_scalar_prefetch=1,
            grid=(1,),
            in_specs=[
                pl.BlockSpec(terms.shape, lambda s, place: (0, 0, 0)),
                pl.BlockSpec(memory_space=pl.ANY),
            ],
            out_specs=[
                pl.BlockSpec((IMAGES, PATCHES, UNITS), lambda s, place: (0, 0, 0)),
                pl.BlockSpec((PATCHES, UNITS), lambda s, place: (0, 0)),
            ],
        ),
        compiler_params=params(),
        interpret=INTERPRET,
    )(place, terms, earlier)


def by_owner_kernel(place_ref, pieces_ref, earlier_ref, out_ref):
    for s in range(2):
        out_ref[s] = pieces_ref[0, 0, s, :, :HEAD]
        for a in range(3):
            out_ref[2 + 3 * s + a] = pieces_ref[1, 0, s, :, a * HEAD : (a + 1) * HEAD]


def by_owner(place, pieces, earlier):
    rows = pieces.shape[-2]
    return pl.pallas_call(
        by_owner_kernel,
        out_shape=jax.ShapeDtypeStruct((8, rows, HEAD), BF16),
        grid_spec=pltpu.PrefetchScalarGridSpec(
            num_scalar_prefetch=1,
            grid=(1,),
            in_specs=[
                pl.BlockSpec(
                    (2, 1, 2, rows, UNITS), lambda s, place: (0, place[0] // 4, 0, 0, 0)
                ),
                pl.BlockSpec(memory_space=pl.ANY),
            ],
            out_specs=pl.BlockSpec((8, rows, HEAD), lambda s, place: (0, 0, 0)),
        ),
        compiler_params=params(),
        interpret=INTERPRET,
    )(place, pieces, earlier)


def halves_kernel(side_ref, keep_in, give_in, earlier_ref, keep_ref, give_ref):
    keep_ref[...] = keep_in[...].reshape(keep_ref.shape)
    give_ref[...] = give_in[...].reshape(give_ref.shape)


def halves(side, gathered, earlier):
    parts, _, rows, dblock = gathered.shape
    half = dblock // 2
    block = (parts, pl.squeezed, rows, half)
    shape = jax.ShapeDtypeStruct((parts * rows, half), BF16)
    return pl.pallas_call(
        halves_kernel,
        out_shape=(shape, shape),
        grid_spec=pltpu.PrefetchScalarGridSpec(
            num_scalar_prefetch=1,
            grid=(1,),
            in_specs=[
                pl.BlockSpec(block, lambda s, side: (0, 0, 0, side[0])),
                pl.BlockSpec(block, lambda s, side: (0, 0, 0, 1 - side[0])),
                pl.BlockSpec(memory_space=pl.ANY),
            ],
            out_specs=[pl.BlockSpec((parts * rows, half), lambda s, side: (0, 0))] * 2,
        ),
        compiler_params=params(),
        interpret=INTERPRET,
    )(side, gathered, gathered, stay(earlier))


def cotangent_kernel(rows_ref, *refs):
    refs[-1][...] = rows_ref[...]


def cotangent_rows(gathered, count, earlier):
    groups, _, rows, dblock = gathered.shape
    return pl.pallas_call(
        cotangent_kernel,
        out_shape=jax.ShapeDtypeStruct((groups, count, dblock), BF16),
        grid=(1,),
        in_specs=[
            pl.BlockSpec((groups, pl.squeezed, count, dblock), lambda s: (0, 1, 0, 0)),
        ]
        + [pl.BlockSpec(memory_space=pl.ANY)] * len(earlier),
        out_specs=pl.BlockSpec((groups, count, dblock), lambda s: (0, 0, 0)),
        compiler_params=params(),
        interpret=INTERPRET,
    )(stay(gathered), *earlier)


def grad_out_kernel(hidden_ref, cot_ref, out_ref, flag_ref, sum_ref):
    step = pl.program_id(0)
    total = cot_ref.shape[0] * cot_ref.shape[1] * cot_ref.shape[2]
    hidden = hidden_ref[...].reshape(total, HEAD)
    cot = cot_ref[...].reshape(total, cot_ref.shape[-1])
    terms = lax.dot_general(hidden, cot, (((0,), (0,)), ((), ())), preferred_element_type=F32)

    @pl.when(step == 0)
    def first():
        sum_ref[...] = terms

    @pl.when(step > 0)
    def later():
        sum_ref[...] += terms

    @pl.when(step == pl.num_programs(0) - 1)
    def last():
        out_ref[...] = sum_ref[...].astype(BF16)
        flag_ref[...] = jnp.zeros_like(flag_ref)


def grad_out_rows(hidden, cot):
    lines, groups, rows, dblock = cot.shape
    steps = 2 if lines % 2 == 0 else 1
    return pl.pallas_call(
        grad_out_kernel,
        out_shape=(
            jax.ShapeDtypeStruct((HEAD, dblock), BF16),
            pltpu.HBM((8, HEAD), F32),
        ),
        grid=(steps,),
        in_specs=[
            pl.BlockSpec((lines // steps, groups, rows, HEAD), lambda s: (s, 0, 0, 0)),
            pl.BlockSpec((lines // steps, groups, rows, dblock), lambda s: (s, 0, 0, 0)),
        ],
        out_specs=[
            pl.BlockSpec((HEAD, dblock), lambda s: (0, 0)),
            pl.BlockSpec((8, HEAD), lambda s: (0, 0)),
        ],
        scratch_shapes=[pltpu.VMEM((HEAD, dblock), F32)],
        compiler_params=params(),
        interpret=INTERPRET,
    )(hidden, stay(cot))


def grad_in_kernel(y_own_ref, y_other_ref, own_ref, other_ref, out_ref):
    dims = (((0,), (0,)), ((), ()))
    y = jnp.concatenate([y_own_ref[...], y_other_ref[...]], axis=0)
    for s in range(4):
        base = s if s < 2 else s + 2
        d_pre = jnp.concatenate(
            [own_ref[base], own_ref[base + 2], other_ref[base], other_ref[base + 2]], axis=0
        )
        terms = lax.dot_general(y, d_pre, dims, preferred_element_type=F32).astype(BF16)
        if s < 2:
            for a in range(3):
                first = (2 * a + s) * HEAD
                out_ref[:, first : first + HEAD] = terms[:, a * HEAD : (a + 1) * HEAD]
        else:
            first = 6 * HEAD + (s - 2) * UNITS
            out_ref[:, first : first + UNITS] = terms


def grad_in_terms(y_own, y_other, own, other):
    features = y_own.shape[-1]
    width = 6 * HEAD + 2 * UNITS
    y = pl.BlockSpec(y_own.shape, lambda s: (0, 0))
    whole = pl.BlockSpec(own.shape, lambda s: (0, 0, 0))
    return pl.pallas_call(
        grad_in_kernel,
        out_shape=jax.ShapeDtypeStruct((features, width), BF16),
        grid=(1,),
        in_specs=[y, y, whole, whole],
        out_specs=pl.BlockSpec((features, width), lambda s: (0, 0)),
        compiler_params=params(),
        interpret=INTERPRET,
    )(y_own, y_other, own, other)


def sum_kernel(parts_ref, earlier_ref, out_ref):
    summed = parts_ref[0].astype(F32)
    for part in range(1, parts_ref.shape[0]):
        summed = summed + parts_ref[part].astype(F32)
    out_ref[...] = summed.astype(BF16)


def sum_parts(parts, earlier):
    shape = parts.shape[1:]
    return pl.pallas_call(
        sum_kernel,
        out_shape=jax.ShapeDtypeStruct(shape, BF16),
        grid=(1,),
        in_specs=[
            pl.BlockSpec(parts.shape, lambda s: (0, 0, 0)),
            pl.BlockSpec(memory_space=pl.ANY),
        ],
        out_specs=pl.BlockSpec(shape, lambda s: (0, 0)),
        compiler_params=params(),
        interpret=INTERPRET,
    )(parts, stay(earlier))


def swap(values, axis):
    return lax.ppermute(values, axis, [(0, 1), (1, 0)])


def send(values, axis):
    shape = values.shape
    flat = values.reshape((shape[0] * shape[1],) + shape[2:])
    return lax.all_to_all(flat, axis, 0, 0, tiled=True).reshape(shape)


def shards(tokens, w_in, w_out, cotangent):
    parts = lax.axis_size(MY)
    groups = lax.axis_size(DP)
    place = lax.axis_index(MY).astype(jnp.int32).reshape(1)
    side = lax.axis_index("dh").astype(jnp.int32).reshape(1)
    dblock = w_in.shape[0]
    total = IMAGES * PATCHES
    kinds = (2, IMAGES, 2)
    lines = 8
    block = total // lines

    with jax.named_scope("token_rows"):
        mine = norm_rows(place, tokens, cotangent)
        rows, longer = join_rows(mine, swap(mine, "zh"))
        gathered = lax.all_gather(rows, "y", axis=0, tiled=False)

    with jax.named_scope("units"):
        partial, flag = products(gathered, w_in, w_out)
        terms = send(partial.reshape(parts, PATCHES, 2 * UNITS), MY)

    with jax.named_scope("y_of_two_groups"):
        y_own, y_give = halves(side, gathered, flag)
        y_other = swap(y_give, "dh")

    with jax.named_scope("units"):
        hidden, d_pre = unit(place, terms, y_own)

    with jax.named_scope("d_pre_of_two_groups"):
        d_pre_other = swap(d_pre, "dh")
        own = lax.all_gather(d_pre, MY, axis=0, tiled=False)
        other = lax.all_gather(d_pre_other, MY, axis=0, tiled=False)
        grad_in = grad_in_terms(y_own, y_other, own, other)
        grad_in = send(grad_in.reshape(4, dblock // 8, grad_in.shape[1]), "dl")

    with jax.named_scope("hidden_of_all_groups"):
        pieces = send(hidden.reshape(parts, block, UNITS), MY)
        owned = by_owner(place, pieces.reshape(kinds + (block, UNITS)), own)

    with jax.named_scope("cotangent_of_all_groups"):
        count = rows.shape[1]
        cot_rows = lax.all_gather(longer, DP, axis=0, tiled=False)
        cot_rows = cotangent_rows(cot_rows, count, (owned, d_pre_other, y_other))
        cot_all = lax.all_gather(cot_rows, "y", axis=0, tiled=False)
        held = cot_all.shape[0]
        cot_all = cot_all.reshape(held, groups, lines // held, block, dblock)
        cot_all = cot_all.swapaxes(1, 2).reshape(lines, groups, block, dblock)

    with jax.named_scope("hidden_of_all_groups"):
        owned = lax.all_gather(send(owned, DP), MY, axis=0, tiled=False)
        grad_out, done = grad_out_rows(owned, cot_all)

    with jax.named_scope("grad_in_sum"):
        grad_in = sum_parts(grad_in, done)

    return grad_in[None], grad_out[None]


def solution(mesh):
    sizes = dict(mesh.shape)
    lines = sizes["mx"] // 2
    cut = (2, sizes["dp"] // 2, lines, 2, sizes["my"] // 2, 2)
    fine = Mesh(mesh.devices.reshape(cut), DP + MX + MY)
    return jax.shard_map(
        shards,
        mesh=fine,
        in_specs=(P(DP + MX, None), P(MY, MX), P(MX, MY), P(DP + MX, MY)),
        out_specs=(P(DP, MY, MX), P(DP, MX, MY)),
        check_vma=False,
    )
```

```python
import functools

import jax
import jax.numpy as jnp
from jax import lax
from jax.experimental import pallas as pl
from jax.experimental.pallas import tpu as pltpu
from jax.sharding import Mesh
from jax.sharding import PartitionSpec as P

HEAD = 128
HEADS_DEV = 2
PATCHES = 128
IMAGES = 2
UNITS = 384
EPS = 1e-06

INTERPRET = False
VMEM_LIMIT = 48 * 2**20

DP = ("dh", "dl")
MX = ("y", "zh")
MY = ("x", "c")

F32 = jnp.float32
BF16 = jnp.bfloat16


def stay(values):
    return pltpu.with_memory_space_constraint(values, pltpu.HBM)


def params():
    return pltpu.CompilerParams(vmem_limit_bytes=VMEM_LIMIT)


def norm_kernel(place_ref, tokens_ref, mine_ref, cot_ref, out_ref):
    x = tokens_ref[...].astype(F32)
    mean = jnp.mean(x, axis=-1, keepdims=True)
    center = x - mean
    spread = jnp.mean(center * center, axis=-1, keepdims=True)
    mine = (mine_ref[...].astype(F32) - mean) * lax.rsqrt(spread + EPS)
    out_ref[0] = mine.astype(BF16)
    out_ref[1] = cot_ref[...]


def norm_rows(place, tokens, cotangent):
    rows, features = tokens.shape
    dblock = cotangent.shape[1]
    return pl.pallas_call(
        norm_kernel,
        out_shape=jax.ShapeDtypeStruct((2, rows, dblock), BF16),
        grid_spec=pltpu.PrefetchScalarGridSpec(
            num_scalar_prefetch=1,
            grid=(1,),
            in_specs=[
                pl.BlockSpec((rows, features), lambda s, place: (0, 0)),
                pl.BlockSpec((rows, dblock), lambda s, place: (0, place[0])),
                pl.BlockSpec((rows, dblock), lambda s, place: (0, 0)),
            ],
            out_specs=pl.BlockSpec((2, rows, dblock), lambda s, place: (0, 0, 0)),
        ),
        compiler_params=params(),
        interpret=INTERPRET,
    )(place, stay(tokens), stay(tokens), stay(cotangent))


def longer_kernel(rows_ref, out_ref):
    sides, kinds, count, _ = rows_ref.shape
    for third, kind in enumerate((1, 0, 1)):
        for side in range(sides):
            first = (third * sides + side) * count
            out_ref[first : first + count] = rows_ref[side, kind]


def longer_rows(rows):
    sides, _, count, dblock = rows.shape
    shape = (3 * sides * count, dblock)
    return pl.pallas_call(
        longer_kernel,
        out_shape=jax.ShapeDtypeStruct(shape, BF16),
        grid=(1,),
        in_specs=[pl.BlockSpec(rows.shape, lambda s: (0, 0, 0, 0))],
        out_specs=pl.BlockSpec(shape, lambda s: (0, 0)),
        compiler_params=params(),
        interpret=INTERPRET,
    )(rows)


def products_kernel(y_ref, cot_ref, w_ref, va, vb, vc, out_ref, flag_ref):
    total = IMAGES * PATCHES
    dblock = w_ref.shape[0]
    y = y_ref[...].reshape(total, dblock)
    cot = cot_ref[...].reshape(total, dblock)
    pre = jnp.dot(y, w_ref[...], preferred_element_type=F32).astype(BF16)
    flag_ref[...] = jnp.zeros_like(flag_ref)

    def back(v):
        terms = lax.dot_general(cot, v, (((1,), (1,)), ((), ())), preferred_element_type=F32)
        return terms.astype(BF16)

    def put(s, first, values):
        width = values.shape[1]
        out_ref[0, :, s, :, first : first + width] = values.reshape(IMAGES, PATCHES, width)

    @pl.when(pl.program_id(0) == 0)
    def heads():
        grad = back(va[...])
        for s in range(2):
            for a in range(3):
                first = (2 * a + s) * HEAD
                put(s, a * HEAD, pre[:, first : first + HEAD])
            put(s, UNITS, grad[:, s * HEAD : (s + 1) * HEAD])
            put(s, UNITS + HEAD, jnp.zeros((total, 2 * HEAD), BF16))

    @pl.when(pl.program_id(0) == 1)
    def units():
        grad = back(jnp.concatenate([va[...], vb[...], vc[...]], axis=0))
        for s in range(2):
            put(s, 0, pre[:, s * UNITS : (s + 1) * UNITS])
            put(s, UNITS, grad[:, s * UNITS : (s + 1) * UNITS])


def products(gathered, w_in, w_out):
    lines, sides, _, rows, dblock = gathered.shape

    def kind(which):
        return pl.BlockSpec(
            (lines, sides, pl.squeezed, rows, dblock), lambda s: (0, 0, which, 0, 0)
        )

    def v_rows(block):
        return pl.BlockSpec((2 * HEAD, dblock), lambda s: (block(s), 0))

    return pl.pallas_call(
        products_kernel,
        out_shape=(
            pltpu.HBM((2, IMAGES, 2, PATCHES, 2 * UNITS), BF16),
            pltpu.HBM((8, HEAD), F32),
        ),
        grid=(2,),
        in_specs=[
            kind(0),
            kind(1),
            pl.BlockSpec((dblock, 2 * UNITS), lambda s: (0, s)),
            v_rows(lambda s: s),
            v_rows(lambda s: 2),
            v_rows(lambda s: 3),
        ],
        out_specs=[
            pl.BlockSpec((1, IMAGES, 2, PATCHES, 2 * UNITS), lambda s: (s, 0, 0, 0, 0)),
            pl.BlockSpec((8, HEAD), lambda s: (0, 0)),
        ],
        compiler_params=params(),
        interpret=INTERPRET,
    )(gathered, gathered, stay(w_in), *[stay(w_out)] * 3)


def exact(a, b, contract):
    return lax.dot_general(
        a, b, (contract, ((), ())), precision=lax.Precision.HIGHEST, preferred_element_type=F32
    )


def head_norm(values):
    center = values - jnp.mean(values, axis=-1, keepdims=True)
    scale = lax.rsqrt(jnp.mean(center * center, axis=-1, keepdims=True) + EPS)
    return center * scale, scale


def head_norm_pull(normed, scale, grad):
    along = jnp.mean(grad * normed, axis=-1, keepdims=True)
    return scale * (grad - jnp.mean(grad, axis=-1, keepdims=True) - normed * along)


def unit_kernel(place_ref, terms_ref, earlier_ref, hidden_ref, d_pre_ref):
    summed = terms_ref[0].astype(F32)
    for part in range(1, terms_ref.shape[0]):
        summed = summed + terms_ref[part].astype(F32)
    pre = summed[:, :UNITS].astype(BF16).astype(F32)
    grad = summed[:, UNITS:]

    @pl.when(place_ref[0] < 4)
    def attention():
        value = pre[:, 2 * HEAD :]
        d_out = grad[:, :HEAD]
        query, query_scale = head_norm(pre[:, :HEAD])
        key, key_scale = head_norm(pre[:, HEAD : 2 * HEAD])
        weights = jnp.exp(exact(query, key, ((1,), (1,))) * HEAD ** (-0.5))
        weights = weights / jnp.sum(weights, axis=-1, keepdims=True)
        out = exact(weights, value, ((1,), (0,)))
        d_value = exact(weights, d_out, ((0,), (0,)))
        d_weights = exact(d_out, value, ((1,), (1,)))
        along = jnp.sum(d_weights * weights, axis=-1, keepdims=True)
        d_scores = weights * (d_weights - along) * HEAD ** (-0.5)
        d_query = exact(d_scores, key, ((1,), (0,)))
        d_key = exact(d_scores, query, ((0,), (0,)))
        for i in range(IMAGES):
            hidden_ref[i, :, :HEAD] = out.astype(BF16)
            hidden_ref[i, :, HEAD:] = jnp.zeros((PATCHES, 2 * HEAD), BF16)
        d_pre_ref[:, :HEAD] = head_norm_pull(query, query_scale, d_query).astype(BF16)
        d_pre_ref[:, HEAD : 2 * HEAD] = head_norm_pull(key, key_scale, d_key).astype(BF16)
        d_pre_ref[:, 2 * HEAD :] = d_value.astype(BF16)

    @pl.when(place_ref[0] >= 4)
    def units():
        below = 0.5 * (1.0 + lax.erf(pre * 2.0**-0.5))
        density = jnp.exp(-0.5 * pre * pre) * 0.3989422804014327
        for i in range(IMAGES):
            hidden_ref[i] = (pre * below).astype(BF16)
        d_pre_ref[...] = (grad * (below + pre * density)).astype(BF16)


def unit(place, terms, earlier):
    return pl.pallas_call(
        unit_kernel,
        out_shape=(
            jax.ShapeDtypeStruct((IMAGES, PATCHES, UNITS), BF16),
            jax.ShapeDtypeStruct((PATCHES, UNITS), BF16),
        ),
        grid_spec=pltpu.PrefetchScalarGridSpec(
            num_scalar_prefetch=1,
            grid=(1,),
            in_specs=[
                pl.BlockSpec(terms.shape, lambda s, place: (0, 0, 0)),
                pl.BlockSpec(memory_space=pl.ANY),
            ],
            out_specs=[
                pl.BlockSpec((IMAGES, PATCHES, UNITS), lambda s, place: (0, 0, 0)),
                pl.BlockSpec((PATCHES, UNITS), lambda s, place: (0, 0)),
            ],
        ),
        compiler_params=params(),
        interpret=INTERPRET,
    )(place, terms, earlier)


def by_owner_kernel(place_ref, pieces_ref, earlier_ref, out_ref):
    for s in range(2):
        out_ref[s] = pieces_ref[0, 0, s, :, :HEAD]
        for a in range(3):
            out_ref[2 + 3 * s + a] = pieces_ref[1, 0, s, :, a * HEAD : (a + 1) * HEAD]


def by_owner(place, pieces, earlier):
    rows = pieces.shape[-2]
    return pl.pallas_call(
        by_owner_kernel,
        out_shape=jax.ShapeDtypeStruct((8, rows, HEAD), BF16),
        grid_spec=pltpu.PrefetchScalarGridSpec(
            num_scalar_prefetch=1,
            grid=(1,),
            in_specs=[
                pl.BlockSpec(
                    (2, 1, 2, rows, UNITS), lambda s, place: (0, place[0] // 4, 0, 0, 0)
                ),
                pl.BlockSpec(memory_space=pl.ANY),
            ],
            out_specs=pl.BlockSpec((8, rows, HEAD), lambda s, place: (0, 0, 0)),
        ),
        compiler_params=params(),
        interpret=INTERPRET,
    )(place, pieces, earlier)


def halves_kernel(side_ref, keep_in, give_in, earlier_ref, keep_ref, give_ref):
    for given, ref in ((keep_in, keep_ref), (give_in, give_ref)):
        ref[...] = given[...].reshape(ref.shape[1], ref.shape[0]).T


def halves(side, gathered, earlier):
    lines, sides, _, rows, dblock = gathered.shape
    half = dblock // 2
    block = (lines, sides, pl.squeezed, rows, half)
    turned = (half, lines * sides * rows)
    shape = jax.ShapeDtypeStruct(turned, BF16)
    return pl.pallas_call(
        halves_kernel,
        out_shape=(shape, shape),
        grid_spec=pltpu.PrefetchScalarGridSpec(
            num_scalar_prefetch=1,
            grid=(1,),
            in_specs=[
                pl.BlockSpec(block, lambda s, side: (0, 0, 0, 0, side[0])),
                pl.BlockSpec(block, lambda s, side: (0, 0, 0, 0, 1 - side[0])),
                pl.BlockSpec(memory_space=pl.ANY),
            ],
            out_specs=[pl.BlockSpec(turned, lambda s, side: (0, 0))] * 2,
        ),
        compiler_params=params(),
        interpret=INTERPRET,
    )(side, gathered, gathered, stay(earlier))


def cotangent_kernel(count, rows_ref, *refs):
    out_ref, done = refs[-2:]
    move = pltpu.make_async_copy(rows_ref.at[:, pl.ds(0, count)], out_ref, done)
    move.start()
    move.wait()


def cotangent_rows(gathered, count, earlier):
    groups, _, dblock = gathered.shape
    return pl.pallas_call(
        functools.partial(cotangent_kernel, count),
        out_shape=pltpu.HBM((groups, count, dblock), BF16),
        in_specs=[pl.BlockSpec(memory_space=pl.ANY)] * (1 + len(earlier)),
        out_specs=pl.BlockSpec(memory_space=pl.ANY),
        scratch_shapes=[pltpu.SemaphoreType.DMA],
        compiler_params=params(),
        interpret=INTERPRET,
    )(stay(gathered), *earlier)


def grad_out_kernel(hidden_ref, cot_ref, out_ref, flag_ref, sum_ref):
    step = pl.program_id(0)
    total = cot_ref.shape[0] * cot_ref.shape[1] * cot_ref.shape[2]
    hidden = hidden_ref[...].reshape(total, HEAD)
    cot = cot_ref[...].reshape(total, cot_ref.shape[-1])
    terms = lax.dot_general(hidden, cot, (((0,), (0,)), ((), ())), preferred_element_type=F32)

    @pl.when(step == 0)
    def first():
        sum_ref[...] = terms

    @pl.when(step > 0)
    def later():
        sum_ref[...] += terms

    @pl.when(step == pl.num_programs(0) - 1)
    def last():
        out_ref[...] = sum_ref[...].astype(BF16)
        flag_ref[...] = jnp.zeros_like(flag_ref)


def grad_out_rows(hidden, cot):
    lines, groups, rows, dblock = cot.shape
    steps = 2 if lines % 2 == 0 else 1
    return pl.pallas_call(
        grad_out_kernel,
        out_shape=(
            jax.ShapeDtypeStruct((HEAD, dblock), BF16),
            pltpu.HBM((8, HEAD), F32),
        ),
        grid=(steps,),
        in_specs=[
            pl.BlockSpec((lines // steps, groups, rows, HEAD), lambda s: (s, 0, 0, 0)),
            pl.BlockSpec((lines // steps, groups, rows, dblock), lambda s: (s, 0, 0, 0)),
        ],
        out_specs=[
            pl.BlockSpec((HEAD, dblock), lambda s: (0, 0)),
            pl.BlockSpec((8, HEAD), lambda s: (0, 0)),
        ],
        scratch_shapes=[pltpu.VMEM((HEAD, dblock), F32)],
        compiler_params=params(),
        interpret=INTERPRET,
    )(hidden, stay(cot))


def grad_in_kernel(y_own_ref, y_other_ref, own_ref, other_ref, out_ref):
    for t in range(2):
        terms = 0.0
        for y_ref, ref in ((y_own_ref, own_ref), (y_other_ref, other_ref)):
            rows = [
                jnp.concatenate([ref[4 * t + 2 * i + s] for s in range(2)], axis=1)
                for i in range(IMAGES)
            ]
            d_pre = jnp.concatenate(rows, axis=0)
            terms = terms + jnp.dot(y_ref[...], d_pre, preferred_element_type=F32)
        terms = terms.astype(BF16)
        if t == 0:
            for s in range(2):
                for a in range(3):
                    first, from_ = (2 * a + s) * HEAD, (3 * s + a) * HEAD
                    out_ref[:, first : first + HEAD] = terms[:, from_ : from_ + HEAD]
        else:
            out_ref[:, 2 * UNITS :] = terms


def grad_in_terms(y_own, y_other, own, other):
    features = y_own.shape[0]
    width = 4 * UNITS
    y = pl.BlockSpec(y_own.shape, lambda s: (0, 0))
    whole = pl.BlockSpec(own.shape, lambda s: (0, 0, 0))
    return pl.pallas_call(
        grad_in_kernel,
        out_shape=pltpu.HBM((features, width), BF16),
        grid=(1,),
        in_specs=[y, y, whole, whole],
        out_specs=pl.BlockSpec((features, width), lambda s: (0, 0)),
        compiler_params=params(),
        interpret=INTERPRET,
    )(y_own, y_other, own, other)


def sum_kernel(parts_ref, earlier_ref, out_ref):
    summed = parts_ref[0].astype(F32)
    for part in range(1, parts_ref.shape[0]):
        summed = summed + parts_ref[part].astype(F32)
    out_ref[...] = summed.astype(BF16)


def sum_parts(parts, earlier):
    shape = parts.shape[1:]
    return pl.pallas_call(
        sum_kernel,
        out_shape=jax.ShapeDtypeStruct(shape, BF16),
        grid=(1,),
        in_specs=[
            pl.BlockSpec(parts.shape, lambda s: (0, 0, 0)),
            pl.BlockSpec(memory_space=pl.ANY),
        ],
        out_specs=pl.BlockSpec(shape, lambda s: (0, 0)),
        compiler_params=params(),
        interpret=INTERPRET,
    )(parts, stay(earlier))


def swap(values, axis):
    return lax.ppermute(values, axis, [(0, 1), (1, 0)])


def send(values, axis):
    shape = values.shape
    flat = values.reshape((shape[0] * shape[1],) + shape[2:])
    return lax.all_to_all(flat, axis, 0, 0, tiled=True).reshape(shape)


def shards(tokens, w_in, w_out, cotangent):
    parts = lax.axis_size(MY)
    groups = lax.axis_size(DP)
    place = lax.axis_index(MY).astype(jnp.int32).reshape(1)
    side = lax.axis_index("dh").astype(jnp.int32).reshape(1)
    dblock = w_in.shape[0]
    total = IMAGES * PATCHES
    kinds = (2, IMAGES, 2)
    lines = 8
    block = total // lines

    with jax.named_scope("token_rows"):
        mine = norm_rows(place, tokens, cotangent)
        rows = lax.all_gather(mine, "zh", axis=0, tiled=False)
        longer = longer_rows(rows)
        gathered = lax.all_gather(rows, "y", axis=0, tiled=False)

    with jax.named_scope("units"):
        partial, flag = products(gathered, w_in, w_out)
        terms = send(partial.reshape(parts, PATCHES, 2 * UNITS), MY)

    with jax.named_scope("y_of_two_groups"):
        y_own, y_give = halves(side, gathered, flag)
        y_other = swap(y_give, "dh")

    with jax.named_scope("units"):
        hidden, d_pre = unit(place, terms, y_own)

    with jax.named_scope("d_pre_of_two_groups"):
        d_pre_other = swap(d_pre, "dh")
        own = lax.all_gather(d_pre, MY, axis=0, tiled=False)
        other = lax.all_gather(d_pre_other, MY, axis=0, tiled=False)
        grad_in = grad_in_terms(y_own, y_other, own, other)
        grad_in = send(grad_in.reshape(4, dblock // 8, grad_in.shape[1]), "dl")

    with jax.named_scope("hidden_of_all_groups"):
        pieces = send(hidden.reshape(parts, block, UNITS), MY)
        owned = by_owner(place, pieces.reshape(kinds + (block, UNITS)), own)

    with jax.named_scope("cotangent_of_all_groups"):
        count = rows.shape[0] * rows.shape[2]
        cot_rows = lax.all_gather(longer, DP, axis=0, tiled=False)
        cot_rows = cotangent_rows(cot_rows, count, (owned, d_pre_other, y_other))
        cot_all = lax.all_gather(cot_rows, "y", axis=0, tiled=False)
        held = cot_all.shape[0]
        cot_all = cot_all.reshape(held, groups, lines // held, block, dblock)
        cot_all = cot_all.swapaxes(1, 2).reshape(lines, groups, block, dblock)

    with jax.named_scope("hidden_of_all_groups"):
        owned = lax.all_gather(send(owned, DP), MY, axis=0, tiled=False)
        grad_out, done = grad_out_rows(owned, cot_all)

    with jax.named_scope("grad_in_sum"):
        grad_in = sum_parts(grad_in, done)

    return grad_in[None], grad_out[None]


def solution(mesh):
    sizes = dict(mesh.shape)
    lines = sizes["mx"] // 2
    cut = (2, sizes["dp"] // 2, lines, 2, sizes["my"] // 2, 2)
    fine = Mesh(mesh.devices.reshape(cut), DP + MX + MY)
    return jax.shard_map(
        shards,
        mesh=fine,
        in_specs=(P(DP + MX, None), P(MY, MX), P(MX, MY), P(DP + MX, MY)),
        out_specs=(P(DP, MY, MX), P(DP, MX, MY)),
        check_vma=False,
    )
```

```python
import functools

import jax
import jax.numpy as jnp
from jax import lax
from jax.experimental import pallas as pl
from jax.experimental.pallas import tpu as pltpu
from jax.sharding import Mesh
from jax.sharding import PartitionSpec as P

HEAD = 128
HEADS_DEV = 2
PATCHES = 128
IMAGES = 2
UNITS = 384
EPS = 1e-06

INTERPRET = False
VMEM_LIMIT = 48 * 2**20

DP = ("dh", "dl")
Y = ("yh", "yl")
MX = Y + ("zh",)
MY = ("x", "c")

F32 = jnp.float32
BF16 = jnp.bfloat16


def stay(values):
    return pltpu.with_memory_space_constraint(values, pltpu.HBM)


def params():
    return pltpu.CompilerParams(vmem_limit_bytes=VMEM_LIMIT)


def norm_kernel(place_ref, tokens_ref, mine_ref, cot_ref, out_ref):
    x = tokens_ref[...].astype(F32)
    mean = jnp.mean(x, axis=-1, keepdims=True)
    center = x - mean
    spread = jnp.mean(center * center, axis=-1, keepdims=True)
    mine = (mine_ref[...].astype(F32) - mean) * lax.rsqrt(spread + EPS)
    out_ref[0] = mine.astype(BF16)
    out_ref[1] = cot_ref[...]


def norm_rows(place, tokens, cotangent):
    rows, features = tokens.shape
    dblock = cotangent.shape[1]
    return pl.pallas_call(
        norm_kernel,
        out_shape=jax.ShapeDtypeStruct((2, rows, dblock), BF16),
        grid_spec=pltpu.PrefetchScalarGridSpec(
            num_scalar_prefetch=1,
            grid=(1,),
            in_specs=[
                pl.BlockSpec((rows, features), lambda s, place: (0, 0)),
                pl.BlockSpec((rows, dblock), lambda s, place: (0, place[0])),
                pl.BlockSpec((rows, dblock), lambda s, place: (0, 0)),
            ],
            out_specs=pl.BlockSpec((2, rows, dblock), lambda s, place: (0, 0, 0)),
        ),
        compiler_params=params(),
        interpret=INTERPRET,
    )(place, stay(tokens), stay(tokens), stay(cotangent))


def copies_kernel(rows_ref, out_ref):
    sides, _, count, dblock = rows_ref.shape
    rows = rows_ref[:, 1].reshape(sides * count, dblock)
    for group in range(out_ref.shape[0]):
        out_ref[group] = rows


def cotangent_copies(rows, groups):
    sides, _, count, dblock = rows.shape
    shape = (groups, sides * count, dblock)
    return pl.pallas_call(
        copies_kernel,
        out_shape=pltpu.HBM(shape, BF16),
        grid=(1,),
        in_specs=[pl.BlockSpec(rows.shape, lambda s: (0, 0, 0, 0))],
        out_specs=pl.BlockSpec(shape, lambda s: (0, 0, 0)),
        compiler_params=params(),
        interpret=INTERPRET,
    )(rows)


def products_kernel(y_ref, cot_ref, w_ref, va, vb, vc, earlier_ref, out_ref):
    total = IMAGES * PATCHES
    dblock = w_ref.shape[0]
    y = y_ref[...].reshape(total, dblock)
    cot = cot_ref[...].reshape(total, dblock)
    pre = jnp.dot(y, w_ref[...], preferred_element_type=F32).astype(BF16)

    def back(v):
        terms = lax.dot_general(cot, v, (((1,), (1,)), ((), ())), preferred_element_type=F32)
        return terms.astype(BF16)

    def put(s, first, values):
        width = values.shape[1]
        out_ref[s, 0, :, :, first : first + width] = values.reshape(IMAGES, PATCHES, width)

    @pl.when(pl.program_id(0) == 0)
    def heads():
        grad = back(va[...])
        for s in range(2):
            for a in range(3):
                first = (2 * a + s) * HEAD
                put(s, a * HEAD, pre[:, first : first + HEAD])
            put(s, UNITS, grad[:, s * HEAD : (s + 1) * HEAD])
            put(s, UNITS + HEAD, jnp.zeros((total, 2 * HEAD), BF16))

    @pl.when(pl.program_id(0) == 1)
    def units():
        grad = back(jnp.concatenate([va[...], vb[...], vc[...]], axis=0))
        for s in range(2):
            put(s, 0, pre[:, s * UNITS : (s + 1) * UNITS])
            put(s, UNITS, grad[:, s * UNITS : (s + 1) * UNITS])


def products(gathered, w_in, w_out, earlier):
    lines, sides, _, rows, dblock = gathered.shape

    def kind(which):
        return pl.BlockSpec(
            (lines, sides, pl.squeezed, rows, dblock), lambda s: (0, 0, which, 0, 0)
        )

    def v_rows(block):
        return pl.BlockSpec((2 * HEAD, dblock), lambda s: (block(s), 0))

    return pl.pallas_call(
        products_kernel,
        out_shape=pltpu.HBM((2, 2, IMAGES, PATCHES, 2 * UNITS), BF16),
        grid=(2,),
        in_specs=[
            kind(0),
            kind(1),
            pl.BlockSpec((dblock, 2 * UNITS), lambda s: (0, s)),
            v_rows(lambda s: s),
            v_rows(lambda s: 2),
            v_rows(lambda s: 3),
            pl.BlockSpec(memory_space=pl.ANY),
        ],
        out_specs=pl.BlockSpec((2, 1, IMAGES, PATCHES, 2 * UNITS), lambda s: (0, s, 0, 0, 0)),
        compiler_params=params(),
        interpret=INTERPRET,
    )(gathered, gathered, stay(w_in), *[stay(w_out)] * 3, earlier)


def pair_kernel(terms_ref, out_ref, flag_ref):
    out_ref[...] = (terms_ref[0].astype(F32) + terms_ref[1].astype(F32)).astype(BF16)
    flag_ref[...] = jnp.zeros_like(flag_ref)


def pair_sum(terms):
    _, rows, width = terms.shape
    return pl.pallas_call(
        pair_kernel,
        out_shape=(pltpu.HBM((rows, width), BF16), pltpu.HBM((8, HEAD), F32)),
        grid=(2,),
        in_specs=[pl.BlockSpec((2, rows // 2, width), lambda s: (0, s, 0))],
        out_specs=[
            pl.BlockSpec((rows // 2, width), lambda s: (s, 0)),
            pl.BlockSpec((8, HEAD), lambda s: (0, 0)),
        ],
        compiler_params=params(),
        interpret=INTERPRET,
    )(terms)


def exact(a, b, contract):
    return lax.dot_general(
        a, b, (contract, ((), ())), precision=lax.Precision.HIGHEST, preferred_element_type=F32
    )


def head_norm(values):
    center = values - jnp.mean(values, axis=-1, keepdims=True)
    scale = lax.rsqrt(jnp.mean(center * center, axis=-1, keepdims=True) + EPS)
    return center * scale, scale


def head_norm_pull(normed, scale, grad):
    along = jnp.mean(grad * normed, axis=-1, keepdims=True)
    return scale * (grad - jnp.mean(grad, axis=-1, keepdims=True) - normed * along)


def unit_kernel(place_ref, terms_ref, earlier_ref, hidden_ref, d_pre_ref):
    summed = terms_ref[0].astype(F32)
    for part in range(1, terms_ref.shape[0]):
        summed = summed + terms_ref[part].astype(F32)
    pre = summed[:, :UNITS].astype(BF16).astype(F32)
    grad = summed[:, UNITS:]

    @pl.when(place_ref[0] < 4)
    def attention():
        value = pre[:, 2 * HEAD :]
        d_out = grad[:, :HEAD]
        query, query_scale = head_norm(pre[:, :HEAD])
        key, key_scale = head_norm(pre[:, HEAD : 2 * HEAD])
        weights = jnp.exp(exact(query, key, ((1,), (1,))) * HEAD ** (-0.5))
        weights = weights / jnp.sum(weights, axis=-1, keepdims=True)
        out = exact(weights, value, ((1,), (0,)))
        d_value = exact(weights, d_out, ((0,), (0,)))
        d_weights = exact(d_out, value, ((1,), (1,)))
        along = jnp.sum(d_weights * weights, axis=-1, keepdims=True)
        d_scores = weights * (d_weights - along) * HEAD ** (-0.5)
        d_query = exact(d_scores, key, ((1,), (0,)))
        d_key = exact(d_scores, query, ((0,), (0,)))
        for i in range(IMAGES):
            hidden_ref[i, :, :HEAD] = out.astype(BF16)
            hidden_ref[i, :, HEAD:] = jnp.zeros((PATCHES, 2 * HEAD), BF16)
        d_pre_ref[:, :HEAD] = head_norm_pull(query, query_scale, d_query).astype(BF16)
        d_pre_ref[:, HEAD : 2 * HEAD] = head_norm_pull(key, key_scale, d_key).astype(BF16)
        d_pre_ref[:, 2 * HEAD :] = d_value.astype(BF16)

    @pl.when(place_ref[0] >= 4)
    def units():
        below = 0.5 * (1.0 + lax.erf(pre * 2.0**-0.5))
        density = jnp.exp(-0.5 * pre * pre) * 0.3989422804014327
        for i in range(IMAGES):
            hidden_ref[i] = (pre * below).astype(BF16)
        d_pre_ref[...] = (grad * (below + pre * density)).astype(BF16)


def unit(place, terms, earlier):
    return pl.pallas_call(
        unit_kernel,
        out_shape=(
            jax.ShapeDtypeStruct((IMAGES, PATCHES, UNITS), BF16),
            jax.ShapeDtypeStruct((PATCHES, UNITS), BF16),
        ),
        grid_spec=pltpu.PrefetchScalarGridSpec(
            num_scalar_prefetch=1,
            grid=(1,),
            in_specs=[
                pl.BlockSpec(terms.shape, lambda s, place: (0, 0, 0)),
                pl.BlockSpec(memory_space=pl.ANY),
            ],
            out_specs=[
                pl.BlockSpec((IMAGES, PATCHES, UNITS), lambda s, place: (0, 0, 0)),
                pl.BlockSpec((PATCHES, UNITS), lambda s, place: (0, 0)),
            ],
        ),
        compiler_params=params(),
        interpret=INTERPRET,
    )(place, terms, earlier)


def by_owner_kernel(place_ref, pieces_ref, earlier_ref, out_ref):
    for s in range(2):
        out_ref[s] = pieces_ref[0, 0, s, :, :HEAD]
        for a in range(3):
            out_ref[2 + 3 * s + a] = pieces_ref[1, 0, s, :, a * HEAD : (a + 1) * HEAD]


def by_owner(place, pieces, earlier):
    rows = pieces.shape[-2]
    return pl.pallas_call(
        by_owner_kernel,
        out_shape=jax.ShapeDtypeStruct((8, rows, HEAD), BF16),
        grid_spec=pltpu.PrefetchScalarGridSpec(
            num_scalar_prefetch=1,
            grid=(1,),
            in_specs=[
                pl.BlockSpec(
                    (2, 1, 2, rows, UNITS), lambda s, place: (0, place[0] // 4, 0, 0, 0)
                ),
                pl.BlockSpec(memory_space=pl.ANY),
            ],
            out_specs=pl.BlockSpec((8, rows, HEAD), lambda s, place: (0, 0, 0)),
        ),
        compiler_params=params(),
        interpret=INTERPRET,
    )(place, pieces, earlier)


def halves_kernel(side_ref, keep_in, give_in, earlier_ref, keep_ref, give_ref):
    for given, ref in ((keep_in, keep_ref), (give_in, give_ref)):
        ref[...] = given[...].reshape(ref.shape[1], ref.shape[0]).T


def halves(side, gathered, earlier):
    lines, sides, _, rows, dblock = gathered.shape
    half = dblock // 2
    block = (lines, sides, pl.squeezed, rows, half)
    turned = (half, lines * sides * rows)
    shape = jax.ShapeDtypeStruct(turned, BF16)
    return pl.pallas_call(
        halves_kernel,
        out_shape=(shape, shape),
        grid_spec=pltpu.PrefetchScalarGridSpec(
            num_scalar_prefetch=1,
            grid=(1,),
            in_specs=[
                pl.BlockSpec(block, lambda s, side: (0, 0, 0, 0, side[0])),
                pl.BlockSpec(block, lambda s, side: (0, 0, 0, 0, 1 - side[0])),
                pl.BlockSpec(memory_space=pl.ANY),
            ],
            out_specs=[pl.BlockSpec(turned, lambda s, side: (0, 0))] * 2,
        ),
        compiler_params=params(),
        interpret=INTERPRET,
    )(side, gathered, gathered, stay(earlier))


def cotangent_kernel(rows_ref, earlier_ref, out_ref):
    out_ref[...] = rows_ref[...]


def cotangent_rows(rows, earlier):
    part = pl.BlockSpec((2,) + rows.shape[1:], lambda s: (s, 0, 0))
    return pl.pallas_call(
        cotangent_kernel,
        out_shape=pltpu.HBM(rows.shape, BF16),
        grid=(rows.shape[0] // 2,),
        in_specs=[part, pl.BlockSpec(memory_space=pl.ANY)],
        out_specs=part,
        compiler_params=params(),
        interpret=INTERPRET,
    )(rows, stay(earlier))


def grad_out_kernel(hidden_ref, cot_ref, out_ref, flag_ref, sum_ref):
    step = pl.program_id(0)
    total = cot_ref.shape[0] * cot_ref.shape[1] * cot_ref.shape[2]
    hidden = hidden_ref[...].reshape(total, HEAD)
    cot = cot_ref[...].reshape(total, cot_ref.shape[-1])
    terms = lax.dot_general(hidden, cot, (((0,), (0,)), ((), ())), preferred_element_type=F32)

    @pl.when(step == 0)
    def first():
        sum_ref[...] = terms

    @pl.when(step > 0)
    def later():
        sum_ref[...] += terms

    @pl.when(step == pl.num_programs(0) - 1)
    def last():
        out_ref[...] = sum_ref[...].astype(BF16)
        flag_ref[...] = jnp.zeros_like(flag_ref)


def grad_out_rows(hidden, cot):
    lines, groups, rows, dblock = cot.shape
    steps = 2 if lines % 2 == 0 else 1
    return pl.pallas_call(
        grad_out_kernel,
        out_shape=(
            jax.ShapeDtypeStruct((HEAD, dblock), BF16),
            pltpu.HBM((8, HEAD), F32),
        ),
        grid=(steps,),
        in_specs=[
            pl.BlockSpec((lines // steps, groups, rows, HEAD), lambda s: (s, 0, 0, 0)),
            pl.BlockSpec((lines // steps, groups, rows, dblock), lambda s: (s, 0, 0, 0)),
        ],
        out_specs=[
            pl.BlockSpec((HEAD, dblock), lambda s: (0, 0)),
            pl.BlockSpec((8, HEAD), lambda s: (0, 0)),
        ],
        scratch_shapes=[pltpu.VMEM((HEAD, dblock), F32)],
        compiler_params=params(),
        interpret=INTERPRET,
    )(hidden, stay(cot))


def grad_in_kernel(y_own_ref, y_other_ref, heads_ref, units_ref, out_ref):
    for t, ref in enumerate((heads_ref, units_ref)):
        terms = 0.0
        for side, y_ref in enumerate((y_own_ref, y_other_ref)):
            rows = [
                jnp.concatenate([ref[s, i, side] for s in range(2)], axis=1)
                for i in range(IMAGES)
            ]
            d_pre = jnp.concatenate(rows, axis=0)
            terms = terms + jnp.dot(y_ref[...], d_pre, preferred_element_type=F32)
        terms = terms.astype(BF16)
        if t == 0:
            for s in range(2):
                for a in range(3):
                    first, from_ = (2 * a + s) * HEAD, (3 * s + a) * HEAD
                    out_ref[:, first : first + HEAD] = terms[:, from_ : from_ + HEAD]
        else:
            out_ref[:, 2 * UNITS :] = terms


def grad_in_terms(y_own, y_other, heads, units):
    features = y_own.shape[0]
    width = 4 * UNITS
    y = pl.BlockSpec(y_own.shape, lambda s: (0, 0))
    whole = pl.BlockSpec(heads.shape, lambda s: (0, 0, 0, 0, 0))
    return pl.pallas_call(
        grad_in_kernel,
        out_shape=pltpu.HBM((features, width), BF16),
        grid=(1,),
        in_specs=[y, y, whole, whole],
        out_specs=pl.BlockSpec((features, width), lambda s: (0, 0)),
        compiler_params=params(),
        interpret=INTERPRET,
    )(y_own, y_other, heads, units)


def both_kernel(one_ref, other_ref, earlier_ref, out_ref):
    out_ref[0] = one_ref[...]
    out_ref[1] = other_ref[...]


def both(one, other, earlier):
    part = pl.BlockSpec(one.shape, lambda s: (0, 0))
    shape = (2,) + one.shape
    return pl.pallas_call(
        both_kernel,
        out_shape=jax.ShapeDtypeStruct(shape, BF16),
        grid=(1,),
        in_specs=[part, part, pl.BlockSpec(memory_space=pl.ANY)],
        out_specs=pl.BlockSpec(shape, lambda s: (0, 0, 0)),
        compiler_params=params(),
        interpret=INTERPRET,
    )(one, other, earlier)


def sum_kernel(parts_ref, earlier_ref, out_ref):
    summed = parts_ref[0].astype(F32)
    for part in range(1, parts_ref.shape[0]):
        summed = summed + parts_ref[part].astype(F32)
    out_ref[...] = summed.astype(BF16)


def sum_parts(parts, earlier):
    shape = parts.shape[1:]
    return pl.pallas_call(
        sum_kernel,
        out_shape=jax.ShapeDtypeStruct(shape, BF16),
        grid=(1,),
        in_specs=[
            pl.BlockSpec(parts.shape, lambda s: (0, 0, 0)),
            pl.BlockSpec(memory_space=pl.ANY),
        ],
        out_specs=pl.BlockSpec(shape, lambda s: (0, 0)),
        compiler_params=params(),
        interpret=INTERPRET,
    )(parts, stay(earlier))


def swap(values, axis):
    return lax.ppermute(values, axis, [(0, 1), (1, 0)])


def send(values, axis):
    shape = values.shape
    flat = values.reshape((shape[0] * shape[1],) + shape[2:])
    return lax.all_to_all(flat, axis, 0, 0, tiled=True).reshape(shape)


def shards(tokens, w_in, w_out, cotangent):
    parts = lax.axis_size(MY)
    groups = lax.axis_size(DP)
    place = lax.axis_index(MY).astype(jnp.int32).reshape(1)
    side = lax.axis_index("dh").astype(jnp.int32).reshape(1)
    dblock = w_in.shape[0]
    total = IMAGES * PATCHES
    kinds = (2, IMAGES, 2)
    lines = 8
    block = total // lines

    with jax.named_scope("token_rows"):
        mine = norm_rows(place, tokens, cotangent)
        rows = lax.all_gather(mine, "zh", axis=0, tiled=False)
        cot_rows = send(cotangent_copies(rows, groups), DP)
        near = lax.all_gather(rows, "yl", axis=0, tiled=False)
        gathered = lax.all_gather(near, "yh", axis=0, tiled=False)
        gathered = gathered.reshape((-1,) + rows.shape)

    with jax.named_scope("units"):
        partial = products(gathered, w_in, w_out, cot_rows)
        partial = send(partial.reshape(2, -1, 2 * UNITS), "c")
        partial, flag = pair_sum(partial)
        terms = send(partial.reshape(-1, PATCHES, 2 * UNITS), "x")

    with jax.named_scope("y_of_two_groups"):
        y_own, y_give = halves(side, gathered, flag)
        y_other = swap(y_give, "dh")

    with jax.named_scope("cotangent_of_all_groups"):
        cot_rows = cotangent_rows(cot_rows, flag)
        cot_all = lax.all_gather(cot_rows, Y, axis=0, tiled=False)
        held = cot_all.shape[0]
        cot_all = cot_all.reshape(held, groups, lines // held, block, dblock)
        cot_all = cot_all.swapaxes(1, 2).reshape(lines, groups, block, dblock)

    with jax.named_scope("units"):
        hidden, d_pre = unit(place, terms, y_own)

    with jax.named_scope("d_pre_of_two_groups"):
        pieces = both(d_pre, swap(d_pre, "dh"), y_other)
        pieces = lax.all_gather(pieces, "x", axis=0, tiled=False)
        heads = lax.all_gather(pieces[:2], "c", axis=0, tiled=False)
        units = lax.all_gather(pieces[2:], "c", axis=0, tiled=False)
        grad_in = grad_in_terms(y_own, y_other, heads, units)
        grad_in = send(grad_in.reshape(4, dblock // 8, grad_in.shape[1]), "dl")

    with jax.named_scope("hidden_of_all_groups"):
        blocks = send(hidden.reshape(parts, block, UNITS), MY)
        owned = by_owner(place, blocks.reshape(kinds + (block, UNITS)), pieces)
        owned = lax.all_gather(send(owned, DP), MY, axis=0, tiled=False)
        grad_out, done = grad_out_rows(owned, cot_all)

    with jax.named_scope("grad_in_sum"):
        grad_in = sum_parts(grad_in, done)

    return grad_in[None], grad_out[None]


def solution(mesh):
    sizes = dict(mesh.shape)
    lines = sizes["mx"] // 2
    near = 2 if lines % 2 == 0 else 1
    cut = (2, sizes["dp"] // 2, lines // near, near, 2, sizes["my"] // 2, 2)
    fine = Mesh(mesh.devices.reshape(cut), DP + MX + MY)
    return jax.shard_map(
        shards,
        mesh=fine,
        in_specs=(P(DP + MX, None), P(MY, MX), P(MX, MY), P(DP + MX, MY)),
        out_specs=(P(DP, MY, MX), P(DP, MX, MY)),
        check_vma=False,
    )
```

```python
import jax
import jax.numpy as jnp
from jax import lax
from jax.experimental import pallas as pl
from jax.experimental.pallas import tpu as pltpu
from jax.sharding import Mesh
from jax.sharding import PartitionSpec as P

HEAD = 128
HEADS_DEV = 2
PATCHES = 128
IMAGES = 2
UNITS = 384
EPS = 1e-06

INTERPRET = False
VMEM_LIMIT = 48 * 2**20

DP = ("dh", "dl")
MX = ("y", "zh")
MY = ("x", "c")

F32 = jnp.float32
BF16 = jnp.bfloat16


def stay(values):
    return pltpu.with_memory_space_constraint(values, pltpu.HBM)


def params():
    return pltpu.CompilerParams(vmem_limit_bytes=VMEM_LIMIT)


def norm_kernel(place_ref, tokens_ref, mine_ref, cot_ref, out_ref):
    x = tokens_ref[...].astype(F32)
    mean = jnp.mean(x, axis=-1, keepdims=True)
    center = x - mean
    spread = jnp.mean(center * center, axis=-1, keepdims=True)
    mine = (mine_ref[...].astype(F32) - mean) * lax.rsqrt(spread + EPS)
    out_ref[0] = mine.astype(BF16)
    out_ref[1] = cot_ref[...]


def norm_rows(place, tokens, cotangent):
    rows, features = tokens.shape
    dblock = cotangent.shape[1]
    return pl.pallas_call(
        norm_kernel,
        out_shape=jax.ShapeDtypeStruct((2, rows, dblock), BF16),
        grid_spec=pltpu.PrefetchScalarGridSpec(
            num_scalar_prefetch=1,
            grid=(1,),
            in_specs=[
                pl.BlockSpec((rows, features), lambda s, place: (0, 0)),
                pl.BlockSpec((rows, dblock), lambda s, place: (0, place[0])),
                pl.BlockSpec((rows, dblock), lambda s, place: (0, 0)),
            ],
            out_specs=pl.BlockSpec((2, rows, dblock), lambda s, place: (0, 0, 0)),
        ),
        compiler_params=params(),
        interpret=INTERPRET,
    )(place, stay(tokens), stay(tokens), stay(cotangent))


def longer_kernel(rows_ref, out_ref):
    sides, kinds, count, _ = rows_ref.shape
    for third, kind in enumerate((1, 0, 1)):
        for side in range(sides):
            first = (third * sides + side) * count
            out_ref[first : first + count] = rows_ref[side, kind]


def longer_rows(rows):
    sides, _, count, dblock = rows.shape
    shape = (3 * sides * count, dblock)
    return pl.pallas_call(
        longer_kernel,
        out_shape=jax.ShapeDtypeStruct(shape, BF16),
        grid=(1,),
        in_specs=[pl.BlockSpec(rows.shape, lambda s: (0, 0, 0, 0))],
        out_specs=pl.BlockSpec(shape, lambda s: (0, 0)),
        compiler_params=params(),
        interpret=INTERPRET,
    )(rows)


def products_kernel(y_ref, cot_ref, w_ref, va, vb, vc, out_ref, flag_ref):
    total = IMAGES * PATCHES
    dblock = w_ref.shape[0]
    y = y_ref[...].reshape(total, dblock)
    cot = cot_ref[...].reshape(total, dblock)
    pre = jnp.dot(y, w_ref[...], preferred_element_type=F32).astype(BF16)
    flag_ref[...] = jnp.zeros_like(flag_ref)

    def back(v):
        terms = lax.dot_general(cot, v, (((1,), (1,)), ((), ())), preferred_element_type=F32)
        return terms.astype(BF16)

    def put(s, first, values):
        width = values.shape[1]
        out_ref[0, :, s, :, first : first + width] = values.reshape(IMAGES, PATCHES, width)

    @pl.when(pl.program_id(0) == 0)
    def heads():
        grad = back(va[...])
        for s in range(2):
            for a in range(3):
                first = (2 * a + s) * HEAD
                put(s, a * HEAD, pre[:, first : first + HEAD])
            put(s, UNITS, grad[:, s * HEAD : (s + 1) * HEAD])
            put(s, UNITS + HEAD, jnp.zeros((total, 2 * HEAD), BF16))

    @pl.when(pl.program_id(0) == 1)
    def units():
        grad = back(jnp.concatenate([va[...], vb[...], vc[...]], axis=0))
        for s in range(2):
            put(s, 0, pre[:, s * UNITS : (s + 1) * UNITS])
            put(s, UNITS, grad[:, s * UNITS : (s + 1) * UNITS])


def products(gathered, w_in, w_out):
    lines, sides, _, rows, dblock = gathered.shape

    def kind(which):
        return pl.BlockSpec(
            (lines, sides, pl.squeezed, rows, dblock), lambda s: (0, 0, which, 0, 0)
        )

    def v_rows(block):
        return pl.BlockSpec((2 * HEAD, dblock), lambda s: (block(s), 0))

    return pl.pallas_call(
        products_kernel,
        out_shape=(
            pltpu.HBM((2, IMAGES, 2, PATCHES, 2 * UNITS), BF16),
            pltpu.HBM((8, HEAD), F32),
        ),
        grid=(2,),
        in_specs=[
            kind(0),
            kind(1),
            pl.BlockSpec((dblock, 2 * UNITS), lambda s: (0, s)),
            v_rows(lambda s: s),
            v_rows(lambda s: 2),
            v_rows(lambda s: 3),
        ],
        out_specs=[
            pl.BlockSpec((1, IMAGES, 2, PATCHES, 2 * UNITS), lambda s: (s, 0, 0, 0, 0)),
            pl.BlockSpec((8, HEAD), lambda s: (0, 0)),
        ],
        compiler_params=params(),
        interpret=INTERPRET,
    )(gathered, gathered, stay(w_in), *[stay(w_out)] * 3)


def exact(a, b, contract):
    return lax.dot_general(
        a, b, (contract, ((), ())), precision=lax.Precision.HIGHEST, preferred_element_type=F32
    )


def quick(a, b, contract):
    return lax.dot_general(
        a.astype(BF16), b.astype(BF16), (contract, ((), ())), preferred_element_type=F32
    )


def head_norm(values):
    center = values - jnp.mean(values, axis=-1, keepdims=True)
    scale = lax.rsqrt(jnp.mean(center * center, axis=-1, keepdims=True) + EPS)
    return center * scale, scale


def head_norm_pull(normed, scale, grad):
    along = jnp.mean(grad * normed, axis=-1, keepdims=True)
    return scale * (grad - jnp.mean(grad, axis=-1, keepdims=True) - normed * along)


def unit_kernel(place_ref, terms_ref, earlier_ref, hidden_ref, d_pre_ref):
    summed = terms_ref[0].astype(F32)
    for part in range(1, terms_ref.shape[0]):
        summed = summed + terms_ref[part].astype(F32)
    pre = summed[:, :UNITS].astype(BF16).astype(F32)
    grad = summed[:, UNITS:]

    @pl.when(place_ref[0] < 4)
    def attention():
        value = pre[:, 2 * HEAD :]
        d_out = grad[:, :HEAD]
        query, query_scale = head_norm(pre[:, :HEAD])
        key, key_scale = head_norm(pre[:, HEAD : 2 * HEAD])
        weights = jnp.exp(exact(query, key, ((1,), (1,))) * HEAD ** (-0.5))
        weights = weights / jnp.sum(weights, axis=-1, keepdims=True)
        out = quick(weights, value, ((1,), (0,)))
        d_value = quick(weights, d_out, ((0,), (0,)))
        d_weights = quick(d_out, value, ((1,), (1,)))
        along = jnp.sum(d_weights * weights, axis=-1, keepdims=True)
        d_scores = weights * (d_weights - along) * HEAD ** (-0.5)
        d_query = quick(d_scores, key, ((1,), (0,)))
        d_key = quick(d_scores, query, ((0,), (0,)))
        for i in range(IMAGES):
            hidden_ref[i, :, :HEAD] = out.astype(BF16)
            hidden_ref[i, :, HEAD:] = jnp.zeros((PATCHES, 2 * HEAD), BF16)
        d_pre_ref[:, :HEAD] = head_norm_pull(query, query_scale, d_query).astype(BF16)
        d_pre_ref[:, HEAD : 2 * HEAD] = head_norm_pull(key, key_scale, d_key).astype(BF16)
        d_pre_ref[:, 2 * HEAD :] = d_value.astype(BF16)

    @pl.when(place_ref[0] >= 4)
    def units():
        below = 0.5 * (1.0 + lax.erf(pre * 2.0**-0.5))
        density = jnp.exp(-0.5 * pre * pre) * 0.3989422804014327
        for i in range(IMAGES):
            hidden_ref[i] = (pre * below).astype(BF16)
        d_pre_ref[...] = (grad * (below + pre * density)).astype(BF16)


def unit(place, terms, earlier):
    return pl.pallas_call(
        unit_kernel,
        out_shape=(
            jax.ShapeDtypeStruct((IMAGES, PATCHES, UNITS), BF16),
            jax.ShapeDtypeStruct((PATCHES, UNITS), BF16),
        ),
        grid_spec=pltpu.PrefetchScalarGridSpec(
            num_scalar_prefetch=1,
            grid=(1,),
            in_specs=[
                pl.BlockSpec(terms.shape, lambda s, place: (0, 0, 0)),
                pl.BlockSpec(memory_space=pl.ANY),
            ],
            out_specs=[
                pl.BlockSpec((IMAGES, PATCHES, UNITS), lambda s, place: (0, 0, 0)),
                pl.BlockSpec((PATCHES, UNITS), lambda s, place: (0, 0)),
            ],
        ),
        compiler_params=params(),
        interpret=INTERPRET,
    )(place, terms, earlier)


def by_owner_kernel(place_ref, pieces_ref, earlier_ref, out_ref):
    for s in range(2):
        out_ref[s] = pieces_ref[0, 0, s, :, :HEAD]
        for a in range(3):
            out_ref[2 + 3 * s + a] = pieces_ref[1, 0, s, :, a * HEAD : (a + 1) * HEAD]


def by_owner(place, pieces, earlier):
    rows = pieces.shape[-2]
    return pl.pallas_call(
        by_owner_kernel,
        out_shape=jax.ShapeDtypeStruct((8, rows, HEAD), BF16),
        grid_spec=pltpu.PrefetchScalarGridSpec(
            num_scalar_prefetch=1,
            grid=(1,),
            in_specs=[
                pl.BlockSpec(
                    (2, 1, 2, rows, UNITS), lambda s, place: (0, place[0] // 4, 0, 0, 0)
                ),
                pl.BlockSpec(memory_space=pl.ANY),
            ],
            out_specs=pl.BlockSpec((8, rows, HEAD), lambda s, place: (0, 0, 0)),
        ),
        compiler_params=params(),
        interpret=INTERPRET,
    )(place, pieces, earlier)


def halves_kernel(side_ref, keep_in, give_in, earlier_ref, keep_ref, give_ref):
    for given, ref in ((keep_in, keep_ref), (give_in, give_ref)):
        ref[...] = given[...].reshape(ref.shape[1], ref.shape[0]).T


def halves(side, gathered, earlier):
    lines, sides, _, rows, dblock = gathered.shape
    half = dblock // 2
    block = (lines, sides, pl.squeezed, rows, half)
    turned = (half, lines * sides * rows)
    shape = jax.ShapeDtypeStruct(turned, BF16)
    return pl.pallas_call(
        halves_kernel,
        out_shape=(shape, shape),
        grid_spec=pltpu.PrefetchScalarGridSpec(
            num_scalar_prefetch=1,
            grid=(1,),
            in_specs=[
                pl.BlockSpec(block, lambda s, side: (0, 0, 0, 0, side[0])),
                pl.BlockSpec(block, lambda s, side: (0, 0, 0, 0, 1 - side[0])),
                pl.BlockSpec(memory_space=pl.ANY),
            ],
            out_specs=[pl.BlockSpec(turned, lambda s, side: (0, 0))] * 2,
        ),
        compiler_params=params(),
        interpret=INTERPRET,
    )(side, gathered, gathered, stay(earlier))


def cotangent_kernel(rows_ref, *refs):
    refs[-1][...] = rows_ref[...]


def cotangent_rows(gathered, count, earlier):
    groups, _, dblock = gathered.shape
    part = pl.BlockSpec((2, count, dblock), lambda s: (s, 0, 0))
    return pl.pallas_call(
        cotangent_kernel,
        out_shape=pltpu.HBM((groups, count, dblock), BF16),
        grid=(groups // 2,),
        in_specs=[part] + [pl.BlockSpec(memory_space=pl.ANY)] * len(earlier),
        out_specs=part,
        compiler_params=params(),
        interpret=INTERPRET,
    )(stay(gathered), *earlier)


def grad_out_kernel(hidden_ref, cot_ref, out_ref, flag_ref, sum_ref):
    step = pl.program_id(0)
    total = cot_ref.shape[0] * cot_ref.shape[1] * cot_ref.shape[2]
    hidden = hidden_ref[...].reshape(total, HEAD)
    cot = cot_ref[...].reshape(total, cot_ref.shape[-1])
    terms = lax.dot_general(hidden, cot, (((0,), (0,)), ((), ())), preferred_element_type=F32)

    @pl.when(step == 0)
    def first():
        sum_ref[...] = terms

    @pl.when(step > 0)
    def later():
        sum_ref[...] += terms

    @pl.when(step == pl.num_programs(0) - 1)
    def last():
        out_ref[...] = sum_ref[...].astype(BF16)
        flag_ref[...] = jnp.zeros_like(flag_ref)


def grad_out_rows(hidden, cot):
    lines, groups, rows, dblock = cot.shape
    steps = 4
    return pl.pallas_call(
        grad_out_kernel,
        out_shape=(
            jax.ShapeDtypeStruct((HEAD, dblock), BF16),
            pltpu.HBM((8, HEAD), F32),
        ),
        grid=(steps,),
        in_specs=[
            pl.BlockSpec((lines // steps, groups, rows, HEAD), lambda s: (s, 0, 0, 0)),
            pl.BlockSpec((lines // steps, groups, rows, dblock), lambda s: (s, 0, 0, 0)),
        ],
        out_specs=[
            pl.BlockSpec((HEAD, dblock), lambda s: (0, 0)),
            pl.BlockSpec((8, HEAD), lambda s: (0, 0)),
        ],
        scratch_shapes=[pltpu.VMEM((HEAD, dblock), F32)],
        compiler_params=params(),
        interpret=INTERPRET,
    )(hidden, stay(cot))


def grad_in_kernel(y_own_ref, y_other_ref, own_ref, other_ref, out_ref):
    for t in range(2):
        terms = 0.0
        for y_ref, ref in ((y_own_ref, own_ref), (y_other_ref, other_ref)):
            rows = [
                jnp.concatenate([ref[4 * t + 2 * i + s] for s in range(2)], axis=1)
                for i in range(IMAGES)
            ]
            d_pre = jnp.concatenate(rows, axis=0)
            terms = terms + jnp.dot(y_ref[...], d_pre, preferred_element_type=F32)
        terms = terms.astype(BF16)
        if t == 0:
            for s in range(2):
                for a in range(3):
                    first, from_ = (2 * a + s) * HEAD, (3 * s + a) * HEAD
                    out_ref[:, first : first + HEAD] = terms[:, from_ : from_ + HEAD]
        else:
            out_ref[:, 2 * UNITS :] = terms


def grad_in_terms(y_own, y_other, own, other):
    features = y_own.shape[0]
    width = 4 * UNITS
    y = pl.BlockSpec(y_own.shape, lambda s: (0, 0))
    whole = pl.BlockSpec(own.shape, lambda s: (0, 0, 0))
    return pl.pallas_call(
        grad_in_kernel,
        out_shape=pltpu.HBM((features, width), BF16),
        grid=(1,),
        in_specs=[y, y, whole, whole],
        out_specs=pl.BlockSpec((features, width), lambda s: (0, 0)),
        compiler_params=params(),
        interpret=INTERPRET,
    )(y_own, y_other, own, other)


def sum_kernel(parts_ref, earlier_ref, out_ref):
    summed = parts_ref[0].astype(F32)
    for part in range(1, parts_ref.shape[0]):
        summed = summed + parts_ref[part].astype(F32)
    out_ref[...] = summed.astype(BF16)


def sum_parts(parts, earlier):
    shape = parts.shape[1:]
    return pl.pallas_call(
        sum_kernel,
        out_shape=jax.ShapeDtypeStruct(shape, BF16),
        grid=(1,),
        in_specs=[
            pl.BlockSpec(parts.shape, lambda s: (0, 0, 0)),
            pl.BlockSpec(memory_space=pl.ANY),
        ],
        out_specs=pl.BlockSpec(shape, lambda s: (0, 0)),
        compiler_params=params(),
        interpret=INTERPRET,
    )(parts, stay(earlier))


def swap(values, axis):
    return lax.ppermute(values, axis, [(0, 1), (1, 0)])


def send(values, axis):
    shape = values.shape
    flat = values.reshape((shape[0] * shape[1],) + shape[2:])
    return lax.all_to_all(flat, axis, 0, 0, tiled=True).reshape(shape)


def shards(tokens, w_in, w_out, cotangent):
    parts = lax.axis_size(MY)
    groups = lax.axis_size(DP)
    place = lax.axis_index(MY).astype(jnp.int32).reshape(1)
    side = lax.axis_index("dh").astype(jnp.int32).reshape(1)
    dblock = w_in.shape[0]
    total = IMAGES * PATCHES
    kinds = (2, IMAGES, 2)
    lines = 8
    block = total // lines

    with jax.named_scope("token_rows"):
        mine = norm_rows(place, tokens, cotangent)
        rows = lax.all_gather(mine, "zh", axis=0, tiled=False)
        longer = longer_rows(rows)
        gathered = lax.all_gather(rows, "y", axis=0, tiled=False)

    with jax.named_scope("units"):
        partial, flag = products(gathered, w_in, w_out)
        terms = send(partial.reshape(parts, PATCHES, 2 * UNITS), MY)

    with jax.named_scope("y_of_two_groups"):
        y_own, y_give = halves(side, gathered, flag)
        y_other = swap(y_give, "dh")

    with jax.named_scope("units"):
        hidden, d_pre = unit(place, terms, y_own)

    with jax.named_scope("d_pre_of_two_groups"):
        d_pre_other = swap(d_pre, "dh")
        own = lax.all_gather(d_pre, MY, axis=0, tiled=False)
        other = lax.all_gather(d_pre_other, MY, axis=0, tiled=False)
        grad_in = grad_in_terms(y_own, y_other, own, other)
        grad_in = send(grad_in.reshape(4, dblock // 8, grad_in.shape[1]), "dl")

    with jax.named_scope("hidden_of_all_groups"):
        pieces = send(hidden.reshape(parts, block, UNITS), MY)
        owned = by_owner(place, pieces.reshape(kinds + (block, UNITS)), own)

    with jax.named_scope("cotangent_of_all_groups"):
        count = rows.shape[0] * rows.shape[2]
        cot_rows = lax.all_gather(longer, DP, axis=0, tiled=False)
        cot_rows = cotangent_rows(cot_rows, count, (owned, d_pre_other, y_other))
        cot_all = lax.all_gather(cot_rows, "y", axis=0, tiled=False)
        held = cot_all.shape[0]
        cot_all = cot_all.reshape(held, groups, lines // held, block, dblock)
        cot_all = cot_all.swapaxes(1, 2).reshape(lines, groups, block, dblock)

    with jax.named_scope("hidden_of_all_groups"):
        owned = lax.all_gather(send(owned, DP), MY, axis=0, tiled=False)
        grad_out, done = grad_out_rows(owned, cot_all)

    with jax.named_scope("grad_in_sum"):
        grad_in = sum_parts(grad_in, done)

    return grad_in[None], grad_out[None]


def solution(mesh):
    sizes = dict(mesh.shape)
    lines = sizes["mx"] // 2
    cut = (2, sizes["dp"] // 2, lines, 2, sizes["my"] // 2, 2)
    fine = Mesh(mesh.devices.reshape(cut), DP + MX + MY)
    return jax.shard_map(
        shards,
        mesh=fine,
        in_specs=(P(DP + MX, None), P(MY, MX), P(MX, MY), P(DP + MX, MY)),
        out_specs=(P(DP, MY, MX), P(DP, MX, MY)),
        check_vma=False,
    )
```

```python
import jax
import jax.numpy as jnp
from jax import lax
from jax.experimental import pallas as pl
from jax.experimental.pallas import tpu as pltpu
from jax.sharding import Mesh
from jax.sharding import PartitionSpec as P

HEAD = 128
HEADS_DEV = 2
PATCHES = 128
IMAGES = 2
UNITS = 384
EPS = 1e-06

INTERPRET = False
VMEM_LIMIT = 48 * 2**20

DP = ("dh", "dl")
MX = ("y", "zh")
MY = ("x", "c")

F32 = jnp.float32
BF16 = jnp.bfloat16


def stay(values):
    return pltpu.with_memory_space_constraint(values, pltpu.HBM)


def params():
    return pltpu.CompilerParams(vmem_limit_bytes=VMEM_LIMIT)


def norm_kernel(place_ref, tokens_ref, mine_ref, cot_ref, out_ref):
    x = tokens_ref[...].astype(F32)
    mean = jnp.mean(x, axis=-1, keepdims=True)
    center = x - mean
    spread = jnp.mean(center * center, axis=-1, keepdims=True)
    mine = (mine_ref[...].astype(F32) - mean) * lax.rsqrt(spread + EPS)
    out_ref[0] = mine.astype(BF16)
    out_ref[1] = cot_ref[...]


def norm_rows(place, tokens, cotangent):
    rows, features = tokens.shape
    dblock = cotangent.shape[1]
    return pl.pallas_call(
        norm_kernel,
        out_shape=jax.ShapeDtypeStruct((2, rows, dblock), BF16),
        grid_spec=pltpu.PrefetchScalarGridSpec(
            num_scalar_prefetch=1,
            grid=(1,),
            in_specs=[
                pl.BlockSpec((rows, features), lambda s, place: (0, 0)),
                pl.BlockSpec((rows, dblock), lambda s, place: (0, place[0])),
                pl.BlockSpec((rows, dblock), lambda s, place: (0, 0)),
            ],
            out_specs=pl.BlockSpec((2, rows, dblock), lambda s, place: (0, 0, 0)),
        ),
        compiler_params=params(),
        interpret=INTERPRET,
    )(place, stay(tokens), stay(tokens), stay(cotangent))


def copies_kernel(rows_ref, out_ref):
    sides, _, count, dblock = rows_ref.shape
    rows = rows_ref[:, 1].reshape(sides * count, dblock)
    for group in range(out_ref.shape[0]):
        out_ref[group] = rows


def cotangent_copies(rows, groups):
    sides, _, count, dblock = rows.shape
    shape = (groups, sides * count, dblock)
    return pl.pallas_call(
        copies_kernel,
        out_shape=pltpu.HBM(shape, BF16),
        grid=(1,),
        in_specs=[pl.BlockSpec(rows.shape, lambda s: (0, 0, 0, 0))],
        out_specs=pl.BlockSpec(shape, lambda s: (0, 0, 0)),
        compiler_params=params(),
        interpret=INTERPRET,
    )(rows)


def products_kernel(y_ref, cot_ref, w_ref, va, vb, vc, earlier_ref, out_ref, flag_ref):
    total = IMAGES * PATCHES
    dblock = w_ref.shape[0]
    y = y_ref[...].reshape(total, dblock)
    cot = cot_ref[...].reshape(total, dblock)
    pre = jnp.dot(y, w_ref[...], preferred_element_type=F32).astype(BF16)
    flag_ref[...] = jnp.zeros_like(flag_ref)

    def back(v):
        terms = lax.dot_general(cot, v, (((1,), (1,)), ((), ())), preferred_element_type=F32)
        return terms.astype(BF16)

    def put(s, first, values):
        width = values.shape[1]
        out_ref[0, :, s, :, first : first + width] = values.reshape(IMAGES, PATCHES, width)

    @pl.when(pl.program_id(0) == 0)
    def heads():
        grad = back(va[...])
        for s in range(2):
            for a in range(3):
                first = (2 * a + s) * HEAD
                put(s, a * HEAD, pre[:, first : first + HEAD])
            put(s, UNITS, grad[:, s * HEAD : (s + 1) * HEAD])
            put(s, UNITS + HEAD, jnp.zeros((total, 2 * HEAD), BF16))

    @pl.when(pl.program_id(0) == 1)
    def units():
        grad = back(jnp.concatenate([va[...], vb[...], vc[...]], axis=0))
        for s in range(2):
            put(s, 0, pre[:, s * UNITS : (s + 1) * UNITS])
            put(s, UNITS, grad[:, s * UNITS : (s + 1) * UNITS])


def products(gathered, w_in, w_out, earlier):
    lines, sides, _, rows, dblock = gathered.shape

    def kind(which):
        return pl.BlockSpec(
            (lines, sides, pl.squeezed, rows, dblock), lambda s: (0, 0, which, 0, 0)
        )

    def v_rows(block):
        return pl.BlockSpec((2 * HEAD, dblock), lambda s: (block(s), 0))

    return pl.pallas_call(
        products_kernel,
        out_shape=(
            pltpu.HBM((2, IMAGES, 2, PATCHES, 2 * UNITS), BF16),
            pltpu.HBM((8, HEAD), F32),
        ),
        grid=(2,),
        in_specs=[
            kind(0),
            kind(1),
            pl.BlockSpec((dblock, 2 * UNITS), lambda s: (0, s)),
            v_rows(lambda s: s),
            v_rows(lambda s: 2),
            v_rows(lambda s: 3),
            pl.BlockSpec(memory_space=pl.ANY),
        ],
        out_specs=[
            pl.BlockSpec((1, IMAGES, 2, PATCHES, 2 * UNITS), lambda s: (s, 0, 0, 0, 0)),
            pl.BlockSpec((8, HEAD), lambda s: (0, 0)),
        ],
        compiler_params=params(),
        interpret=INTERPRET,
    )(gathered, gathered, stay(w_in), *[stay(w_out)] * 3, earlier)


def exact(a, b, contract):
    return lax.dot_general(
        a, b, (contract, ((), ())), precision=lax.Precision.HIGHEST, preferred_element_type=F32
    )


def head_norm(values):
    center = values - jnp.mean(values, axis=-1, keepdims=True)
    scale = lax.rsqrt(jnp.mean(center * center, axis=-1, keepdims=True) + EPS)
    return center * scale, scale


def head_norm_pull(normed, scale, grad):
    along = jnp.mean(grad * normed, axis=-1, keepdims=True)
    return scale * (grad - jnp.mean(grad, axis=-1, keepdims=True) - normed * along)


def unit_kernel(place_ref, terms_ref, earlier_ref, hidden_ref, d_pre_ref):
    summed = terms_ref[0].astype(F32)
    for part in range(1, terms_ref.shape[0]):
        summed = summed + terms_ref[part].astype(F32)
    pre = summed[:, :UNITS].astype(BF16).astype(F32)
    grad = summed[:, UNITS:]

    @pl.when(place_ref[0] < 4)
    def attention():
        value = pre[:, 2 * HEAD :]
        d_out = grad[:, :HEAD]
        query, query_scale = head_norm(pre[:, :HEAD])
        key, key_scale = head_norm(pre[:, HEAD : 2 * HEAD])
        weights = jnp.exp(exact(query, key, ((1,), (1,))) * HEAD ** (-0.5))
        weights = weights / jnp.sum(weights, axis=-1, keepdims=True)
        out = exact(weights, value, ((1,), (0,)))
        d_value = exact(weights, d_out, ((0,), (0,)))
        d_weights = exact(d_out, value, ((1,), (1,)))
        along = jnp.sum(d_weights * weights, axis=-1, keepdims=True)
        d_scores = weights * (d_weights - along) * HEAD ** (-0.5)
        d_query = exact(d_scores, key, ((1,), (0,)))
        d_key = exact(d_scores, query, ((0,), (0,)))
        for i in range(IMAGES):
            hidden_ref[i, :, :HEAD] = out.astype(BF16)
            hidden_ref[i, :, HEAD:] = jnp.zeros((PATCHES, 2 * HEAD), BF16)
        d_pre_ref[:, :HEAD] = head_norm_pull(query, query_scale, d_query).astype(BF16)
        d_pre_ref[:, HEAD : 2 * HEAD] = head_norm_pull(key, key_scale, d_key).astype(BF16)
        d_pre_ref[:, 2 * HEAD :] = d_value.astype(BF16)

    @pl.when(place_ref[0] >= 4)
    def units():
        below = 0.5 * (1.0 + lax.erf(pre * 2.0**-0.5))
        density = jnp.exp(-0.5 * pre * pre) * 0.3989422804014327
        for i in range(IMAGES):
            hidden_ref[i] = (pre * below).astype(BF16)
        d_pre_ref[...] = (grad * (below + pre * density)).astype(BF16)


def unit(place, terms, earlier):
    return pl.pallas_call(
        unit_kernel,
        out_shape=(
            jax.ShapeDtypeStruct((IMAGES, PATCHES, UNITS), BF16),
            jax.ShapeDtypeStruct((PATCHES, UNITS), BF16),
        ),
        grid_spec=pltpu.PrefetchScalarGridSpec(
            num_scalar_prefetch=1,
            grid=(1,),
            in_specs=[
                pl.BlockSpec(terms.shape, lambda s, place: (0, 0, 0)),
                pl.BlockSpec(memory_space=pl.ANY),
            ],
            out_specs=[
                pl.BlockSpec((IMAGES, PATCHES, UNITS), lambda s, place: (0, 0, 0)),
                pl.BlockSpec((PATCHES, UNITS), lambda s, place: (0, 0)),
            ],
        ),
        compiler_params=params(),
        interpret=INTERPRET,
    )(place, terms, earlier)


def by_owner_kernel(place_ref, pieces_ref, *refs):
    out_ref = refs[-1]
    for s in range(2):
        out_ref[s] = pieces_ref[0, 0, s, :, :HEAD]
        for a in range(3):
            out_ref[2 + 3 * s + a] = pieces_ref[1, 0, s, :, a * HEAD : (a + 1) * HEAD]


def by_owner(place, pieces, earlier):
    rows = pieces.shape[-2]
    return pl.pallas_call(
        by_owner_kernel,
        out_shape=jax.ShapeDtypeStruct((8, rows, HEAD), BF16),
        grid_spec=pltpu.PrefetchScalarGridSpec(
            num_scalar_prefetch=1,
            grid=(1,),
            in_specs=[
                pl.BlockSpec(
                    (2, 1, 2, rows, UNITS), lambda s, place: (0, place[0] // 4, 0, 0, 0)
                ),
            ]
            + [pl.BlockSpec(memory_space=pl.ANY)] * len(earlier),
            out_specs=pl.BlockSpec((8, rows, HEAD), lambda s, place: (0, 0, 0)),
        ),
        compiler_params=params(),
        interpret=INTERPRET,
    )(place, pieces, *earlier)


def halves_kernel(side_ref, keep_in, give_in, earlier_ref, keep_ref, give_ref):
    for given, ref in ((keep_in, keep_ref), (give_in, give_ref)):
        ref[...] = given[...].reshape(ref.shape[1], ref.shape[0]).T


def halves(side, gathered, earlier):
    lines, sides, _, rows, dblock = gathered.shape
    half = dblock // 2
    block = (lines, sides, pl.squeezed, rows, half)
    turned = (half, lines * sides * rows)
    shape = jax.ShapeDtypeStruct(turned, BF16)
    return pl.pallas_call(
        halves_kernel,
        out_shape=(shape, shape),
        grid_spec=pltpu.PrefetchScalarGridSpec(
            num_scalar_prefetch=1,
            grid=(1,),
            in_specs=[
                pl.BlockSpec(block, lambda s, side: (0, 0, 0, 0, side[0])),
                pl.BlockSpec(block, lambda s, side: (0, 0, 0, 0, 1 - side[0])),
                pl.BlockSpec(memory_space=pl.ANY),
            ],
            out_specs=[pl.BlockSpec(turned, lambda s, side: (0, 0))] * 2,
        ),
        compiler_params=params(),
        interpret=INTERPRET,
    )(side, gathered, gathered, stay(earlier))


def cotangent_kernel(rows_ref, earlier_ref, out_ref):
    out_ref[...] = rows_ref[...]


def cotangent_rows(rows, earlier):
    part = pl.BlockSpec(rows.shape, lambda s: (0, 0, 0))
    return pl.pallas_call(
        cotangent_kernel,
        out_shape=pltpu.HBM(rows.shape, BF16),
        grid=(1,),
        in_specs=[part, pl.BlockSpec(memory_space=pl.ANY)],
        out_specs=part,
        compiler_params=params(),
        interpret=INTERPRET,
    )(rows, stay(earlier))


def grad_out_kernel(hidden_ref, cot_ref, out_ref, flag_ref, sum_ref):
    step = pl.program_id(0)
    total = cot_ref.shape[0] * cot_ref.shape[1] * cot_ref.shape[2]
    hidden = hidden_ref[...].reshape(total, HEAD)
    cot = cot_ref[...].reshape(total, cot_ref.shape[-1])
    terms = lax.dot_general(hidden, cot, (((0,), (0,)), ((), ())), preferred_element_type=F32)

    @pl.when(step == 0)
    def first():
        sum_ref[...] = terms

    @pl.when(step > 0)
    def later():
        sum_ref[...] += terms

    @pl.when(step == pl.num_programs(0) - 1)
    def last():
        out_ref[...] = sum_ref[...].astype(BF16)
        flag_ref[...] = jnp.zeros_like(flag_ref)


def grad_out_rows(hidden, cot):
    lines, groups, rows, dblock = cot.shape
    steps = 2 if lines % 2 == 0 else 1
    return pl.pallas_call(
        grad_out_kernel,
        out_shape=(
            jax.ShapeDtypeStruct((HEAD, dblock), BF16),
            pltpu.HBM((8, HEAD), F32),
        ),
        grid=(steps,),
        in_specs=[
            pl.BlockSpec((lines // steps, groups, rows, HEAD), lambda s: (s, 0, 0, 0)),
            pl.BlockSpec((lines // steps, groups, rows, dblock), lambda s: (s, 0, 0, 0)),
        ],
        out_specs=[
            pl.BlockSpec((HEAD, dblock), lambda s: (0, 0)),
            pl.BlockSpec((8, HEAD), lambda s: (0, 0)),
        ],
        scratch_shapes=[pltpu.VMEM((HEAD, dblock), F32)],
        compiler_params=params(),
        interpret=INTERPRET,
    )(hidden, stay(cot))


def grad_in_kernel(y_own_ref, y_other_ref, own_ref, other_ref, out_ref):
    for t in range(2):
        terms = 0.0
        for y_ref, ref in ((y_own_ref, own_ref), (y_other_ref, other_ref)):
            rows = [
                jnp.concatenate([ref[4 * t + 2 * i + s] for s in range(2)], axis=1)
                for i in range(IMAGES)
            ]
            d_pre = jnp.concatenate(rows, axis=0)
            terms = terms + jnp.dot(y_ref[...], d_pre, preferred_element_type=F32)
        terms = terms.astype(BF16)
        if t == 0:
            for s in range(2):
                for a in range(3):
                    first, from_ = (2 * a + s) * HEAD, (3 * s + a) * HEAD
                    out_ref[:, first : first + HEAD] = terms[:, from_ : from_ + HEAD]
        else:
            out_ref[:, 2 * UNITS :] = terms


def grad_in_terms(y_own, y_other, own, other):
    features = y_own.shape[0]
    width = 4 * UNITS
    y = pl.BlockSpec(y_own.shape, lambda s: (0, 0))
    whole = pl.BlockSpec(own.shape, lambda s: (0, 0, 0))
    return pl.pallas_call(
        grad_in_kernel,
        out_shape=pltpu.HBM((features, width), BF16),
        grid=(1,),
        in_specs=[y, y, whole, whole],
        out_specs=pl.BlockSpec((features, width), lambda s: (0, 0)),
        compiler_params=params(),
        interpret=INTERPRET,
    )(y_own, y_other, own, other)


def sum_kernel(parts_ref, earlier_ref, out_ref):
    summed = parts_ref[0].astype(F32)
    for part in range(1, parts_ref.shape[0]):
        summed = summed + parts_ref[part].astype(F32)
    out_ref[...] = summed.astype(BF16)


def sum_parts(parts, earlier):
    shape = parts.shape[1:]
    return pl.pallas_call(
        sum_kernel,
        out_shape=jax.ShapeDtypeStruct(shape, BF16),
        grid=(1,),
        in_specs=[
            pl.BlockSpec(parts.shape, lambda s: (0, 0, 0)),
            pl.BlockSpec(memory_space=pl.ANY),
        ],
        out_specs=pl.BlockSpec(shape, lambda s: (0, 0)),
        compiler_params=params(),
        interpret=INTERPRET,
    )(parts, stay(earlier))


def swap(values, axis):
    return lax.ppermute(values, axis, [(0, 1), (1, 0)])


def send(values, axis):
    shape = values.shape
    flat = values.reshape((shape[0] * shape[1],) + shape[2:])
    return lax.all_to_all(flat, axis, 0, 0, tiled=True).reshape(shape)


def shards(tokens, w_in, w_out, cotangent):
    parts = lax.axis_size(MY)
    groups = lax.axis_size(DP)
    place = lax.axis_index(MY).astype(jnp.int32).reshape(1)
    side = lax.axis_index("dh").astype(jnp.int32).reshape(1)
    dblock = w_in.shape[0]
    total = IMAGES * PATCHES
    kinds = (2, IMAGES, 2)
    lines = 8
    block = total // lines

    with jax.named_scope("token_rows"):
        mine = norm_rows(place, tokens, cotangent)
        rows = lax.all_gather(mine, "zh", axis=0, tiled=False)
        cot_rows = send(cotangent_copies(rows, groups), DP)
        gathered = lax.all_gather(rows, "y", axis=0, tiled=False)

    with jax.named_scope("units"):
        partial, flag = products(gathered, w_in, w_out, cot_rows)
        terms = send(partial.reshape(parts, PATCHES, 2 * UNITS), MY)

    with jax.named_scope("cotangent_of_all_groups"):
        cot_rows = cotangent_rows(cot_rows, flag)
        cot_all = lax.all_gather(cot_rows, "y", axis=0, tiled=False)
        held = cot_all.shape[0]
        cot_all = cot_all.reshape(held, groups, lines // held, block, dblock)
        cot_all = cot_all.swapaxes(1, 2).reshape(lines, groups, block, dblock)

    with jax.named_scope("y_of_two_groups"):
        y_own, y_give = halves(side, gathered, flag)
        y_other = swap(y_give, "dh")

    with jax.named_scope("units"):
        hidden, d_pre = unit(place, terms, y_own)

    with jax.named_scope("d_pre_of_two_groups"):
        d_pre_other = swap(d_pre, "dh")
        own = lax.all_gather(d_pre, MY, axis=0, tiled=False)
        other = lax.all_gather(d_pre_other, MY, axis=0, tiled=False)
        grad_in = grad_in_terms(y_own, y_other, own, other)
        grad_in = send(grad_in.reshape(4, dblock // 8, grad_in.shape[1]), "dl")

    with jax.named_scope("hidden_of_all_groups"):
        blocks = send(hidden.reshape(parts, block, UNITS), MY)
        blocks = blocks.reshape(kinds + (block, UNITS))
        owned = by_owner(place, blocks, (own, d_pre_other, y_other))
        owned = lax.all_gather(send(owned, DP), MY, axis=0, tiled=False)
        grad_out, done = grad_out_rows(owned, cot_all)

    with jax.named_scope("grad_in_sum"):
        grad_in = sum_parts(grad_in, done)

    return grad_in[None], grad_out[None]


def solution(mesh):
    sizes = dict(mesh.shape)
    lines = sizes["mx"] // 2
    cut = (2, sizes["dp"] // 2, lines, 2, sizes["my"] // 2, 2)
    fine = Mesh(mesh.devices.reshape(cut), DP + MX + MY)
    return jax.shard_map(
        shards,
        mesh=fine,
        in_specs=(P(DP + MX, None), P(MY, MX), P(MX, MY), P(DP + MX, MY)),
        out_specs=(P(DP, MY, MX), P(DP, MX, MY)),
        check_vma=False,
    )
```

```python
import jax
import jax.numpy as jnp
from jax import lax
from jax.experimental import pallas as pl
from jax.experimental.pallas import tpu as pltpu
from jax.sharding import Mesh
from jax.sharding import PartitionSpec as P

HEAD = 128
HEADS_DEV = 2
PATCHES = 128
IMAGES = 2
UNITS = 384
EPS = 1e-06

INTERPRET = False
VMEM_LIMIT = 48 * 2**20

DP = ("dh", "dl")
MX = ("y", "zh")
MY = ("x", "c")

F32 = jnp.float32
BF16 = jnp.bfloat16


def stay(values):
    return pltpu.with_memory_space_constraint(values, pltpu.HBM)


def params():
    return pltpu.CompilerParams(vmem_limit_bytes=VMEM_LIMIT)


def norm_kernel(place_ref, tokens_ref, mine_ref, cot_ref, out_ref):
    x = tokens_ref[...].astype(F32)
    mean = jnp.mean(x, axis=-1, keepdims=True)
    center = x - mean
    spread = jnp.mean(center * center, axis=-1, keepdims=True)
    mine = (mine_ref[...].astype(F32) - mean) * lax.rsqrt(spread + EPS)
    out_ref[0] = mine.astype(BF16)
    out_ref[1] = cot_ref[...]


def norm_rows(place, tokens, cotangent):
    rows, features = tokens.shape
    dblock = cotangent.shape[1]
    return pl.pallas_call(
        norm_kernel,
        out_shape=jax.ShapeDtypeStruct((2, rows, dblock), BF16),
        grid_spec=pltpu.PrefetchScalarGridSpec(
            num_scalar_prefetch=1,
            grid=(1,),
            in_specs=[
                pl.BlockSpec((rows, features), lambda s, place: (0, 0)),
                pl.BlockSpec((rows, dblock), lambda s, place: (0, place[0])),
                pl.BlockSpec((rows, dblock), lambda s, place: (0, 0)),
            ],
            out_specs=pl.BlockSpec((2, rows, dblock), lambda s, place: (0, 0, 0)),
        ),
        compiler_params=params(),
        interpret=INTERPRET,
    )(place, stay(tokens), stay(tokens), stay(cotangent))


def longer_kernel(rows_ref, out_ref):
    sides, kinds, count, _ = rows_ref.shape
    for third, kind in enumerate((1, 0, 1)):
        for side in range(sides):
            first = (third * sides + side) * count
            out_ref[first : first + count] = rows_ref[side, kind]


def longer_rows(rows):
    sides, _, count, dblock = rows.shape
    shape = (3 * sides * count, dblock)
    return pl.pallas_call(
        longer_kernel,
        out_shape=jax.ShapeDtypeStruct(shape, BF16),
        grid=(1,),
        in_specs=[pl.BlockSpec(rows.shape, lambda s: (0, 0, 0, 0))],
        out_specs=pl.BlockSpec(shape, lambda s: (0, 0)),
        compiler_params=params(),
        interpret=INTERPRET,
    )(rows)


def products_kernel(y_ref, cot_ref, w_ref, va, vb, vc, out_ref, flag_ref):
    total = IMAGES * PATCHES
    dblock = w_ref.shape[0]
    y = y_ref[...].reshape(total, dblock)
    cot = cot_ref[...].reshape(total, dblock)
    pre = jnp.dot(y, w_ref[...], preferred_element_type=F32).astype(BF16)
    flag_ref[...] = jnp.zeros_like(flag_ref)

    def back(v):
        terms = lax.dot_general(cot, v, (((1,), (1,)), ((), ())), preferred_element_type=F32)
        return terms.astype(BF16)

    def put(s, first, values):
        width = values.shape[1]
        out_ref[0, :, s, :, first : first + width] = values.reshape(IMAGES, PATCHES, width)

    @pl.when(pl.program_id(0) == 0)
    def heads():
        grad = back(va[...])
        for s in range(2):
            for a in range(3):
                first = (2 * a + s) * HEAD
                put(s, a * HEAD, pre[:, first : first + HEAD])
            put(s, UNITS, grad[:, s * HEAD : (s + 1) * HEAD])
            put(s, UNITS + HEAD, jnp.zeros((total, 2 * HEAD), BF16))

    @pl.when(pl.program_id(0) == 1)
    def units():
        grad = back(jnp.concatenate([va[...], vb[...], vc[...]], axis=0))
        for s in range(2):
            put(s, 0, pre[:, s * UNITS : (s + 1) * UNITS])
            put(s, UNITS, grad[:, s * UNITS : (s + 1) * UNITS])


def products(gathered, w_in, w_out):
    lines, sides, _, rows, dblock = gathered.shape

    def kind(which):
        return pl.BlockSpec(
            (lines, sides, pl.squeezed, rows, dblock), lambda s: (0, 0, which, 0, 0)
        )

    def v_rows(block):
        return pl.BlockSpec((2 * HEAD, dblock), lambda s: (block(s), 0))

    return pl.pallas_call(
        products_kernel,
        out_shape=(
            pltpu.HBM((2, IMAGES, 2, PATCHES, 2 * UNITS), BF16),
            pltpu.HBM((8, HEAD), F32),
        ),
        grid=(2,),
        in_specs=[
            kind(0),
            kind(1),
            pl.BlockSpec((dblock, 2 * UNITS), lambda s: (0, s)),
            v_rows(lambda s: s),
            v_rows(lambda s: 2),
            v_rows(lambda s: 3),
        ],
        out_specs=[
            pl.BlockSpec((1, IMAGES, 2, PATCHES, 2 * UNITS), lambda s: (s, 0, 0, 0, 0)),
            pl.BlockSpec((8, HEAD), lambda s: (0, 0)),
        ],
        compiler_params=params(),
        interpret=INTERPRET,
    )(gathered, gathered, stay(w_in), *[stay(w_out)] * 3)


def exact(a, b, contract):
    return lax.dot_general(
        a, b, (contract, ((), ())), precision=lax.Precision.HIGHEST, preferred_element_type=F32
    )


def head_norm(values):
    center = values - jnp.mean(values, axis=-1, keepdims=True)
    scale = lax.rsqrt(jnp.mean(center * center, axis=-1, keepdims=True) + EPS)
    return center * scale, scale


def head_norm_pull(normed, scale, grad):
    along = jnp.mean(grad * normed, axis=-1, keepdims=True)
    return scale * (grad - jnp.mean(grad, axis=-1, keepdims=True) - normed * along)


def unit_kernel(place_ref, terms_ref, earlier_ref, hidden_ref, d_pre_ref):
    summed = terms_ref[0].astype(F32)
    for part in range(1, terms_ref.shape[0]):
        summed = summed + terms_ref[part].astype(F32)
    pre = summed[:, :UNITS].astype(BF16).astype(F32)
    grad = summed[:, UNITS:]

    @pl.when(place_ref[0] < 4)
    def attention():
        value = pre[:, 2 * HEAD :]
        d_out = grad[:, :HEAD]
        query, query_scale = head_norm(pre[:, :HEAD])
        key, key_scale = head_norm(pre[:, HEAD : 2 * HEAD])
        weights = jnp.exp(exact(query, key, ((1,), (1,))) * HEAD ** (-0.5))
        weights = weights / jnp.sum(weights, axis=-1, keepdims=True)
        out = exact(weights, value, ((1,), (0,)))
        d_value = exact(weights, d_out, ((0,), (0,)))
        d_weights = exact(d_out, value, ((1,), (1,)))
        along = jnp.sum(d_weights * weights, axis=-1, keepdims=True)
        d_scores = weights * (d_weights - along) * HEAD ** (-0.5)
        d_query = exact(d_scores, key, ((1,), (0,)))
        d_key = exact(d_scores, query, ((0,), (0,)))
        for i in range(IMAGES):
            hidden_ref[i, :, :HEAD] = out.astype(BF16)
            hidden_ref[i, :, HEAD:] = jnp.zeros((PATCHES, 2 * HEAD), BF16)
        d_pre_ref[:, :HEAD] = head_norm_pull(query, query_scale, d_query).astype(BF16)
        d_pre_ref[:, HEAD : 2 * HEAD] = head_norm_pull(key, key_scale, d_key).astype(BF16)
        d_pre_ref[:, 2 * HEAD :] = d_value.astype(BF16)

    @pl.when(place_ref[0] >= 4)
    def units():
        below = 0.5 * (1.0 + lax.erf(pre * 2.0**-0.5))
        density = jnp.exp(-0.5 * pre * pre) * 0.3989422804014327
        for i in range(IMAGES):
            hidden_ref[i] = (pre * below).astype(BF16)
        d_pre_ref[...] = (grad * (below + pre * density)).astype(BF16)


def unit(place, terms, earlier):
    return pl.pallas_call(
        unit_kernel,
        out_shape=(
            jax.ShapeDtypeStruct((IMAGES, PATCHES, UNITS), BF16),
            jax.ShapeDtypeStruct((PATCHES, UNITS), BF16),
        ),
        grid_spec=pltpu.PrefetchScalarGridSpec(
            num_scalar_prefetch=1,
            grid=(1,),
            in_specs=[
                pl.BlockSpec(terms.shape, lambda s, place: (0, 0, 0)),
                pl.BlockSpec(memory_space=pl.ANY),
            ],
            out_specs=[
                pl.BlockSpec((IMAGES, PATCHES, UNITS), lambda s, place: (0, 0, 0)),
                pl.BlockSpec((PATCHES, UNITS), lambda s, place: (0, 0)),
            ],
        ),
        compiler_params=params(),
        interpret=INTERPRET,
    )(place, terms, earlier)


def by_owner_kernel(place_ref, pieces_ref, earlier_ref, out_ref):
    for s in range(2):
        out_ref[s] = pieces_ref[0, 0, s, :, :HEAD]
        for a in range(3):
            out_ref[2 + 3 * s + a] = pieces_ref[1, 0, s, :, a * HEAD : (a + 1) * HEAD]


def by_owner(place, pieces, earlier):
    rows = pieces.shape[-2]
    return pl.pallas_call(
        by_owner_kernel,
        out_shape=jax.ShapeDtypeStruct((8, rows, HEAD), BF16),
        grid_spec=pltpu.PrefetchScalarGridSpec(
            num_scalar_prefetch=1,
            grid=(1,),
            in_specs=[
                pl.BlockSpec(
                    (2, 1, 2, rows, UNITS), lambda s, place: (0, place[0] // 4, 0, 0, 0)
                ),
                pl.BlockSpec(memory_space=pl.ANY),
            ],
            out_specs=pl.BlockSpec((8, rows, HEAD), lambda s, place: (0, 0, 0)),
        ),
        compiler_params=params(),
        interpret=INTERPRET,
    )(place, pieces, earlier)


def halves_kernel(side_ref, keep_in, give_in, earlier_ref, keep_ref, give_ref):
    for given, ref in ((keep_in, keep_ref), (give_in, give_ref)):
        ref[...] = given[...].reshape(ref.shape[1], ref.shape[0]).T


def halves(side, gathered, earlier):
    lines, sides, _, rows, dblock = gathered.shape
    half = dblock // 2
    block = (lines, sides, pl.squeezed, rows, half)
    turned = (half, lines * sides * rows)
    shape = jax.ShapeDtypeStruct(turned, BF16)
    return pl.pallas_call(
        halves_kernel,
        out_shape=(shape, shape),
        grid_spec=pltpu.PrefetchScalarGridSpec(
            num_scalar_prefetch=1,
            grid=(1,),
            in_specs=[
                pl.BlockSpec(block, lambda s, side: (0, 0, 0, 0, side[0])),
                pl.BlockSpec(block, lambda s, side: (0, 0, 0, 0, 1 - side[0])),
                pl.BlockSpec(memory_space=pl.ANY),
            ],
            out_specs=[pl.BlockSpec(turned, lambda s, side: (0, 0))] * 2,
        ),
        compiler_params=params(),
        interpret=INTERPRET,
    )(side, gathered, gathered, stay(earlier))


def cotangent_kernel(rows_ref, *refs):
    refs[-1][...] = rows_ref[...]


def cotangent_rows(gathered, count, earlier):
    groups, _, dblock = gathered.shape
    part = pl.BlockSpec((groups, count, dblock), lambda s: (0, 0, 0))
    return pl.pallas_call(
        cotangent_kernel,
        out_shape=pltpu.HBM((groups, count, dblock), BF16),
        grid=(1,),
        in_specs=[part] + [pl.BlockSpec(memory_space=pl.ANY)] * len(earlier),
        out_specs=part,
        compiler_params=params(),
        interpret=INTERPRET,
    )(stay(gathered), *earlier)


def grad_out_kernel(hidden_ref, cot_ref, out_ref, flag_ref, sum_ref):
    step = pl.program_id(0)
    total = cot_ref.shape[0] * cot_ref.shape[1] * cot_ref.shape[2]
    hidden = hidden_ref[...].reshape(total, HEAD)
    cot = cot_ref[...].reshape(total, cot_ref.shape[-1])
    terms = lax.dot_general(hidden, cot, (((0,), (0,)), ((), ())), preferred_element_type=F32)

    @pl.when(step == 0)
    def first():
        sum_ref[...] = terms

    @pl.when(step > 0)
    def later():
        sum_ref[...] += terms

    @pl.when(step == pl.num_programs(0) - 1)
    def last():
        out_ref[...] = sum_ref[...].astype(BF16)
        flag_ref[...] = jnp.zeros_like(flag_ref)


def grad_out_rows(hidden, cot):
    lines, groups, rows, dblock = cot.shape
    steps = 2
    return pl.pallas_call(
        grad_out_kernel,
        out_shape=(
            jax.ShapeDtypeStruct((HEAD, dblock), BF16),
            pltpu.HBM((8, HEAD), F32),
        ),
        grid=(steps,),
        in_specs=[
            pl.BlockSpec((lines // steps, groups, rows, HEAD), lambda s: (s, 0, 0, 0)),
            pl.BlockSpec((lines // steps, groups, rows, dblock), lambda s: (s, 0, 0, 0)),
        ],
        out_specs=[
            pl.BlockSpec((HEAD, dblock), lambda s: (0, 0)),
            pl.BlockSpec((8, HEAD), lambda s: (0, 0)),
        ],
        scratch_shapes=[pltpu.VMEM((HEAD, dblock), F32)],
        compiler_params=params(),
        interpret=INTERPRET,
    )(hidden, stay(cot))


def grad_in_kernel(y_own_ref, y_other_ref, own_ref, other_ref, out_ref):
    for t in range(2):
        terms = 0.0
        for y_ref, ref in ((y_own_ref, own_ref), (y_other_ref, other_ref)):
            rows = [
                jnp.concatenate([ref[4 * t + 2 * i + s] for s in range(2)], axis=1)
                for i in range(IMAGES)
            ]
            d_pre = jnp.concatenate(rows, axis=0)
            terms = terms + jnp.dot(y_ref[...], d_pre, preferred_element_type=F32)
        terms = terms.astype(BF16)
        if t == 0:
            for s in range(2):
                for a in range(3):
                    first, from_ = (2 * a + s) * HEAD, (3 * s + a) * HEAD
                    out_ref[:, first : first + HEAD] = terms[:, from_ : from_ + HEAD]
        else:
            out_ref[:, 2 * UNITS :] = terms


def grad_in_terms(y_own, y_other, own, other):
    features = y_own.shape[0]
    width = 4 * UNITS
    y = pl.BlockSpec(y_own.shape, lambda s: (0, 0))
    whole = pl.BlockSpec(own.shape, lambda s: (0, 0, 0))
    return pl.pallas_call(
        grad_in_kernel,
        out_shape=pltpu.HBM((features, width), BF16),
        grid=(1,),
        in_specs=[y, y, whole, whole],
        out_specs=pl.BlockSpec((features, width), lambda s: (0, 0)),
        compiler_params=params(),
        interpret=INTERPRET,
    )(y_own, y_other, own, other)


def sum_kernel(parts_ref, earlier_ref, out_ref):
    summed = parts_ref[0].astype(F32)
    for part in range(1, parts_ref.shape[0]):
        summed = summed + parts_ref[part].astype(F32)
    out_ref[...] = summed.astype(BF16)


def sum_parts(parts, earlier):
    shape = parts.shape[1:]
    return pl.pallas_call(
        sum_kernel,
        out_shape=jax.ShapeDtypeStruct(shape, BF16),
        grid=(1,),
        in_specs=[
            pl.BlockSpec(parts.shape, lambda s: (0, 0, 0)),
            pl.BlockSpec(memory_space=pl.ANY),
        ],
        out_specs=pl.BlockSpec(shape, lambda s: (0, 0)),
        compiler_params=params(),
        interpret=INTERPRET,
    )(parts, stay(earlier))


def swap(values, axis):
    return lax.ppermute(values, axis, [(0, 1), (1, 0)])


def send(values, axis):
    shape = values.shape
    flat = values.reshape((shape[0] * shape[1],) + shape[2:])
    return lax.all_to_all(flat, axis, 0, 0, tiled=True).reshape(shape)


def shards(tokens, w_in, w_out, cotangent):
    parts = lax.axis_size(MY)
    groups = lax.axis_size(DP)
    place = lax.axis_index(MY).astype(jnp.int32).reshape(1)
    side = lax.axis_index("dh").astype(jnp.int32).reshape(1)
    dblock = w_in.shape[0]
    total = IMAGES * PATCHES
    kinds = (2, IMAGES, 2)
    lines = 8
    block = total // lines

    with jax.named_scope("token_rows"):
        mine = norm_rows(place, tokens, cotangent)
        rows = lax.all_gather(mine, "zh", axis=0, tiled=False)
        longer = longer_rows(rows)
        gathered = lax.all_gather(rows, "y", axis=0, tiled=False)

    with jax.named_scope("units"):
        partial, flag = products(gathered, w_in, w_out)
        terms = send(partial.reshape(parts, PATCHES, 2 * UNITS), MY)

    with jax.named_scope("y_of_two_groups"):
        y_own, y_give = halves(side, gathered, flag)
        y_other = swap(y_give, "dh")

    with jax.named_scope("units"):
        hidden, d_pre = unit(place, terms, y_own)

    with jax.named_scope("d_pre_of_two_groups"):
        d_pre_other = swap(d_pre, "dh")
        own = lax.all_gather(d_pre, MY, axis=0, tiled=False)
        other = lax.all_gather(d_pre_other, MY, axis=0, tiled=False)
        grad_in = grad_in_terms(y_own, y_other, own, other)
        grad_in = send(grad_in.reshape(4, dblock // 8, grad_in.shape[1]), "dl")

    with jax.named_scope("hidden_of_all_groups"):
        pieces = send(hidden.reshape(parts, block, UNITS), MY)
        owned = by_owner(place, pieces.reshape(kinds + (block, UNITS)), own)

    with jax.named_scope("cotangent_of_all_groups"):
        count = rows.shape[0] * rows.shape[2]
        cot_rows = lax.all_gather(longer, DP, axis=0, tiled=False)
        cot_rows = cotangent_rows(cot_rows, count, (owned, d_pre_other, y_other))
        cot_all = lax.all_gather(cot_rows, "y", axis=0, tiled=False)
        held = cot_all.shape[0]
        cot_all = cot_all.reshape(held, groups, lines // held, block, dblock)
        cot_all = cot_all.swapaxes(1, 2).reshape(lines, groups, block, dblock)

    with jax.named_scope("hidden_of_all_groups"):
        owned = lax.all_gather(send(owned, DP), MY, axis=0, tiled=False)
        grad_out, done = grad_out_rows(owned, cot_all)

    with jax.named_scope("grad_in_sum"):
        grad_in = sum_parts(grad_in, done)

    return grad_in[None], grad_out[None]


def solution(mesh):
    sizes = dict(mesh.shape)
    lines = sizes["mx"] // 2
    cut = (2, sizes["dp"] // 2, lines, 2, sizes["my"] // 2, 2)
    fine = Mesh(mesh.devices.reshape(cut), DP + MX + MY)
    return jax.shard_map(
        shards,
        mesh=fine,
        in_specs=(P(DP + MX, None), P(MY, MX), P(MX, MY), P(DP + MX, MY)),
        out_specs=(P(DP, MY, MX), P(DP, MX, MY)),
        check_vma=False,
    )
```

```python
import jax
import jax.numpy as jnp
from jax import lax
from jax.experimental import pallas as pl
from jax.experimental.pallas import tpu as pltpu
from jax.sharding import Mesh
from jax.sharding import PartitionSpec as P

HEAD = 128
HEADS_DEV = 2
PATCHES = 128
IMAGES = 2
UNITS = 384
EPS = 1e-06

INTERPRET = False
VMEM_LIMIT = 48 * 2**20

DP = ("dh", "dl")
MX = ("y", "zh")
MY = ("x", "c")

F32 = jnp.float32
BF16 = jnp.bfloat16


def stay(values):
    return pltpu.with_memory_space_constraint(values, pltpu.HBM)


def params():
    return pltpu.CompilerParams(vmem_limit_bytes=VMEM_LIMIT)


def norm_kernel(place_ref, tokens_ref, mine_ref, cot_ref, out_ref):
    x = tokens_ref[...].astype(F32)
    mean = jnp.mean(x, axis=-1, keepdims=True)
    center = x - mean
    spread = jnp.mean(center * center, axis=-1, keepdims=True)
    mine = (mine_ref[...].astype(F32) - mean) * lax.rsqrt(spread + EPS)
    out_ref[0] = mine.astype(BF16)
    out_ref[1] = cot_ref[...]


def norm_rows(place, tokens, cotangent):
    rows, features = tokens.shape
    dblock = cotangent.shape[1]
    return pl.pallas_call(
        norm_kernel,
        out_shape=jax.ShapeDtypeStruct((2, rows, dblock), BF16),
        grid_spec=pltpu.PrefetchScalarGridSpec(
            num_scalar_prefetch=1,
            grid=(1,),
            in_specs=[
                pl.BlockSpec((rows, features), lambda s, place: (0, 0)),
                pl.BlockSpec((rows, dblock), lambda s, place: (0, place[0])),
                pl.BlockSpec((rows, dblock), lambda s, place: (0, 0)),
            ],
            out_specs=pl.BlockSpec((2, rows, dblock), lambda s, place: (0, 0, 0)),
        ),
        compiler_params=params(),
        interpret=INTERPRET,
    )(place, stay(tokens), stay(tokens), stay(cotangent))


def products_kernel(y_ref, cot_ref, w_ref, va, vb, vc, out_ref, rows_ref):
    total = IMAGES * PATCHES
    dblock = w_ref.shape[0]
    y = y_ref[...].reshape(total, dblock)
    cot = cot_ref[...].reshape(total, dblock)
    pre = jnp.dot(y, w_ref[...], preferred_element_type=F32).astype(BF16)

    def back(v):
        terms = lax.dot_general(cot, v, (((1,), (1,)), ((), ())), preferred_element_type=F32)
        return terms.astype(BF16)

    def put(s, first, values):
        width = values.shape[1]
        out_ref[0, :, s, :, first : first + width] = values.reshape(IMAGES, PATCHES, width)

    @pl.when(pl.program_id(0) == 0)
    def heads():
        rows_ref[...] = cot
        grad = back(va[...])
        for s in range(2):
            for a in range(3):
                first = (2 * a + s) * HEAD
                put(s, a * HEAD, pre[:, first : first + HEAD])
            put(s, UNITS, grad[:, s * HEAD : (s + 1) * HEAD])
            put(s, UNITS + HEAD, jnp.zeros((total, 2 * HEAD), BF16))

    @pl.when(pl.program_id(0) == 1)
    def units():
        grad = back(jnp.concatenate([va[...], vb[...], vc[...]], axis=0))
        for s in range(2):
            put(s, 0, pre[:, s * UNITS : (s + 1) * UNITS])
            put(s, UNITS, grad[:, s * UNITS : (s + 1) * UNITS])


def products(gathered, w_in, w_out):
    lines, sides, _, rows, dblock = gathered.shape

    def kind(which):
        return pl.BlockSpec(
            (lines, sides, pl.squeezed, rows, dblock), lambda s: (0, 0, which, 0, 0)
        )

    def v_rows(block):
        return pl.BlockSpec((2 * HEAD, dblock), lambda s: (block(s), 0))

    return pl.pallas_call(
        products_kernel,
        out_shape=(
            pltpu.HBM((2, IMAGES, 2, PATCHES, 2 * UNITS), BF16),
            jax.ShapeDtypeStruct((IMAGES * PATCHES, dblock), BF16),
        ),
        grid=(2,),
        in_specs=[
            kind(0),
            kind(1),
            pl.BlockSpec((dblock, 2 * UNITS), lambda s: (0, s)),
            v_rows(lambda s: s),
            v_rows(lambda s: 2),
            v_rows(lambda s: 3),
        ],
        out_specs=[
            pl.BlockSpec((1, IMAGES, 2, PATCHES, 2 * UNITS), lambda s: (s, 0, 0, 0, 0)),
            pl.BlockSpec((IMAGES * PATCHES, dblock), lambda s: (0, 0)),
        ],
        compiler_params=params(),
        interpret=INTERPRET,
    )(gathered, gathered, stay(w_in), *[stay(w_out)] * 3)


def exact(a, b, contract):
    return lax.dot_general(
        a, b, (contract, ((), ())), precision=lax.Precision.HIGHEST, preferred_element_type=F32
    )


def head_norm(values):
    center = values - jnp.mean(values, axis=-1, keepdims=True)
    scale = lax.rsqrt(jnp.mean(center * center, axis=-1, keepdims=True) + EPS)
    return center * scale, scale


def head_norm_pull(normed, scale, grad):
    along = jnp.mean(grad * normed, axis=-1, keepdims=True)
    return scale * (grad - jnp.mean(grad, axis=-1, keepdims=True) - normed * along)


def unit_kernel(place_ref, terms_ref, earlier_ref, hidden_ref, d_pre_ref):
    summed = terms_ref[0].astype(F32)
    for part in range(1, terms_ref.shape[0]):
        summed = summed + terms_ref[part].astype(F32)
    pre = summed[:, :UNITS].astype(BF16).astype(F32)
    grad = summed[:, UNITS:]

    @pl.when(place_ref[0] < 4)
    def attention():
        value = pre[:, 2 * HEAD :]
        d_out = grad[:, :HEAD]
        query, query_scale = head_norm(pre[:, :HEAD])
        key, key_scale = head_norm(pre[:, HEAD : 2 * HEAD])
        weights = jnp.exp(exact(query, key, ((1,), (1,))) * HEAD ** (-0.5))
        weights = weights / jnp.sum(weights, axis=-1, keepdims=True)
        out = exact(weights, value, ((1,), (0,)))
        d_value = exact(weights, d_out, ((0,), (0,)))
        d_weights = exact(d_out, value, ((1,), (1,)))
        along = jnp.sum(d_weights * weights, axis=-1, keepdims=True)
        d_scores = weights * (d_weights - along) * HEAD ** (-0.5)
        d_query = exact(d_scores, key, ((1,), (0,)))
        d_key = exact(d_scores, query, ((0,), (0,)))
        hidden_ref[:, :HEAD] = out.astype(BF16)
        hidden_ref[:, HEAD:] = jnp.zeros((PATCHES, 2 * HEAD), BF16)
        d_pre_ref[:, :HEAD] = head_norm_pull(query, query_scale, d_query).astype(BF16)
        d_pre_ref[:, HEAD : 2 * HEAD] = head_norm_pull(key, key_scale, d_key).astype(BF16)
        d_pre_ref[:, 2 * HEAD :] = d_value.astype(BF16)

    @pl.when(place_ref[0] >= 4)
    def units():
        below = 0.5 * (1.0 + lax.erf(pre * 2.0**-0.5))
        density = jnp.exp(-0.5 * pre * pre) * 0.3989422804014327
        hidden_ref[...] = (pre * below).astype(BF16)
        d_pre_ref[...] = (grad * (below + pre * density)).astype(BF16)


def unit(place, terms, earlier):
    return pl.pallas_call(
        unit_kernel,
        out_shape=(
            pltpu.HBM((PATCHES, UNITS), BF16),
            jax.ShapeDtypeStruct((PATCHES, UNITS), BF16),
        ),
        grid_spec=pltpu.PrefetchScalarGridSpec(
            num_scalar_prefetch=1,
            grid=(1,),
            in_specs=[
                pl.BlockSpec(terms.shape, lambda s, place: (0, 0, 0)),
                pl.BlockSpec(memory_space=pl.ANY),
            ],
            out_specs=[
                pl.BlockSpec((PATCHES, UNITS), lambda s, place: (0, 0)),
                pl.BlockSpec((PATCHES, UNITS), lambda s, place: (0, 0)),
            ],
        ),
        compiler_params=params(),
        interpret=INTERPRET,
    )(place, terms, earlier)


def halves_kernel(side_ref, keep_in, give_in, earlier_ref, keep_ref, give_ref):
    for given, ref in ((keep_in, keep_ref), (give_in, give_ref)):
        ref[...] = given[...].reshape(ref.shape[1], ref.shape[0]).T


def halves(side, gathered, earlier):
    lines, sides, _, rows, dblock = gathered.shape
    half = dblock // 2
    block = (lines, sides, pl.squeezed, rows, half)
    turned = (half, lines * sides * rows)
    shape = jax.ShapeDtypeStruct(turned, BF16)
    return pl.pallas_call(
        halves_kernel,
        out_shape=(shape, shape),
        grid_spec=pltpu.PrefetchScalarGridSpec(
            num_scalar_prefetch=1,
            grid=(1,),
            in_specs=[
                pl.BlockSpec(block, lambda s, side: (0, 0, 0, 0, side[0])),
                pl.BlockSpec(block, lambda s, side: (0, 0, 0, 0, 1 - side[0])),
                pl.BlockSpec(memory_space=pl.ANY),
            ],
            out_specs=[pl.BlockSpec(turned, lambda s, side: (0, 0))] * 2,
        ),
        compiler_params=params(),
        interpret=INTERPRET,
    )(side, gathered, gathered, earlier)


def later_kernel(values_ref, earlier_ref, out_ref):
    out_ref[...] = values_ref[...]


def later(values, earlier):
    part = pl.BlockSpec(values.shape, lambda s: (0, 0))
    return pl.pallas_call(
        later_kernel,
        out_shape=jax.ShapeDtypeStruct(values.shape, BF16),
        grid=(1,),
        in_specs=[part, pl.BlockSpec(memory_space=pl.ANY)],
        out_specs=part,
        compiler_params=params(),
        interpret=INTERPRET,
    )(stay(values), stay(earlier))


def grad_out_kernel(side_ref, own_ref, other_ref, cot_own_ref, cot_other_ref, earlier_ref, out_ref):
    def terms(columns):
        summed = 0.0
        for ref, cot_ref in ((own_ref, cot_own_ref), (other_ref, cot_other_ref)):
            rows = [
                jnp.concatenate([ref[2 * i + unit][:, a:b] for unit, a, b in columns], axis=1)
                for i in range(IMAGES)
            ]
            hidden = jnp.concatenate(rows, axis=0)
            summed = summed + lax.dot_general(
                hidden, cot_ref[...], (((0,), (0,)), ((), ())), preferred_element_type=F32
            )
        out_ref[...] = summed.astype(BF16)

    @pl.when(side_ref[0] == 0)
    def low():
        terms(((0, 0, HEAD), (1, 0, HEAD), (4, 0, 2 * HEAD)))

    @pl.when(side_ref[0] == 1)
    def high():
        terms(((4, 2 * HEAD, UNITS), (5, 0, UNITS)))


def grad_out_terms(side, own, other, cot_own, cot_other, earlier):
    dblock = cot_own.shape[1]
    pieces = pl.BlockSpec(own.shape, lambda s, side: (0, 0, 0))
    rows = pl.BlockSpec(cot_own.shape, lambda s, side: (0, 0))
    return pl.pallas_call(
        grad_out_kernel,
        out_shape=pltpu.HBM((4 * HEAD, dblock), BF16),
        grid_spec=pltpu.PrefetchScalarGridSpec(
            num_scalar_prefetch=1,
            grid=(1,),
            in_specs=[pieces, pieces, rows, rows, pl.BlockSpec(memory_space=pl.ANY)],
            out_specs=pl.BlockSpec((4 * HEAD, dblock), lambda s, side: (0, 0)),
        ),
        compiler_params=params(),
        interpret=INTERPRET,
    )(side, own, other, cot_own, cot_other, earlier)


def grad_in_kernel(y_own_ref, y_other_ref, own_ref, other_ref, earlier_ref, out_ref):
    for t in range(2):
        terms = 0.0
        for y_ref, ref in ((y_own_ref, own_ref), (y_other_ref, other_ref)):
            rows = [
                jnp.concatenate([ref[4 * t + 2 * i + s] for s in range(2)], axis=1)
                for i in range(IMAGES)
            ]
            d_pre = jnp.concatenate(rows, axis=0)
            terms = terms + jnp.dot(y_ref[...], d_pre, preferred_element_type=F32)
        terms = terms.astype(BF16)
        if t == 0:
            for s in range(2):
                for a in range(3):
                    first, from_ = (2 * a + s) * HEAD, (3 * s + a) * HEAD
                    out_ref[:, first : first + HEAD] = terms[:, from_ : from_ + HEAD]
        else:
            out_ref[:, 2 * UNITS :] = terms


def grad_in_terms(y_own, y_other, own, other, earlier):
    features = y_own.shape[0]
    width = 4 * UNITS
    y = pl.BlockSpec(y_own.shape, lambda s: (0, 0))
    whole = pl.BlockSpec(own.shape, lambda s: (0, 0, 0))
    return pl.pallas_call(
        grad_in_kernel,
        out_shape=pltpu.HBM((features, width), BF16),
        grid=(1,),
        in_specs=[y, y, whole, whole, pl.BlockSpec(memory_space=pl.ANY)],
        out_specs=pl.BlockSpec((features, width), lambda s: (0, 0)),
        compiler_params=params(),
        interpret=INTERPRET,
    )(y_own, y_other, own, other, earlier)


def sum_kernel(parts_ref, earlier_ref, out_ref):
    summed = parts_ref[0].astype(F32)
    for part in range(1, parts_ref.shape[0]):
        summed = summed + parts_ref[part].astype(F32)
    out_ref[...] = summed.astype(BF16)


def sum_parts(parts, earlier):
    shape = parts.shape[1:]
    return pl.pallas_call(
        sum_kernel,
        out_shape=jax.ShapeDtypeStruct(shape, BF16),
        grid=(1,),
        in_specs=[
            pl.BlockSpec(parts.shape, lambda s: (0, 0, 0)),
            pl.BlockSpec(memory_space=pl.ANY),
        ],
        out_specs=pl.BlockSpec(shape, lambda s: (0, 0)),
        compiler_params=params(),
        interpret=INTERPRET,
    )(parts, stay(earlier))


def swap(values, axis):
    return lax.ppermute(values, axis, [(0, 1), (1, 0)])


def send(values, axis):
    shape = values.shape
    flat = values.reshape((shape[0] * shape[1],) + shape[2:])
    return lax.all_to_all(flat, axis, 0, 0, tiled=True).reshape(shape)


def shards(tokens, w_in, w_out, cotangent):
    parts = lax.axis_size(MY)
    place = lax.axis_index(MY).astype(jnp.int32).reshape(1)
    side = lax.axis_index("dh").astype(jnp.int32).reshape(1)
    dblock = w_in.shape[0]

    with jax.named_scope("token_rows"):
        mine = norm_rows(place, tokens, cotangent)
        rows = lax.all_gather(mine, "zh", axis=0, tiled=False)
        gathered = lax.all_gather(rows, "y", axis=0, tiled=False)

    with jax.named_scope("units"):
        partial, cot_own = products(gathered, w_in, w_out)
        terms = send(partial.reshape(parts, PATCHES, 2 * UNITS), MY)

    with jax.named_scope("rows_of_two_groups"):
        y_own, y_give = halves(side, gathered, cot_own)
        y_other = swap(y_give, "dh")
        cot_other = swap(cot_own, "dh")

    with jax.named_scope("units"):
        hidden, d_pre = unit(place, terms, y_own)

    with jax.named_scope("d_pre_of_two_groups"):
        d_pre_other = swap(d_pre, "dh")
        own = lax.all_gather(d_pre, MY, axis=0, tiled=False)
        other = lax.all_gather(d_pre_other, MY, axis=0, tiled=False)
        grad_in = grad_in_terms(y_own, y_other, own, other, cot_other)
        in_parts = send(grad_in.reshape(4, dblock // 8, grad_in.shape[1]), "dl")

    with jax.named_scope("hidden_of_two_groups"):
        hidden = later(hidden, grad_in)
        hidden_other = swap(hidden, "dh")
        own = lax.all_gather(hidden, MY, axis=0, tiled=False)
        other = lax.all_gather(hidden_other, MY, axis=0, tiled=False)
        grad_out = grad_out_terms(side, own, other, cot_own, cot_other, in_parts)
        out_parts = send(grad_out.reshape(4, HEAD, dblock), "dl")

    with jax.named_scope("sums"):
        grad_in = sum_parts(in_parts, grad_out)
        grad_out = sum_parts(out_parts, grad_out)

    return grad_in[None], grad_out[None]


def solution(mesh):
    sizes = dict(mesh.shape)
    lines = sizes["mx"] // 2
    cut = (2, sizes["dp"] // 2, lines, 2, sizes["my"] // 2, 2)
    fine = Mesh(mesh.devices.reshape(cut), DP + MX + MY)
    return jax.shard_map(
        shards,
        mesh=fine,
        in_specs=(P(DP + MX, None), P(MY, MX), P(MX, MY), P(DP + MX, MY)),
        out_specs=(P(DP, MY, MX), P(DP, MX, MY)),
        check_vma=False,
    )
```

```python
import jax
import jax.numpy as jnp
from jax import lax
from jax.experimental import pallas as pl
from jax.experimental.pallas import tpu as pltpu
from jax.sharding import Mesh
from jax.sharding import PartitionSpec as P

HEAD = 128
HEADS_DEV = 2
PATCHES = 128
IMAGES = 2
UNITS = 384
EPS = 1e-06

INTERPRET = False
VMEM_LIMIT = 48 * 2**20

DP = ("dh", "dl")
Y = ("yh", "yl")
MX = Y + ("zh",)
MY = ("x", "c")

F32 = jnp.float32
BF16 = jnp.bfloat16


def stay(values):
    return pltpu.with_memory_space_constraint(values, pltpu.HBM)


def params():
    return pltpu.CompilerParams(vmem_limit_bytes=VMEM_LIMIT)


def norm_kernel(place_ref, tokens_ref, mine_ref, cot_ref, out_ref):
    x = tokens_ref[...].astype(F32)
    mean = jnp.mean(x, axis=-1, keepdims=True)
    center = x - mean
    spread = jnp.mean(center * center, axis=-1, keepdims=True)
    mine = (mine_ref[...].astype(F32) - mean) * lax.rsqrt(spread + EPS)
    out_ref[0] = mine.astype(BF16)
    out_ref[1] = cot_ref[...]


def norm_rows(place, tokens, cotangent):
    rows, features = tokens.shape
    dblock = cotangent.shape[1]
    return pl.pallas_call(
        norm_kernel,
        out_shape=jax.ShapeDtypeStruct((2, rows, dblock), BF16),
        grid_spec=pltpu.PrefetchScalarGridSpec(
            num_scalar_prefetch=1,
            grid=(1,),
            in_specs=[
                pl.BlockSpec((rows, features), lambda s, place: (0, 0)),
                pl.BlockSpec((rows, dblock), lambda s, place: (0, place[0])),
                pl.BlockSpec((rows, dblock), lambda s, place: (0, 0)),
            ],
            out_specs=pl.BlockSpec((2, rows, dblock), lambda s, place: (0, 0, 0)),
        ),
        compiler_params=params(),
        interpret=INTERPRET,
    )(place, stay(tokens), stay(tokens), stay(cotangent))


def longer_kernel(rows_ref, out_ref):
    sides, kinds, count, _ = rows_ref.shape
    for third, kind in enumerate((1, 0, 1)):
        for side in range(sides):
            first = (third * sides + side) * count
            out_ref[first : first + count] = rows_ref[side, kind]


def longer_rows(rows):
    sides, _, count, dblock = rows.shape
    shape = (3 * sides * count, dblock)
    return pl.pallas_call(
        longer_kernel,
        out_shape=jax.ShapeDtypeStruct(shape, BF16),
        grid=(1,),
        in_specs=[pl.BlockSpec(rows.shape, lambda s: (0, 0, 0, 0))],
        out_specs=pl.BlockSpec(shape, lambda s: (0, 0)),
        compiler_params=params(),
        interpret=INTERPRET,
    )(rows)


def products_kernel(y_ref, cot_ref, w_ref, va, vb, vc, out_ref, flag_ref):
    total = IMAGES * PATCHES
    dblock = w_ref.shape[0]
    y = y_ref[...].reshape(total, dblock)
    cot = cot_ref[...].reshape(total, dblock)
    pre = jnp.dot(y, w_ref[...], preferred_element_type=F32).astype(BF16)
    flag_ref[...] = jnp.zeros_like(flag_ref)

    def back(v):
        terms = lax.dot_general(cot, v, (((1,), (1,)), ((), ())), preferred_element_type=F32)
        return terms.astype(BF16)

    def put(s, first, values):
        width = values.shape[1]
        out_ref[0, :, s, :, first : first + width] = values.reshape(IMAGES, PATCHES, width)

    @pl.when(pl.program_id(0) == 0)
    def heads():
        grad = back(va[...])
        for s in range(2):
            for a in range(3):
                first = (2 * a + s) * HEAD
                put(s, a * HEAD, pre[:, first : first + HEAD])
            put(s, UNITS, grad[:, s * HEAD : (s + 1) * HEAD])
            put(s, UNITS + HEAD, jnp.zeros((total, 2 * HEAD), BF16))

    @pl.when(pl.program_id(0) == 1)
    def units():
        grad = back(jnp.concatenate([va[...], vb[...], vc[...]], axis=0))
        for s in range(2):
            put(s, 0, pre[:, s * UNITS : (s + 1) * UNITS])
            put(s, UNITS, grad[:, s * UNITS : (s + 1) * UNITS])


def products(gathered, w_in, w_out):
    lines, sides, _, rows, dblock = gathered.shape

    def kind(which):
        return pl.BlockSpec(
            (lines, sides, pl.squeezed, rows, dblock), lambda s: (0, 0, which, 0, 0)
        )

    def v_rows(block):
        return pl.BlockSpec((2 * HEAD, dblock), lambda s: (block(s), 0))

    return pl.pallas_call(
        products_kernel,
        out_shape=(
            pltpu.HBM((2, IMAGES, 2, PATCHES, 2 * UNITS), BF16),
            pltpu.HBM((8, HEAD), F32),
        ),
        grid=(2,),
        in_specs=[
            kind(0),
            kind(1),
            pl.BlockSpec((dblock, 2 * UNITS), lambda s: (0, s)),
            v_rows(lambda s: s),
            v_rows(lambda s: 2),
            v_rows(lambda s: 3),
        ],
        out_specs=[
            pl.BlockSpec((1, IMAGES, 2, PATCHES, 2 * UNITS), lambda s: (s, 0, 0, 0, 0)),
            pl.BlockSpec((8, HEAD), lambda s: (0, 0)),
        ],
        compiler_params=params(),
        interpret=INTERPRET,
    )(gathered, gathered, stay(w_in), *[stay(w_out)] * 3)


def exact(a, b, contract):
    return lax.dot_general(
        a, b, (contract, ((), ())), precision=lax.Precision.HIGHEST, preferred_element_type=F32
    )


def head_norm(values):
    center = values - jnp.mean(values, axis=-1, keepdims=True)
    scale = lax.rsqrt(jnp.mean(center * center, axis=-1, keepdims=True) + EPS)
    return center * scale, scale


def head_norm_pull(normed, scale, grad):
    along = jnp.mean(grad * normed, axis=-1, keepdims=True)
    return scale * (grad - jnp.mean(grad, axis=-1, keepdims=True) - normed * along)


def unit_kernel(place_ref, terms_ref, earlier_ref, hidden_ref, d_pre_ref):
    summed = terms_ref[0].astype(F32)
    for part in range(1, terms_ref.shape[0]):
        summed = summed + terms_ref[part].astype(F32)
    pre = summed[:, :UNITS].astype(BF16).astype(F32)
    grad = summed[:, UNITS:]

    @pl.when(place_ref[0] < 4)
    def attention():
        value = pre[:, 2 * HEAD :]
        d_out = grad[:, :HEAD]
        query, query_scale = head_norm(pre[:, :HEAD])
        key, key_scale = head_norm(pre[:, HEAD : 2 * HEAD])
        weights = jnp.exp(exact(query, key, ((1,), (1,))) * HEAD ** (-0.5))
        weights = weights / jnp.sum(weights, axis=-1, keepdims=True)
        out = exact(weights, value, ((1,), (0,)))
        d_value = exact(weights, d_out, ((0,), (0,)))
        d_weights = exact(d_out, value, ((1,), (1,)))
        along = jnp.sum(d_weights * weights, axis=-1, keepdims=True)
        d_scores = weights * (d_weights - along) * HEAD ** (-0.5)
        d_query = exact(d_scores, key, ((1,), (0,)))
        d_key = exact(d_scores, query, ((0,), (0,)))
        for i in range(IMAGES):
            hidden_ref[i, :, :HEAD] = out.astype(BF16)
            hidden_ref[i, :, HEAD:] = jnp.zeros((PATCHES, 2 * HEAD), BF16)
        d_pre_ref[:, :HEAD] = head_norm_pull(query, query_scale, d_query).astype(BF16)
        d_pre_ref[:, HEAD : 2 * HEAD] = head_norm_pull(key, key_scale, d_key).astype(BF16)
        d_pre_ref[:, 2 * HEAD :] = d_value.astype(BF16)

    @pl.when(place_ref[0] >= 4)
    def units():
        below = 0.5 * (1.0 + lax.erf(pre * 2.0**-0.5))
        density = jnp.exp(-0.5 * pre * pre) * 0.3989422804014327
        for i in range(IMAGES):
            hidden_ref[i] = (pre * below).astype(BF16)
        d_pre_ref[...] = (grad * (below + pre * density)).astype(BF16)


def unit(place, terms, earlier):
    return pl.pallas_call(
        unit_kernel,
        out_shape=(
            jax.ShapeDtypeStruct((IMAGES, PATCHES, UNITS), BF16),
            jax.ShapeDtypeStruct((PATCHES, UNITS), BF16),
        ),
        grid_spec=pltpu.PrefetchScalarGridSpec(
            num_scalar_prefetch=1,
            grid=(1,),
            in_specs=[
                pl.BlockSpec(terms.shape, lambda s, place: (0, 0, 0)),
                pl.BlockSpec(memory_space=pl.ANY),
            ],
            out_specs=[
                pl.BlockSpec((IMAGES, PATCHES, UNITS), lambda s, place: (0, 0, 0)),
                pl.BlockSpec((PATCHES, UNITS), lambda s, place: (0, 0)),
            ],
        ),
        compiler_params=params(),
        interpret=INTERPRET,
    )(place, terms, earlier)


def by_owner_kernel(place_ref, pieces_ref, earlier_ref, out_ref):
    for s in range(2):
        out_ref[s] = pieces_ref[0, 0, s, :, :HEAD]
        for a in range(3):
            out_ref[2 + 3 * s + a] = pieces_ref[1, 0, s, :, a * HEAD : (a + 1) * HEAD]


def by_owner(place, pieces, earlier):
    rows = pieces.shape[-2]
    return pl.pallas_call(
        by_owner_kernel,
        out_shape=jax.ShapeDtypeStruct((8, rows, HEAD), BF16),
        grid_spec=pltpu.PrefetchScalarGridSpec(
            num_scalar_prefetch=1,
            grid=(1,),
            in_specs=[
                pl.BlockSpec(
                    (2, 1, 2, rows, UNITS), lambda s, place: (0, place[0] // 4, 0, 0, 0)
                ),
                pl.BlockSpec(memory_space=pl.ANY),
            ],
            out_specs=pl.BlockSpec((8, rows, HEAD), lambda s, place: (0, 0, 0)),
        ),
        compiler_params=params(),
        interpret=INTERPRET,
    )(place, pieces, earlier)


def halves_kernel(side_ref, keep_in, give_in, earlier_ref, keep_ref, give_ref):
    for given, ref in ((keep_in, keep_ref), (give_in, give_ref)):
        ref[...] = given[...].reshape(ref.shape[1], ref.shape[0]).T


def halves(side, gathered, earlier):
    lines, sides, _, rows, dblock = gathered.shape
    half = dblock // 2
    block = (lines, sides, pl.squeezed, rows, half)
    turned = (half, lines * sides * rows)
    shape = jax.ShapeDtypeStruct(turned, BF16)
    return pl.pallas_call(
        halves_kernel,
        out_shape=(shape, shape),
        grid_spec=pltpu.PrefetchScalarGridSpec(
            num_scalar_prefetch=1,
            grid=(1,),
            in_specs=[
                pl.BlockSpec(block, lambda s, side: (0, 0, 0, 0, side[0])),
                pl.BlockSpec(block, lambda s, side: (0, 0, 0, 0, 1 - side[0])),
                pl.BlockSpec(memory_space=pl.ANY),
            ],
            out_specs=[pl.BlockSpec(turned, lambda s, side: (0, 0))] * 2,
        ),
        compiler_params=params(),
        interpret=INTERPRET,
    )(side, gathered, gathered, stay(earlier))


def cotangent_kernel(rows_ref, *refs):
    refs[-1][...] = rows_ref[...]


def cotangent_rows(gathered, count, earlier):
    groups, _, dblock = gathered.shape
    part = pl.BlockSpec((groups, count, dblock), lambda s: (0, 0, 0))
    return pl.pallas_call(
        cotangent_kernel,
        out_shape=pltpu.HBM((groups, count, dblock), BF16),
        grid=(1,),
        in_specs=[part] + [pl.BlockSpec(memory_space=pl.ANY)] * len(earlier),
        out_specs=part,
        compiler_params=params(),
        interpret=INTERPRET,
    )(stay(gathered), *earlier)


def grad_out_kernel(hidden_ref, cot_ref, out_ref, flag_ref, sum_ref):
    step = pl.program_id(0)
    total = cot_ref.shape[0] * cot_ref.shape[1] * cot_ref.shape[2]
    hidden = hidden_ref[...].reshape(total, HEAD)
    cot = cot_ref[...].reshape(total, cot_ref.shape[-1])
    terms = lax.dot_general(hidden, cot, (((0,), (0,)), ((), ())), preferred_element_type=F32)

    @pl.when(step == 0)
    def first():
        sum_ref[...] = terms

    @pl.when(step > 0)
    def later():
        sum_ref[...] += terms

    @pl.when(step == pl.num_programs(0) - 1)
    def last():
        out_ref[...] = sum_ref[...].astype(BF16)
        flag_ref[...] = jnp.zeros_like(flag_ref)


def grad_out_rows(hidden, cot):
    lines, groups, rows, dblock = cot.shape
    steps = 2
    return pl.pallas_call(
        grad_out_kernel,
        out_shape=(
            jax.ShapeDtypeStruct((HEAD, dblock), BF16),
            pltpu.HBM((8, HEAD), F32),
        ),
        grid=(steps,),
        in_specs=[
            pl.BlockSpec((lines // steps, groups, rows, HEAD), lambda s: (s, 0, 0, 0)),
            pl.BlockSpec((lines // steps, groups, rows, dblock), lambda s: (s, 0, 0, 0)),
        ],
        out_specs=[
            pl.BlockSpec((HEAD, dblock), lambda s: (0, 0)),
            pl.BlockSpec((8, HEAD), lambda s: (0, 0)),
        ],
        scratch_shapes=[pltpu.VMEM((HEAD, dblock), F32)],
        compiler_params=params(),
        interpret=INTERPRET,
    )(hidden, stay(cot))


def grad_in_kernel(y_own_ref, y_other_ref, own_ref, other_ref, out_ref):
    for t in range(2):
        terms = 0.0
        for y_ref, ref in ((y_own_ref, own_ref), (y_other_ref, other_ref)):
            rows = [
                jnp.concatenate([ref[4 * t + 2 * i + s] for s in range(2)], axis=1)
                for i in range(IMAGES)
            ]
            d_pre = jnp.concatenate(rows, axis=0)
            terms = terms + jnp.dot(y_ref[...], d_pre, preferred_element_type=F32)
        terms = terms.astype(BF16)
        if t == 0:
            for s in range(2):
                for a in range(3):
                    first, from_ = (2 * a + s) * HEAD, (3 * s + a) * HEAD
                    out_ref[:, first : first + HEAD] = terms[:, from_ : from_ + HEAD]
        else:
            out_ref[:, 2 * UNITS :] = terms


def grad_in_terms(y_own, y_other, own, other):
    features = y_own.shape[0]
    width = 4 * UNITS
    y = pl.BlockSpec(y_own.shape, lambda s: (0, 0))
    whole = pl.BlockSpec(own.shape, lambda s: (0, 0, 0))
    return pl.pallas_call(
        grad_in_kernel,
        out_shape=pltpu.HBM((features, width), BF16),
        grid=(1,),
        in_specs=[y, y, whole, whole],
        out_specs=pl.BlockSpec((features, width), lambda s: (0, 0)),
        compiler_params=params(),
        interpret=INTERPRET,
    )(y_own, y_other, own, other)


def sum_kernel(parts_ref, earlier_ref, out_ref):
    summed = parts_ref[0].astype(F32)
    for part in range(1, parts_ref.shape[0]):
        summed = summed + parts_ref[part].astype(F32)
    out_ref[...] = summed.astype(BF16)


def sum_parts(parts, earlier):
    shape = parts.shape[1:]
    return pl.pallas_call(
        sum_kernel,
        out_shape=jax.ShapeDtypeStruct(shape, BF16),
        grid=(1,),
        in_specs=[
            pl.BlockSpec(parts.shape, lambda s: (0, 0, 0)),
            pl.BlockSpec(memory_space=pl.ANY),
        ],
        out_specs=pl.BlockSpec(shape, lambda s: (0, 0)),
        compiler_params=params(),
        interpret=INTERPRET,
    )(parts, stay(earlier))


def swap(values, axis):
    return lax.ppermute(values, axis, [(0, 1), (1, 0)])


def send(values, axis):
    shape = values.shape
    flat = values.reshape((shape[0] * shape[1],) + shape[2:])
    return lax.all_to_all(flat, axis, 0, 0, tiled=True).reshape(shape)


def shards(tokens, w_in, w_out, cotangent):
    parts = lax.axis_size(MY)
    groups = lax.axis_size(DP)
    place = lax.axis_index(MY).astype(jnp.int32).reshape(1)
    side = lax.axis_index("dh").astype(jnp.int32).reshape(1)
    dblock = w_in.shape[0]
    total = IMAGES * PATCHES
    kinds = (2, IMAGES, 2)
    lines = 8
    block = total // lines

    with jax.named_scope("token_rows"):
        mine = norm_rows(place, tokens, cotangent)
        rows = lax.all_gather(mine, "zh", axis=0, tiled=False)
        longer = longer_rows(rows)
        near = lax.all_gather(rows, "yl", axis=0, tiled=False)
        gathered = lax.all_gather(near, "yh", axis=0, tiled=False)
        gathered = gathered.reshape((-1,) + rows.shape)

    with jax.named_scope("units"):
        partial, flag = products(gathered, w_in, w_out)
        terms = send(partial.reshape(parts, PATCHES, 2 * UNITS), MY)

    with jax.named_scope("y_of_two_groups"):
        y_own, y_give = halves(side, gathered, flag)
        y_other = swap(y_give, "dh")

    with jax.named_scope("units"):
        hidden, d_pre = unit(place, terms, y_own)

    with jax.named_scope("d_pre_of_two_groups"):
        d_pre_other = swap(d_pre, "dh")
        own = lax.all_gather(d_pre, MY, axis=0, tiled=False)
        other = lax.all_gather(d_pre_other, MY, axis=0, tiled=False)
        grad_in = grad_in_terms(y_own, y_other, own, other)
        grad_in = send(grad_in.reshape(4, dblock // 8, grad_in.shape[1]), "dl")

    with jax.named_scope("hidden_of_all_groups"):
        blocks = send(hidden.reshape(parts, block, UNITS), MY)
        owned = by_owner(place, blocks.reshape(kinds + (block, UNITS)), own)

    with jax.named_scope("cotangent_of_all_groups"):
        count = rows.shape[0] * rows.shape[2]
        cot_rows = lax.all_gather(longer, DP, axis=0, tiled=False)
        cot_rows = cotangent_rows(cot_rows, count, (blocks, own, d_pre_other, y_other))
        cot_all = lax.all_gather(cot_rows, Y, axis=0, tiled=False)
        held = cot_all.shape[0]
        cot_all = cot_all.reshape(held, groups, lines // held, block, dblock)
        cot_all = cot_all.swapaxes(1, 2).reshape(lines, groups, block, dblock)

    with jax.named_scope("hidden_of_all_groups"):
        owned = lax.all_gather(send(owned, DP), MY, axis=0, tiled=False)
        grad_out, done = grad_out_rows(owned, cot_all)

    with jax.named_scope("grad_in_sum"):
        grad_in = sum_parts(grad_in, done)

    return grad_in[None], grad_out[None]


def solution(mesh):
    sizes = dict(mesh.shape)
    lines = sizes["mx"] // 2
    near = 2 if lines % 2 == 0 else 1
    cut = (2, sizes["dp"] // 2, lines // near, near, 2, sizes["my"] // 2, 2)
    fine = Mesh(mesh.devices.reshape(cut), DP + MX + MY)
    return jax.shard_map(
        shards,
        mesh=fine,
        in_specs=(P(DP + MX, None), P(MY, MX), P(MX, MY), P(DP + MX, MY)),
        out_specs=(P(DP, MY, MX), P(DP, MX, MY)),
        check_vma=False,
    )
```

```python
import jax
import jax.numpy as jnp
from jax import lax
from jax.experimental import pallas as pl
from jax.experimental.pallas import tpu as pltpu
from jax.sharding import Mesh
from jax.sharding import PartitionSpec as P

HEAD = 128
HEADS_DEV = 2
PATCHES = 128
IMAGES = 2
UNITS = 384
EPS = 1e-06

INTERPRET = False
VMEM_LIMIT = 48 * 2**20

DP = ("dh", "dl")
Y = ("yh", "yl")
MX = Y + ("zh",)
MY = ("x", "c")

F32 = jnp.float32
BF16 = jnp.bfloat16


def stay(values):
    return pltpu.with_memory_space_constraint(values, pltpu.HBM)


def params():
    return pltpu.CompilerParams(vmem_limit_bytes=VMEM_LIMIT)


def norm_kernel(place_ref, tokens_ref, mine_ref, cot_ref, out_ref):
    x = tokens_ref[...].astype(F32)
    mean = jnp.mean(x, axis=-1, keepdims=True)
    center = x - mean
    spread = jnp.mean(center * center, axis=-1, keepdims=True)
    mine = (mine_ref[...].astype(F32) - mean) * lax.rsqrt(spread + EPS)
    out_ref[0] = mine.astype(BF16)
    out_ref[1] = cot_ref[...]


def norm_rows(place, tokens, cotangent):
    rows, features = tokens.shape
    dblock = cotangent.shape[1]
    return pl.pallas_call(
        norm_kernel,
        out_shape=jax.ShapeDtypeStruct((2, rows, dblock), BF16),
        grid_spec=pltpu.PrefetchScalarGridSpec(
            num_scalar_prefetch=1,
            grid=(1,),
            in_specs=[
                pl.BlockSpec((rows, features), lambda s, place: (0, 0)),
                pl.BlockSpec((rows, dblock), lambda s, place: (0, place[0])),
                pl.BlockSpec((rows, dblock), lambda s, place: (0, 0)),
            ],
            out_specs=pl.BlockSpec((2, rows, dblock), lambda s, place: (0, 0, 0)),
        ),
        compiler_params=params(),
        interpret=INTERPRET,
    )(place, stay(tokens), stay(tokens), stay(cotangent))


def longer_kernel(rows_ref, out_ref):
    sides, kinds, count, _ = rows_ref.shape
    for third, kind in enumerate((1, 0, 1)):
        for side in range(sides):
            first = (third * sides + side) * count
            out_ref[first : first + count] = rows_ref[side, kind]


def longer_rows(rows):
    sides, _, count, dblock = rows.shape
    shape = (3 * sides * count, dblock)
    return pl.pallas_call(
        longer_kernel,
        out_shape=jax.ShapeDtypeStruct(shape, BF16),
        grid=(1,),
        in_specs=[pl.BlockSpec(rows.shape, lambda s: (0, 0, 0, 0))],
        out_specs=pl.BlockSpec(shape, lambda s: (0, 0)),
        compiler_params=params(),
        interpret=INTERPRET,
    )(rows)


def products_kernel(y_ref, cot_ref, w_ref, va, vb, vc, out_ref, flag_ref):
    total = IMAGES * PATCHES
    dblock = w_ref.shape[0]
    y = y_ref[...].reshape(total, dblock)
    cot = cot_ref[...].reshape(total, dblock)
    pre = jnp.dot(y, w_ref[...], preferred_element_type=F32).astype(BF16)
    flag_ref[...] = jnp.zeros_like(flag_ref)

    def back(v):
        terms = lax.dot_general(cot, v, (((1,), (1,)), ((), ())), preferred_element_type=F32)
        return terms.astype(BF16)

    def put(s, first, values):
        width = values.shape[1]
        out_ref[0, :, s, :, first : first + width] = values.reshape(IMAGES, PATCHES, width)

    @pl.when(pl.program_id(0) == 0)
    def heads():
        grad = back(va[...])
        for s in range(2):
            for a in range(3):
                first = (2 * a + s) * HEAD
                put(s, a * HEAD, pre[:, first : first + HEAD])
            put(s, UNITS, grad[:, s * HEAD : (s + 1) * HEAD])
            put(s, UNITS + HEAD, jnp.zeros((total, 2 * HEAD), BF16))

    @pl.when(pl.program_id(0) == 1)
    def units():
        grad = back(jnp.concatenate([va[...], vb[...], vc[...]], axis=0))
        for s in range(2):
            put(s, 0, pre[:, s * UNITS : (s + 1) * UNITS])
            put(s, UNITS, grad[:, s * UNITS : (s + 1) * UNITS])


def products(gathered, w_in, w_out):
    lines, sides, _, rows, dblock = gathered.shape

    def kind(which):
        return pl.BlockSpec(
            (lines, sides, pl.squeezed, rows, dblock), lambda s: (0, 0, which, 0, 0)
        )

    def v_rows(block):
        return pl.BlockSpec((2 * HEAD, dblock), lambda s: (block(s), 0))

    return pl.pallas_call(
        products_kernel,
        out_shape=(
            pltpu.HBM((2, IMAGES, 2, PATCHES, 2 * UNITS), BF16),
            pltpu.HBM((8, HEAD), F32),
        ),
        grid=(2,),
        in_specs=[
            kind(0),
            kind(1),
            pl.BlockSpec((dblock, 2 * UNITS), lambda s: (0, s)),
            v_rows(lambda s: s),
            v_rows(lambda s: 2),
            v_rows(lambda s: 3),
        ],
        out_specs=[
            pl.BlockSpec((1, IMAGES, 2, PATCHES, 2 * UNITS), lambda s: (s, 0, 0, 0, 0)),
            pl.BlockSpec((8, HEAD), lambda s: (0, 0)),
        ],
        compiler_params=params(),
        interpret=INTERPRET,
    )(gathered, gathered, stay(w_in), *[stay(w_out)] * 3)


def exact(a, b, contract):
    return lax.dot_general(
        a, b, (contract, ((), ())), precision=lax.Precision.HIGHEST, preferred_element_type=F32
    )


def head_norm(values):
    center = values - jnp.mean(values, axis=-1, keepdims=True)
    scale = lax.rsqrt(jnp.mean(center * center, axis=-1, keepdims=True) + EPS)
    return center * scale, scale


def head_norm_pull(normed, scale, grad):
    along = jnp.mean(grad * normed, axis=-1, keepdims=True)
    return scale * (grad - jnp.mean(grad, axis=-1, keepdims=True) - normed * along)


def unit_kernel(place_ref, terms_ref, earlier_ref, hidden_ref, d_pre_ref):
    summed = terms_ref[0].astype(F32)
    for part in range(1, terms_ref.shape[0]):
        summed = summed + terms_ref[part].astype(F32)
    pre = summed[:, :UNITS].astype(BF16).astype(F32)
    grad = summed[:, UNITS:]

    @pl.when(place_ref[0] < 4)
    def attention():
        value = pre[:, 2 * HEAD :]
        d_out = grad[:, :HEAD]
        query, query_scale = head_norm(pre[:, :HEAD])
        key, key_scale = head_norm(pre[:, HEAD : 2 * HEAD])
        weights = jnp.exp(exact(query, key, ((1,), (1,))) * HEAD ** (-0.5))
        weights = weights / jnp.sum(weights, axis=-1, keepdims=True)
        out = exact(weights, value, ((1,), (0,)))
        d_value = exact(weights, d_out, ((0,), (0,)))
        d_weights = exact(d_out, value, ((1,), (1,)))
        along = jnp.sum(d_weights * weights, axis=-1, keepdims=True)
        d_scores = weights * (d_weights - along) * HEAD ** (-0.5)
        d_query = exact(d_scores, key, ((1,), (0,)))
        d_key = exact(d_scores, query, ((0,), (0,)))
        for i in range(IMAGES):
            hidden_ref[i, :, :HEAD] = out.astype(BF16)
            hidden_ref[i, :, HEAD:] = jnp.zeros((PATCHES, 2 * HEAD), BF16)
        d_pre_ref[:, :HEAD] = head_norm_pull(query, query_scale, d_query).astype(BF16)
        d_pre_ref[:, HEAD : 2 * HEAD] = head_norm_pull(key, key_scale, d_key).astype(BF16)
        d_pre_ref[:, 2 * HEAD :] = d_value.astype(BF16)

    @pl.when(place_ref[0] >= 4)
    def units():
        below = 0.5 * (1.0 + lax.erf(pre * 2.0**-0.5))
        density = jnp.exp(-0.5 * pre * pre) * 0.3989422804014327
        for i in range(IMAGES):
            hidden_ref[i] = (pre * below).astype(BF16)
        d_pre_ref[...] = (grad * (below + pre * density)).astype(BF16)


def unit(place, terms, earlier):
    return pl.pallas_call(
        unit_kernel,
        out_shape=(
            jax.ShapeDtypeStruct((IMAGES, PATCHES, UNITS), BF16),
            jax.ShapeDtypeStruct((PATCHES, UNITS), BF16),
        ),
        grid_spec=pltpu.PrefetchScalarGridSpec(
            num_scalar_prefetch=1,
            grid=(1,),
            in_specs=[
                pl.BlockSpec(terms.shape, lambda s, place: (0, 0, 0)),
                pl.BlockSpec(memory_space=pl.ANY),
            ],
            out_specs=[
                pl.BlockSpec((IMAGES, PATCHES, UNITS), lambda s, place: (0, 0, 0)),
                pl.BlockSpec((PATCHES, UNITS), lambda s, place: (0, 0)),
            ],
        ),
        compiler_params=params(),
        interpret=INTERPRET,
    )(place, terms, earlier)


def by_owner_kernel(place_ref, pieces_ref, rows_ref, *refs):
    out_ref, cot_ref = refs[-2:]
    for s in range(2):
        out_ref[s] = pieces_ref[0, 0, s, :, :HEAD]
        for a in range(3):
            out_ref[2 + 3 * s + a] = pieces_ref[1, 0, s, :, a * HEAD : (a + 1) * HEAD]
    cot_ref[...] = rows_ref[...]


def by_owner(place, pieces, gathered, count, earlier):
    rows = pieces.shape[-2]
    groups, _, dblock = gathered.shape
    return pl.pallas_call(
        by_owner_kernel,
        out_shape=(
            pltpu.HBM((8, rows, HEAD), BF16),
            pltpu.HBM((groups, count, dblock), BF16),
        ),
        grid_spec=pltpu.PrefetchScalarGridSpec(
            num_scalar_prefetch=1,
            grid=(1,),
            in_specs=[
                pl.BlockSpec(
                    (2, 1, 2, rows, UNITS), lambda s, place: (0, place[0] // 4, 0, 0, 0)
                ),
                pl.BlockSpec((groups, count, dblock), lambda s, place: (0, 0, 0)),
            ]
            + [pl.BlockSpec(memory_space=pl.ANY)] * len(earlier),
            out_specs=[
                pl.BlockSpec((8, rows, HEAD), lambda s, place: (0, 0, 0)),
                pl.BlockSpec((groups, count, dblock), lambda s, place: (0, 0, 0)),
            ],
        ),
        compiler_params=params(),
        interpret=INTERPRET,
    )(place, pieces, stay(gathered), *earlier)


def halves_kernel(side_ref, keep_in, give_in, earlier_ref, keep_ref, give_ref):
    for given, ref in ((keep_in, keep_ref), (give_in, give_ref)):
        ref[...] = given[...].reshape(ref.shape[1], ref.shape[0]).T


def halves(side, gathered, earlier):
    lines, sides, _, rows, dblock = gathered.shape
    half = dblock // 2
    block = (lines, sides, pl.squeezed, rows, half)
    turned = (half, lines * sides * rows)
    shape = jax.ShapeDtypeStruct(turned, BF16)
    return pl.pallas_call(
        halves_kernel,
        out_shape=(shape, shape),
        grid_spec=pltpu.PrefetchScalarGridSpec(
            num_scalar_prefetch=1,
            grid=(1,),
            in_specs=[
                pl.BlockSpec(block, lambda s, side: (0, 0, 0, 0, side[0])),
                pl.BlockSpec(block, lambda s, side: (0, 0, 0, 0, 1 - side[0])),
                pl.BlockSpec(memory_space=pl.ANY),
            ],
            out_specs=[pl.BlockSpec(turned, lambda s, side: (0, 0))] * 2,
        ),
        compiler_params=params(),
        interpret=INTERPRET,
    )(side, gathered, gathered, stay(earlier))


def grad_out_kernel(hidden_ref, cot_ref, out_ref, flag_ref, sum_ref):
    step = pl.program_id(0)
    total = cot_ref.shape[0] * cot_ref.shape[1] * cot_ref.shape[2]
    hidden = hidden_ref[...].reshape(total, HEAD)
    cot = cot_ref[...].reshape(total, cot_ref.shape[-1])
    terms = lax.dot_general(hidden, cot, (((0,), (0,)), ((), ())), preferred_element_type=F32)

    @pl.when(step == 0)
    def first():
        sum_ref[...] = terms

    @pl.when(step > 0)
    def later():
        sum_ref[...] += terms

    @pl.when(step == pl.num_programs(0) - 1)
    def last():
        out_ref[...] = sum_ref[...].astype(BF16)
        flag_ref[...] = jnp.zeros_like(flag_ref)


def grad_out_rows(hidden, cot):
    lines, groups, rows, dblock = cot.shape
    steps = 2
    return pl.pallas_call(
        grad_out_kernel,
        out_shape=(
            jax.ShapeDtypeStruct((HEAD, dblock), BF16),
            pltpu.HBM((8, HEAD), F32),
        ),
        grid=(steps,),
        in_specs=[
            pl.BlockSpec((lines // steps, groups, rows, HEAD), lambda s: (s, 0, 0, 0)),
            pl.BlockSpec((lines // steps, groups, rows, dblock), lambda s: (s, 0, 0, 0)),
        ],
        out_specs=[
            pl.BlockSpec((HEAD, dblock), lambda s: (0, 0)),
            pl.BlockSpec((8, HEAD), lambda s: (0, 0)),
        ],
        scratch_shapes=[pltpu.VMEM((HEAD, dblock), F32)],
        compiler_params=params(),
        interpret=INTERPRET,
    )(hidden, stay(cot))


def grad_in_kernel(y_own_ref, y_other_ref, own_ref, other_ref, out_ref):
    for t in range(2):
        terms = 0.0
        for y_ref, ref in ((y_own_ref, own_ref), (y_other_ref, other_ref)):
            rows = [
                jnp.concatenate([ref[4 * t + 2 * i + s] for s in range(2)], axis=1)
                for i in range(IMAGES)
            ]
            d_pre = jnp.concatenate(rows, axis=0)
            terms = terms + jnp.dot(y_ref[...], d_pre, preferred_element_type=F32)
        terms = terms.astype(BF16)
        if t == 0:
            for s in range(2):
                for a in range(3):
                    first, from_ = (2 * a + s) * HEAD, (3 * s + a) * HEAD
                    out_ref[:, first : first + HEAD] = terms[:, from_ : from_ + HEAD]
        else:
            out_ref[:, 2 * UNITS :] = terms


def grad_in_terms(y_own, y_other, own, other):
    features = y_own.shape[0]
    width = 4 * UNITS
    y = pl.BlockSpec(y_own.shape, lambda s: (0, 0))
    whole = pl.BlockSpec(own.shape, lambda s: (0, 0, 0))
    return pl.pallas_call(
        grad_in_kernel,
        out_shape=pltpu.HBM((features, width), BF16),
        grid=(1,),
        in_specs=[y, y, whole, whole],
        out_specs=pl.BlockSpec((features, width), lambda s: (0, 0)),
        compiler_params=params(),
        interpret=INTERPRET,
    )(y_own, y_other, own, other)


def sum_kernel(parts_ref, earlier_ref, out_ref):
    summed = parts_ref[0].astype(F32)
    for part in range(1, parts_ref.shape[0]):
        summed = summed + parts_ref[part].astype(F32)
    out_ref[...] = summed.astype(BF16)


def sum_parts(parts, earlier):
    shape = parts.shape[1:]
    return pl.pallas_call(
        sum_kernel,
        out_shape=jax.ShapeDtypeStruct(shape, BF16),
        grid=(1,),
        in_specs=[
            pl.BlockSpec(parts.shape, lambda s: (0, 0, 0)),
            pl.BlockSpec(memory_space=pl.ANY),
        ],
        out_specs=pl.BlockSpec(shape, lambda s: (0, 0)),
        compiler_params=params(),
        interpret=INTERPRET,
    )(parts, stay(earlier))


def swap(values, axis):
    return lax.ppermute(values, axis, [(0, 1), (1, 0)])


def send(values, axis):
    shape = values.shape
    flat = values.reshape((shape[0] * shape[1],) + shape[2:])
    return lax.all_to_all(flat, axis, 0, 0, tiled=True).reshape(shape)


def shards(tokens, w_in, w_out, cotangent):
    parts = lax.axis_size(MY)
    groups = lax.axis_size(DP)
    place = lax.axis_index(MY).astype(jnp.int32).reshape(1)
    side = lax.axis_index("dh").astype(jnp.int32).reshape(1)
    dblock = w_in.shape[0]
    total = IMAGES * PATCHES
    kinds = (2, IMAGES, 2)
    lines = 8
    block = total // lines

    with jax.named_scope("token_rows"):
        mine = norm_rows(place, tokens, cotangent)
        rows = lax.all_gather(mine, "zh", axis=0, tiled=False)
        longer = longer_rows(rows)
        near = lax.all_gather(rows, "yl", axis=0, tiled=False)
        gathered = lax.all_gather(near, "yh", axis=0, tiled=False)
        gathered = gathered.reshape((-1,) + rows.shape)

    with jax.named_scope("units"):
        partial, flag = products(gathered, w_in, w_out)
        terms = send(partial.reshape(parts, PATCHES, 2 * UNITS), MY)

    with jax.named_scope("y_of_two_groups"):
        y_own, y_give = halves(side, gathered, flag)
        y_other = swap(y_give, "dh")

    with jax.named_scope("units"):
        hidden, d_pre = unit(place, terms, y_own)

    with jax.named_scope("d_pre_of_two_groups"):
        d_pre_other = swap(d_pre, "dh")
        own = lax.all_gather(d_pre, MY, axis=0, tiled=False)
        other = lax.all_gather(d_pre_other, MY, axis=0, tiled=False)
        grad_in = grad_in_terms(y_own, y_other, own, other)
        grad_in = send(grad_in.reshape(4, dblock // 8, grad_in.shape[1]), "dl")

    with jax.named_scope("hidden_of_all_groups"):
        blocks = send(hidden.reshape(parts, block, UNITS), MY)
        blocks = blocks.reshape(kinds + (block, UNITS))

    with jax.named_scope("cotangent_of_all_groups"):
        count = rows.shape[0] * rows.shape[2]
        cot_rows = lax.all_gather(longer, DP, axis=0, tiled=False)
        ready = (own, d_pre_other, y_other)
        owned, cot_rows = by_owner(place, blocks, cot_rows, count, ready)
        cot_all = lax.all_gather(cot_rows, Y, axis=0, tiled=False)
        held = cot_all.shape[0]
        cot_all = cot_all.reshape(held, groups, lines // held, block, dblock)
        cot_all = cot_all.swapaxes(1, 2).reshape(lines, groups, block, dblock)

    with jax.named_scope("hidden_of_all_groups"):
        owned = lax.all_gather(send(owned, DP), MY, axis=0, tiled=False)
        grad_out, done = grad_out_rows(owned, cot_all)

    with jax.named_scope("grad_in_sum"):
        grad_in = sum_parts(grad_in, done)

    return grad_in[None], grad_out[None]


def solution(mesh):
    sizes = dict(mesh.shape)
    lines = sizes["mx"] // 2
    near = 2 if lines % 2 == 0 else 1
    cut = (2, sizes["dp"] // 2, lines // near, near, 2, sizes["my"] // 2, 2)
    fine = Mesh(mesh.devices.reshape(cut), DP + MX + MY)
    return jax.shard_map(
        shards,
        mesh=fine,
        in_specs=(P(DP + MX, None), P(MY, MX), P(MX, MY), P(DP + MX, MY)),
        out_specs=(P(DP, MY, MX), P(DP, MX, MY)),
        check_vma=False,
    )
```
